256 devices in a mesh: gy: 16 (over z, core), gz: 16 (over x, y).
Axes of the slice: x: 4, y: 4, z: 8, core: 2. Of those that a mesh axis runs over, the one named last changes fastest.
Arguments:
- velocity: float32 [3, 2, 512, 16384], P(None, None, 'gz', 'gy'), may hold values from -6 to 6
- z_lower: float32 [512], P('gz'), may hold values from 2000 to 20500, as said below
- z_upper: float32 [512], P('gz'), may hold values from 2000 to 20500
- z_slope: float32 [512], P('gz'), may hold values from 22 to 72
Outputs:
- projected: float32 [3, 2, 512, 16384], P(None, None, 'gz', 'gy')
The draws below stay inside these ranges and needn't reach their ends.
Inputs may be any that keep to these rules, and one draw needn't show every extreme that they name: z_lower(k) = 1 / (d(k) c(k)), z_upper(k) = 1 / (d(k+1) c(k)) and z_slope(k) = 1 / (d(k) + d(k+1)) for spacings d(0) to d(512) between neighbouring planes, with c(k) = (d(k) + d(k+1)) / 2.
All inputs are finite; a program needn't handle non-finite values.
Results may differ from the reference program's by a relative error of at most 0.0003.
Values sent between devices are 32-bit elements; how exact they have to be, the bound alone decides.
A program may use at most 128 MiB of HBM per device.

```python
import jax
import jax.numpy as jnp
from jax import lax

NY = 1024
KX = 16
NZ = 512


def face_widths(key):
    uniform_draw = jax.random.uniform(key, (NZ + 1,), jnp.float32)
    low_log = jnp.log(jnp.float32(0.007))
    high_log = jnp.log(jnp.float32(0.022))
    return jnp.exp(low_log + uniform_draw * (high_log - low_log))


def draw_z_lower(key, part):
    widths = face_widths(key)
    below = widths[:-1]
    above = widths[1:]
    return (1.0 / (below * 0.5 * (below + above))).astype(jnp.float32)


def draw_z_upper(key, part):
    widths = face_widths(key)
    below = widths[:-1]
    above = widths[1:]
    return (1.0 / (above * 0.5 * (below + above))).astype(jnp.float32)


def draw_z_slope(key, part):
    widths = face_widths(key)
    return (1.0 / (widths[:-1] + widths[1:])).astype(jnp.float32)


def block_scale(own_key, shape, cuts, least, top_value):
    factor_of, own = 1.0, jax.random.fold_in(own_key, 6)
    for position, blocks in cuts:
        draws = jnp.exp(jax.random.uniform(jax.random.fold_in(own, position), (blocks,), jnp.float32, least / len(cuts), top_value / len(cuts)))
        factor_of = factor_of * jnp.repeat(draws, shape[position] // blocks).reshape([-1 if axis == position else 1 for axis in range(len(shape))])
    return factor_of


def bell_draw(own_key, shape, spread, bound, cuts=(), kind=jnp.bfloat16):
    level = block_scale(own_key, shape, cuts, -0.22, 0.18) if cuts else 1.0
    drawn = jax.random.normal(own_key, shape, jnp.float32) * spread * level
    return jnp.minimum(jnp.maximum(drawn, -bound), bound).astype(kind)


def setup_inputs(seed: int = 0) -> dict:
    key_list = jax.random.split(jax.random.key(seed), 5)
    velocity = bell_draw(key_list[0], (3, 2, NZ, NY * KX), 1.0, 6.0, ((2, 16), (3, 16)), jnp.float32)
    z_lower = draw_z_lower(jax.random.fold_in(key_list[4], 71), 0)
    z_upper = draw_z_upper(jax.random.fold_in(key_list[4], 71), 0)
    z_slope = draw_z_slope(jax.random.fold_in(key_list[4], 71), 0)
    return {"velocity": velocity, "z_lower": z_lower, "z_upper": z_upper, "z_slope": z_slope}


def wave_numbers():
    positions = jnp.arange(NY, dtype=jnp.int32)
    return jnp.where(positions < NY // 2, positions, positions - NY).astype(jnp.float32)


def slope_diff(quantity, slope_coef):
    empty = jnp.zeros((1, quantity.shape[1]), quantity.dtype)
    padded = jnp.concatenate([empty, quantity, empty], axis=0)
    return slope_coef[:, None] * (padded[2:] - padded[:-2])


def solve_lines(coef_below, coef_above, centre, source):
    def forward(state_now, inputs):
        ratio, shifted = state_now
        coef_low, coef_high, middle, driven = inputs
        pivot = middle - coef_low * ratio
        ratio_new = coef_high / pivot
        shifted_new = (driven - coef_low * shifted) / pivot
        return (ratio_new, shifted_new), (ratio_new, shifted_new)

    initial = (jnp.zeros((NY,), jnp.float32), jnp.zeros((NY,), source.dtype))
    _, (ratios, shifts) = lax.scan(forward, initial, (coef_below, coef_above, centre, source))

    def backward(following, inputs):
        ratio, shifted = inputs
        solved = shifted - ratio * following
        return solved, solved

    _, pressure = lax.scan(backward, jnp.zeros((NY,), source.dtype), (ratios, shifts), reverse=True)
    return pressure


def reference(velocity, z_lower, z_upper, z_slope):
    grid = velocity.reshape(3, 2, NZ, NY, KX)
    wave_y = wave_numbers()

    def one_slab(slab_index):
        wave_x = (slab_index + 1).astype(jnp.float32)
        slab = lax.dynamic_index_in_dim(grid, slab_index, 4, keepdims=False)
        complex_field = slab[:, 0] + 1j * slab[:, 1]
        spectrum = jnp.fft.fft(complex_field, axis=2)
        divergence = 1j * wave_x * spectrum[0] + 1j * wave_y[None, :] * spectrum[1] + slope_diff(spectrum[2], z_slope)
        centre = -(z_lower + z_upper)[:, None] - (wave_x * wave_x + wave_y * wave_y)[None, :]
        pressure = solve_lines(z_lower, z_upper, centre, divergence)
        updated = jnp.stack([spectrum[0] - 1j * wave_x * pressure,
                             spectrum[1] - 1j * wave_y[None, :] * pressure,
                             spectrum[2] - slope_diff(pressure, z_slope)])
        restored = jnp.fft.ifft(updated, axis=2)
        return jnp.stack([jnp.real(restored), jnp.imag(restored)], axis=1).astype(jnp.float32)

    slabs = lax.map(one_slab, jnp.arange(KX, dtype=jnp.int32))
    return jnp.transpose(slabs, (1, 2, 3, 4, 0)).reshape(3, 2, NZ, NY * KX)
```

```python
import functools

import jax
import jax.numpy as jnp
import ml_dtypes
import numpy as np
from jax import lax
from jax.experimental import pallas as pl
from jax.experimental.pallas import tpu as pltpu
from jax.sharding import PartitionSpec as P

NY = 1024
KX = 16
LANES = 128
MESH = pl.DeviceIdType.MESH


def fourier_tables():
    place = np.arange(256)
    y = 64 * ((place % 128) // 32) + 32 * (place // 128) + place % 32

    def pair(m):
        phase = 2.0 * np.pi * ((y[:, None] * m[None, :]) % NY) / NY
        return np.cos(phase), np.sin(phase)

    c0, s0 = pair(4 * np.arange(128))
    s0[:, 0] = (-1.0) ** y
    c2, s2 = pair(4 * np.arange(128) + 2)
    c1, s1 = pair(4 * np.arange(256) + 1)
    table = np.concatenate([c0, s0, c2, s2, c1, s1], axis=1)

    def split(values):
        high = values.astype(ml_dtypes.bfloat16)
        low = (values - high.astype(np.float64)).astype(ml_dtypes.bfloat16)
        return np.stack([high, low])

    return split(table), split(table.T / NY)


def dot(a, b):
    return jnp.dot(a, b, preferred_element_type=jnp.float32)


def product(values, high, low):
    top = values.astype(jnp.bfloat16)
    rest = (values - top.astype(jnp.float32)).astype(jnp.bfloat16)
    rows = values.shape[0]
    both = dot(jnp.concatenate([top, rest], axis=0), high)
    return both[:rows] + both[rows:] + dot(top, low)


def kernel(
    planes, gy, gz,
    vel, zl, zu, zs, ftab_hbm, itab_hbm, out,
    ftab, itab, rows_buf, send_f, recv_f, send_b, recv_b,
    halo_send, halo_recv, vhat, field_re, field_im,
    inv_piv, mult, ratio, beta, gamma,
    mat_all, rhs_all, red_den, red_bden, red_psi, red_b31, red_br, red_r, red_e, red_phi, red_f,
    grad,
    tab_sem, halo_ssem, halo_rsem, f_ssem, f_rsem, b_ssem, b_rsem, m_ssem, m_rsem, r_ssem, r_rsem,
):
    me = lax.axis_index("gy")
    mz = lax.axis_index("gz")
    f32 = jnp.float32

    barrier = pltpu.get_barrier_semaphore()

    def greet(o, _):
        pl.semaphore_signal(barrier, inc=1, device_id={"gy": lax.rem(me + o, gy)}, device_id_type=MESH)
        pl.semaphore_signal(barrier, inc=1, device_id={"gz": lax.rem(mz + o, gz)}, device_id_type=MESH)
        return 0

    lax.fori_loop(1, gy, greet, 0)
    copy_ft = pltpu.make_async_copy(ftab_hbm, ftab, tab_sem.at[0])
    copy_it = pltpu.make_async_copy(itab_hbm, itab, tab_sem.at[1])
    copy_ft.start()
    copy_it.start()

    def stage(f, re, im):
        for c in range(4):
            a = slice(c * 128, c * 128 + 128)
            b = slice(512 + c * 128, 512 + c * 128 + 128)
            block = jnp.concatenate([re[:, a], im[:, a], re[:, b], im[:, b]], axis=0)
            rows_buf[c * 128:(c + 1) * 128, :] = block.T
        for j in range(KX):
            send_f[f, j] = rows_buf[pl.ds(j, 32, stride=16), :]

    def y_copy(src, dst, ssem, rsem, f, o, slot_src, slot_dst):
        return pltpu.make_async_remote_copy(
            src_ref=src.at[f, slot_src], dst_ref=dst.at[f, slot_dst],
            send_sem=ssem.at[f, o], recv_sem=rsem.at[f, o],
            device_id={"gy": lax.rem(me + o, gy)}, device_id_type=MESH)

    def y_send(src, dst, ssem, rsem, f):
        def one(o, _):
            y_copy(src, dst, ssem, rsem, f, o, lax.rem(me + o, gy), me).start()
            return 0

        lax.fori_loop(1, gy, one, 0)
        dst[f, me] = src[f, me]

    def y_wait_recv(src, dst, ssem, rsem, f):
        def one(o, _):
            d = lax.rem(me + gy - o, gy)
            y_copy(src, dst, ssem, rsem, f, o, d, d).wait_recv()
            return 0

        lax.fori_loop(1, gy, one, 0)

    def y_wait_send(src, dst, ssem, rsem, f):
        def one(o, _):
            y_copy(src, dst, ssem, rsem, f, o, lax.rem(me + o, gy), me).wait_send()
            return 0

        lax.fori_loop(1, gy, one, 0)

    def z_copy(buf, ssem, rsem, o, slot):
        return pltpu.make_async_remote_copy(
            src_ref=buf.at[slot], dst_ref=buf.at[slot],
            send_sem=ssem.at[o], recv_sem=rsem.at[o],
            device_id={"gz": lax.rem(mz + o, gz)}, device_id_type=MESH)

    def z_send(buf, ssem, rsem):
        def one(o, _):
            z_copy(buf, ssem, rsem, o, mz).start()
            return 0

        lax.fori_loop(1, gz, one, 0)

    def z_wait_recv(buf, ssem, rsem):
        def one(o, _):
            z_copy(buf, ssem, rsem, o, lax.rem(mz + gz - o, gz)).wait_recv()
            return 0

        lax.fori_loop(1, gz, one, 0)

    def z_wait_send(buf, ssem, rsem):
        def one(o, _):
            z_copy(buf, ssem, rsem, o, mz).wait_send()
            return 0

        lax.fori_loop(1, gz, one, 0)

    def halo_copies(f):
        up = pltpu.make_async_remote_copy(
            src_ref=halo_send.at[f, 0], dst_ref=halo_recv.at[f, 0],
            send_sem=halo_ssem.at[f, 0], recv_sem=halo_rsem.at[f, 0],
            device_id={"gz": lax.rem(mz + 1, gz)}, device_id_type=MESH)
        down = pltpu.make_async_remote_copy(
            src_ref=halo_send.at[f, 1], dst_ref=halo_recv.at[f, 1],
            send_sem=halo_ssem.at[f, 1], recv_sem=halo_rsem.at[f, 1],
            device_id={"gz": lax.rem(mz + gz - 1, gz)}, device_id_type=MESH)
        return up, down

    plane_id = lax.broadcasted_iota(jnp.int32, (planes, LANES), 0)

    def column(ref):
        def one(k, col):
            return jnp.where(plane_id == k, ref[k], col)

        return lax.fori_loop(0, planes, one, jnp.zeros((planes, LANES), f32))

    slope = column(zs)
    slope_wide = jnp.concatenate([slope] * 8, axis=1)
    kx_lane = (lax.broadcasted_iota(jnp.int32, (1, NY), 1) % KX + 1).astype(f32)

    def slope_diff(values, f, part):
        low = jnp.where(mz > 0, halo_recv[f, 0, part:part + 1, :], 0.0)
        high = jnp.where(mz < gz - 1, halo_recv[f, 1, part:part + 1, :], 0.0)
        above = jnp.concatenate([values[1:], high], axis=0)
        below = jnp.concatenate([low, values[:-1]], axis=0)
        return slope_wide * (above - below)

    for part in range(2):
        halo_send[0, 0, part:part + 1, :] = vel[2, part, planes - 1:planes, :]
        halo_send[0, 1, part:part + 1, :] = vel[2, part, 0:1, :]
    stage(1, vel[1, 0], vel[1, 1])
    pl.semaphore_wait(barrier, 2 * (gy - 1))
    halo_w = halo_copies(0)
    halo_w[0].start()
    halo_w[1].start()
    y_send(send_f, recv_f, f_ssem, f_rsem, 1)

    halo_w[0].wait_recv()
    halo_w[1].wait_recv()
    stage(0, slope_diff(vel[2, 0], 0, 0) - kx_lane * vel[0, 1], slope_diff(vel[2, 1], 0, 1) + kx_lane * vel[0, 0])
    y_send(send_f, recv_f, f_ssem, f_rsem, 0)

    row = lax.broadcasted_iota(jnp.int32, (8, LANES), 0)
    lane = lax.broadcasted_iota(jnp.int32, (8, LANES), 1)
    offset = jnp.where(row < 2, 0, jnp.where(row < 4, 2, jnp.where((row == 4) | (row == 6), 1, -511)))
    ky_int = 4 * lane + offset
    ky_int = jnp.where((row == 1) | (row == 3) | (row >= 6), -ky_int, ky_int)
    ky_int = jnp.where((row == 1) & (lane == 0), -512, ky_int)
    ky = ky_int.astype(f32)
    kx = (me + 1).astype(f32)
    square = kx * kx + ky * ky

    def rows_of(k):
        return pl.ds(pl.multiple_of(k * 8, 8), 8)

    def factor(k, state):
        r, g = state
        low, up = zl[k], zu[k]
        inverse = 1.0 / (-(low + up) - square - low * r)
        m = low * inverse
        r = up * inverse
        g = -m * g
        inv_piv[rows_of(k), :] = inverse
        mult[rows_of(k), :] = m
        ratio[rows_of(k), :] = r
        beta[rows_of(k), :] = g
        return r, g

    zero = jnp.zeros((8, LANES), f32)
    one_v = jnp.ones((8, LANES), f32)
    lax.fori_loop(0, planes, factor, (zero, one_v))

    def unfold(i, state):
        b, g = state
        k = planes - 1 - i
        r = ratio[rows_of(k), :]
        b = beta[rows_of(k), :] - r * b
        g = -r * g
        beta[rows_of(k), :] = b
        gamma[rows_of(k), :] = g
        return b, g

    b0, g0 = lax.fori_loop(0, planes, unfold, (zero, one_v))
    last = slice((planes - 1) * 8, planes * 8)
    mat_all[mz, 0] = b0
    mat_all[mz, 1] = g0
    mat_all[mz, 2] = beta[last, :]
    mat_all[mz, 3] = gamma[last, :]
    z_send(mat_all, m_ssem, m_rsem)
    z_wait_recv(mat_all, m_ssem, m_rsem)

    red_r[0] = zero
    red_e[0, 0] = zero
    red_e[0, 1] = zero

    def reduce_matrix(d, r):
        den = 1.0 / (1.0 - mat_all[d, 0] * r)
        psi = mat_all[d, 1] * den
        br = mat_all[d, 2] * r
        red_den[d] = den
        red_bden[d] = mat_all[d, 0] * den
        red_psi[d] = psi
        red_br[d] = br
        r = mat_all[d, 3] + br * psi
        red_r[d + 1] = r
        return r

    lax.fori_loop(0, gz, reduce_matrix, zero)

    copy_ft.wait()
    first_lane = lax.broadcasted_iota(jnp.int32, (planes, LANES), 1) == 0

    def forward(f):
        quarters = []
        for q in range(4):
            block = recv_f[f, 4 * q:4 * q + 4].reshape(LANES, LANES).T
            quarters.append(jnp.concatenate([block[:64], block[64:]], axis=1))
        a = quarters[0] + quarters[2]
        b = quarters[0] - quarters[2]
        c = quarters[1] + quarters[3]
        e = quarters[1] - quarters[3]
        turned = jnp.concatenate([e[planes:], -e[:planes]], axis=0)
        spectra = []
        for first, z in ((0, a + c), (256, a - c)):
            both = product(z, ftab[0, :, first:first + 256], ftab[1, :, first:first + 256])
            rc, rs = both[:planes, :128], both[:planes, 128:]
            ic, is_ = both[planes:, :128], both[planes:, 128:]
            if first == 0:
                rs0, is0 = jnp.where(first_lane, 0.0, rs), jnp.where(first_lane, 0.0, is_)
                spectra.append((rc + is0, ic - rs0))
                spectra.append((jnp.where(first_lane, rs, rc - is_), jnp.where(first_lane, is_, ic + rs)))
            else:
                spectra.append((rc + is_, ic - rs))
                spectra.append((rc - is_, ic + rs))
        both = product(jnp.concatenate([b + turned, b - turned], axis=0), ftab[0, :, 512:], ftab[1, :, 512:])
        for half in range(2):
            cos, sin = both[:, half * 128:half * 128 + 128], both[:, 256 + half * 128:384 + half * 128]
            spectra.append((cos[:planes] + sin[planes:2 * planes], cos[planes:2 * planes] - sin[:planes]))
        for half in range(2):
            cos, sin = both[:, half * 128:half * 128 + 128], both[:, 256 + half * 128:384 + half * 128]
            spectra.append((cos[2 * planes:3 * planes] - sin[3 * planes:], cos[3 * planes:] + sin[2 * planes:3 * planes]))
        return spectra

    y_wait_recv(send_f, recv_f, f_ssem, f_rsem, 1)
    for s, (re, im) in enumerate(forward(1)):
        ky_row = ky[s:s + 1, :]
        vhat[s, 0] = -ky_row * im
        vhat[s, 1] = ky_row * re
    y_wait_recv(send_f, recv_f, f_ssem, f_rsem, 0)
    for s, (re, im) in enumerate(forward(0)):
        field_re[pl.ds(s, planes, stride=8), :] = re + vhat[s, 0]
        field_im[pl.ds(s, planes, stride=8), :] = im + vhat[s, 1]

    def down(k, state):
        sr, si = state
        inverse, m = inv_piv[rows_of(k), :], mult[rows_of(k), :]
        sr = field_re[rows_of(k), :] * inverse - m * sr
        si = field_im[rows_of(k), :] * inverse - m * si
        field_re[rows_of(k), :] = sr
        field_im[rows_of(k), :] = si
        return sr, si

    lax.fori_loop(0, planes, down, (zero, zero), unroll=True)

    def back(i, state):
        ar, ai = state
        k = planes - 1 - i
        r = ratio[rows_of(k), :]
        ar = field_re[rows_of(k), :] - r * ar
        ai = field_im[rows_of(k), :] - r * ai
        field_re[rows_of(k), :] = ar
        field_im[rows_of(k), :] = ai
        return ar, ai

    ar, ai = lax.fori_loop(0, planes, back, (zero, zero), unroll=True)
    rhs_all[mz, 0] = ar
    rhs_all[mz, 1] = ai
    rhs_all[mz, 2] = field_re[last, :]
    rhs_all[mz, 3] = field_im[last, :]
    z_send(rhs_all, r_ssem, r_rsem)
    z_wait_recv(rhs_all, r_ssem, r_rsem)

    def reduce_rhs(d, state):
        er, ei = state
        den, bden, br, b31 = red_den[d], red_bden[d], red_br[d], mat_all[d, 2]
        pr = den * rhs_all[d, 0] + bden * er
        pi = den * rhs_all[d, 1] + bden * ei
        er = rhs_all[d, 2] + b31 * er + br * pr
        ei = rhs_all[d, 3] + b31 * ei + br * pi
        red_phi[d, 0] = pr
        red_phi[d, 1] = pi
        red_e[d + 1, 0] = er
        red_e[d + 1, 1] = ei
        return er, ei

    lax.fori_loop(0, gz, reduce_rhs, (zero, zero), unroll=True)
    red_f[gz, 0] = zero
    red_f[gz, 1] = zero

    def reduce_back(i, state):
        fr, fi = state
        d = gz - 1 - i
        psi = red_psi[d]
        fr = red_phi[d, 0] + psi * fr
        fi = red_phi[d, 1] + psi * fi
        red_f[d, 0] = fr
        red_f[d, 1] = fi
        return fr, fi

    lax.fori_loop(0, gz, reduce_back, (zero, zero), unroll=True)
    before = [red_e[mz, part] + red_r[mz] * red_f[mz, part] for part in range(2)]
    after = [red_f[mz + 1, part] for part in range(2)]

    def finish(k, _):
        b, g = beta[rows_of(k), :], gamma[rows_of(k), :]
        field_re[rows_of(k), :] = field_re[rows_of(k), :] + b * before[0] + g * after[0]
        field_im[rows_of(k), :] = field_im[rows_of(k), :] + b * before[1] + g * after[1]
        return 0

    lax.fori_loop(0, planes, finish, 0, unroll=True)

    copy_it.wait()

    def inverse(f, spectra):
        parts = []
        for first in (0, 256):
            (pr, pi), (nr, ni) = spectra[first // 128], spectra[first // 128 + 1]
            cr, sr, ci, si = pr + nr, ni - pi, pi + ni, pr - nr
            if first == 0:
                cr, sr = jnp.where(first_lane, pr, cr), jnp.where(first_lane, nr, sr)
                ci, si = jnp.where(first_lane, pi, ci), jnp.where(first_lane, ni, si)
            z = jnp.concatenate([jnp.concatenate([cr, sr], axis=1), jnp.concatenate([ci, si], axis=1)], axis=0)
            parts.append(product(z, itab[0, first:first + 256, :], itab[1, first:first + 256, :]))
        (ar, ai), (br, bi), (cr, ci), (dr, di) = spectra[4:]
        z = jnp.concatenate([
            jnp.concatenate([ar, br, -ai, -bi], axis=1),
            jnp.concatenate([ai, bi, ar, br], axis=1),
            jnp.concatenate([cr, dr, ci, di], axis=1),
            jnp.concatenate([ci, di, -cr, -dr], axis=1)], axis=0)
        odd = product(z, itab[0, 512:, :], itab[1, 512:, :])
        g1, g3 = odd[:64], odd[64:]
        s02, d02 = parts[0] + parts[1], parts[0] - parts[1]
        s13, d13 = g1 + g3, g1 - g3
        turned = jnp.concatenate([-d13[planes:], d13[:planes]], axis=0)
        for q, value in enumerate((s02 + s13, d02 + turned, s02 - s13, d02 - turned)):
            block = jnp.concatenate([value[:, :128], value[:, 128:]], axis=0).T
            send_b[f, 4 * q:4 * q + 4] = block.reshape(4, 32, LANES)

    tiles = [(field_re[pl.ds(s, planes, stride=8), :], field_im[pl.ds(s, planes, stride=8), :]) for s in range(8)]
    inverse(0, tiles)
    y_send(send_b, recv_b, b_ssem, b_rsem, 0)
    inverse(1, [(-ky[s:s + 1, :] * im, ky[s:s + 1, :] * re) for s, (re, im) in enumerate(tiles)])
    y_send(send_b, recv_b, b_ssem, b_rsem, 1)

    def unstage(f):
        for j in range(KX):
            rows_buf[pl.ds(j, 32, stride=16), :] = recv_b[f, j]
        for c in range(4):
            block = rows_buf[c * 128:(c + 1) * 128, :].T
            for h in range(2):
                for part in range(2):
                    first = h * 64 + part * 32
                    grad[part, :, h * 512 + c * 128:h * 512 + c * 128 + 128] = block[first:first + 32]

    y_wait_recv(send_b, recv_b, b_ssem, b_rsem, 0)
    unstage(0)
    for part in range(2):
        halo_send[1, 0, part:part + 1, :] = grad[part, planes - 1:planes, :]
        halo_send[1, 1, part:part + 1, :] = grad[part, 0:1, :]
    halo_p = halo_copies(1)
    halo_p[0].start()
    halo_p[1].start()
    out[0, 0] = vel[0, 0] + kx_lane * grad[1]
    out[0, 1] = vel[0, 1] - kx_lane * grad[0]
    halo_p[0].wait_recv()
    halo_p[1].wait_recv()
    for part in range(2):
        out[2, part] = vel[2, part] - slope_diff(grad[part], 1, part)
    y_wait_recv(send_b, recv_b, b_ssem, b_rsem, 1)
    unstage(1)
    for part in range(2):
        out[1, part] = vel[1, part] - grad[part]

    for copy in (*halo_w, *halo_p):
        copy.wait_send()
    for f in range(2):
        y_wait_send(send_f, recv_f, f_ssem, f_rsem, f)
        y_wait_send(send_b, recv_b, b_ssem, b_rsem, f)
    z_wait_send(mat_all, m_ssem, m_rsem)
    z_wait_send(rhs_all, r_ssem, r_rsem)


def shards(velocity, z_lower, z_upper, z_slope):
    gy, gz = lax.axis_size("gy"), lax.axis_size("gz")
    planes = velocity.shape[2]
    ftab, itab = (jnp.asarray(table) for table in fourier_tables())
    f32 = jnp.float32
    vmem = pl.BlockSpec(memory_space=pltpu.VMEM)
    smem = pl.BlockSpec(memory_space=pltpu.SMEM)
    hbm = pl.BlockSpec(memory_space=pl.ANY)
    lines = (planes * 8, LANES)
    dma = pltpu.SemaphoreType.DMA
    return pl.pallas_call(
        functools.partial(kernel, planes, gy, gz),
        out_shape=jax.ShapeDtypeStruct(velocity.shape, f32),
        in_specs=[vmem, smem, smem, smem, hbm, hbm],
        out_specs=vmem,
        scratch_shapes=[
            pltpu.VMEM(ftab.shape, jnp.bfloat16),
            pltpu.VMEM(itab.shape, jnp.bfloat16),
            pltpu.VMEM((512, LANES), f32),
            pltpu.VMEM((2, gy, 32, LANES), f32),
            pltpu.VMEM((2, gy, 32, LANES), f32),
            pltpu.VMEM((2, gy, 32, LANES), f32),
            pltpu.VMEM((2, gy, 32, LANES), f32),
            pltpu.VMEM((2, 2, 2, NY), f32),
            pltpu.VMEM((2, 2, 2, NY), f32),
            pltpu.VMEM((8, 2, planes, LANES), f32),
            pltpu.VMEM(lines, f32),
            pltpu.VMEM(lines, f32),
            pltpu.VMEM(lines, f32),
            pltpu.VMEM(lines, f32),
            pltpu.VMEM(lines, f32),
            pltpu.VMEM(lines, f32),
            pltpu.VMEM(lines, f32),
            pltpu.VMEM((gz, 4, 8, LANES), f32),
            pltpu.VMEM((gz, 4, 8, LANES), f32),
            pltpu.VMEM((gz, 8, LANES), f32),
            pltpu.VMEM((gz, 8, LANES), f32),
            pltpu.VMEM((gz, 8, LANES), f32),
            pltpu.VMEM((gz, 8, LANES), f32),
            pltpu.VMEM((gz, 8, LANES), f32),
            pltpu.VMEM((gz + 1, 8, LANES), f32),
            pltpu.VMEM((gz + 1, 2, 8, LANES), f32),
            pltpu.VMEM((gz, 2, 8, LANES), f32),
            pltpu.VMEM((gz + 1, 2, 8, LANES), f32),
            pltpu.VMEM((2, planes, NY), f32),
            dma((2,)), dma((2, 2)), dma((2, 2)),
            dma((2, gy)), dma((2, gy)), dma((2, gy)), dma((2, gy)),
            dma((gz,)), dma((gz,)), dma((gz,)), dma((gz,)),
        ],
        compiler_params=pltpu.CompilerParams(
            collective_id=0, has_side_effects=True, vmem_limit_bytes=40 * 1024 * 1024
        ),
        name="project",
    )(velocity, z_lower, z_upper, z_slope, ftab, itab)


def solution(mesh):
    placed = (P(None, None, "gz", "gy"), P("gz"), P("gz"), P("gz"))
    return jax.shard_map(
        shards, mesh=mesh, in_specs=placed, out_specs=P(None, None, "gz", "gy"), check_vma=False
    )
```

```python
import functools

import jax
import jax.numpy as jnp
import ml_dtypes
import numpy as np
from jax import lax
from jax.experimental import pallas as pl
from jax.experimental.pallas import tpu as pltpu
from jax.sharding import PartitionSpec as P

NY = 1024
KX = 16
LANES = 128
MESH = pl.DeviceIdType.MESH


def fourier_tables():
    place = np.arange(256)
    y = 64 * ((place % 128) // 32) + 32 * (place // 128) + place % 32

    def pair(m):
        phase = 2.0 * np.pi * ((y[:, None] * m[None, :]) % NY) / NY
        return np.cos(phase), np.sin(phase)

    c0, s0 = pair(4 * np.arange(128))
    s0[:, 0] = (-1.0) ** y
    c2, s2 = pair(4 * np.arange(128) + 2)
    c1, s1 = pair(4 * np.arange(256) + 1)
    table = np.concatenate([c0, s0, c2, s2, c1, s1], axis=1)

    def split(values):
        high = values.astype(ml_dtypes.bfloat16)
        low = (values - high.astype(np.float64)).astype(ml_dtypes.bfloat16)
        return np.stack([high, low])

    return split(table), split(table.T / NY)


def dot(a, b):
    return jnp.dot(a, b, preferred_element_type=jnp.float32)


def product(values, high, low):
    top = values.astype(jnp.bfloat16)
    rest = (values - top.astype(jnp.float32)).astype(jnp.bfloat16)
    rows = values.shape[0]
    both = dot(jnp.concatenate([top, rest], axis=0), high)
    return both[:rows] + both[rows:] + dot(top, low)


def kernel(
    planes, gy, gz,
    vel_hbm, zl_hbm, zu_hbm, zs_hbm, ftab_hbm, itab_hbm, out_hbm,
    vel, out, zl, zu, zs, ftab, itab, rows_buf, send_f, recv_f, send_b, recv_b,
    halo_send, halo_recv, vhat, field_re, field_im,
    inv_piv, mult, ratio, beta, gamma,
    mat_all, rhs_all, red_den, red_bden, red_psi, red_b31, red_br, red_r, red_e, red_phi, red_f,
    grad,
    in_sem, out_sem, halo_ssem, halo_rsem, f_ssem, f_rsem, b_ssem, b_rsem, m_ssem, m_rsem, r_ssem, r_rsem,
):
    me = lax.axis_index("gy")
    mz = lax.axis_index("gz")
    f32 = jnp.float32

    copy_in = [pltpu.make_async_copy(vel_hbm.at[c], vel.at[c], in_sem.at[c]) for c in range(3)]
    copy_z = [
        pltpu.make_async_copy(src, dst, in_sem.at[3 + i])
        for i, (src, dst) in enumerate(((zl_hbm, zl), (zu_hbm, zu), (zs_hbm, zs)))
    ]
    copy_ft = pltpu.make_async_copy(ftab_hbm, ftab, in_sem.at[6])
    copy_it = pltpu.make_async_copy(itab_hbm, itab, in_sem.at[7])
    copy_out = [pltpu.make_async_copy(out.at[c], out_hbm.at[c], out_sem.at[c]) for c in range(3)]
    copy_in[1].start()
    copy_in[2].start()
    barrier = pltpu.get_barrier_semaphore()

    def greet(o, _):
        pl.semaphore_signal(barrier, inc=1, device_id={"gy": lax.rem(me + o, gy)}, device_id_type=MESH)
        pl.semaphore_signal(barrier, inc=1, device_id={"gz": lax.rem(mz + o, gz)}, device_id_type=MESH)
        return 0

    lax.fori_loop(1, gy, greet, 0)
    for copy in (copy_z[2], copy_in[0], copy_z[0], copy_z[1], copy_ft, copy_it):
        copy.start()

    def stage(f, re, im):
        for c in range(4):
            a = slice(c * 128, c * 128 + 128)
            b = slice(512 + c * 128, 512 + c * 128 + 128)
            block = jnp.concatenate([re[:, a], im[:, a], re[:, b], im[:, b]], axis=0)
            rows_buf[c * 128:(c + 1) * 128, :] = block.T
        for j in range(KX):
            send_f[f, j] = rows_buf[pl.ds(j, 32, stride=16), :]

    def y_copy(src, dst, ssem, rsem, f, o, slot_src, slot_dst):
        return pltpu.make_async_remote_copy(
            src_ref=src.at[f, slot_src], dst_ref=dst.at[f, slot_dst],
            send_sem=ssem.at[f, o], recv_sem=rsem.at[f, o],
            device_id={"gy": lax.rem(me + o, gy)}, device_id_type=MESH)

    def y_send(src, dst, ssem, rsem, f):
        def one(o, _):
            y_copy(src, dst, ssem, rsem, f, o, lax.rem(me + o, gy), me).start()
            return 0

        lax.fori_loop(1, gy, one, 0)
        dst[f, me] = src[f, me]

    def y_wait_recv(src, dst, ssem, rsem, f):
        def one(o, _):
            d = lax.rem(me + gy - o, gy)
            y_copy(src, dst, ssem, rsem, f, o, d, d).wait_recv()
            return 0

        lax.fori_loop(1, gy, one, 0)

    def y_wait_send(src, dst, ssem, rsem, f):
        def one(o, _):
            y_copy(src, dst, ssem, rsem, f, o, lax.rem(me + o, gy), me).wait_send()
            return 0

        lax.fori_loop(1, gy, one, 0)

    def z_copy(buf, ssem, rsem, o, slot):
        return pltpu.make_async_remote_copy(
            src_ref=buf.at[slot], dst_ref=buf.at[slot],
            send_sem=ssem.at[o], recv_sem=rsem.at[o],
            device_id={"gz": lax.rem(mz + o, gz)}, device_id_type=MESH)

    def z_send(buf, ssem, rsem):
        def one(o, _):
            z_copy(buf, ssem, rsem, o, mz).start()
            return 0

        lax.fori_loop(1, gz, one, 0)

    def z_wait_recv(buf, ssem, rsem):
        def one(o, _):
            z_copy(buf, ssem, rsem, o, lax.rem(mz + gz - o, gz)).wait_recv()
            return 0

        lax.fori_loop(1, gz, one, 0)

    def z_wait_send(buf, ssem, rsem):
        def one(o, _):
            z_copy(buf, ssem, rsem, o, mz).wait_send()
            return 0

        lax.fori_loop(1, gz, one, 0)

    def halo_copies(f):
        up = pltpu.make_async_remote_copy(
            src_ref=halo_send.at[f, 0], dst_ref=halo_recv.at[f, 0],
            send_sem=halo_ssem.at[f, 0], recv_sem=halo_rsem.at[f, 0],
            device_id={"gz": lax.rem(mz + 1, gz)}, device_id_type=MESH)
        down = pltpu.make_async_remote_copy(
            src_ref=halo_send.at[f, 1], dst_ref=halo_recv.at[f, 1],
            send_sem=halo_ssem.at[f, 1], recv_sem=halo_rsem.at[f, 1],
            device_id={"gz": lax.rem(mz + gz - 1, gz)}, device_id_type=MESH)
        return up, down

    plane_id = lax.broadcasted_iota(jnp.int32, (planes, LANES), 0)

    def column(ref):
        def one(k, col):
            return jnp.where(plane_id == k, ref[k], col)

        return lax.fori_loop(0, planes, one, jnp.zeros((planes, LANES), f32))

    kx_lane = (lax.broadcasted_iota(jnp.int32, (1, NY), 1) % KX + 1).astype(f32)

    def slope_diff(values, f, part, slope_wide):
        low = jnp.where(mz > 0, halo_recv[f, 0, part:part + 1, :], 0.0)
        high = jnp.where(mz < gz - 1, halo_recv[f, 1, part:part + 1, :], 0.0)
        above = jnp.concatenate([values[1:], high], axis=0)
        below = jnp.concatenate([low, values[:-1]], axis=0)
        return slope_wide * (above - below)

    copy_in[1].wait()
    stage(1, vel[1, 0], vel[1, 1])
    copy_in[2].wait()
    for part in range(2):
        halo_send[0, 0, part:part + 1, :] = vel[2, part, planes - 1:planes, :]
        halo_send[0, 1, part:part + 1, :] = vel[2, part, 0:1, :]
    pl.semaphore_wait(barrier, 2 * (gy - 1))
    halo_w = halo_copies(0)
    halo_w[0].start()
    halo_w[1].start()
    y_send(send_f, recv_f, f_ssem, f_rsem, 1)

    copy_z[2].wait()
    slope = column(zs)
    slope_wide = jnp.concatenate([slope] * 8, axis=1)
    copy_in[0].wait()
    halo_w[0].wait_recv()
    halo_w[1].wait_recv()
    stage(0, slope_diff(vel[2, 0], 0, 0, slope_wide) - kx_lane * vel[0, 1], slope_diff(vel[2, 1], 0, 1, slope_wide) + kx_lane * vel[0, 0])
    y_send(send_f, recv_f, f_ssem, f_rsem, 0)

    copy_z[0].wait()
    copy_z[1].wait()
    row = lax.broadcasted_iota(jnp.int32, (8, LANES), 0)
    lane = lax.broadcasted_iota(jnp.int32, (8, LANES), 1)
    offset = jnp.where(row < 2, 0, jnp.where(row < 4, 2, jnp.where((row == 4) | (row == 6), 1, -511)))
    ky_int = 4 * lane + offset
    ky_int = jnp.where((row == 1) | (row == 3) | (row >= 6), -ky_int, ky_int)
    ky_int = jnp.where((row == 1) & (lane == 0), -512, ky_int)
    ky = ky_int.astype(f32)
    kx = (me + 1).astype(f32)
    square = kx * kx + ky * ky

    def rows_of(k):
        return pl.ds(pl.multiple_of(k * 8, 8), 8)

    def factor(k, state):
        r, g = state
        low, up = zl[k], zu[k]
        inverse = 1.0 / (-(low + up) - square - low * r)
        m = low * inverse
        r = up * inverse
        g = -m * g
        inv_piv[rows_of(k), :] = inverse
        mult[rows_of(k), :] = m
        ratio[rows_of(k), :] = r
        beta[rows_of(k), :] = g
        return r, g

    zero = jnp.zeros((8, LANES), f32)
    one_v = jnp.ones((8, LANES), f32)
    lax.fori_loop(0, planes, factor, (zero, one_v))

    def unfold(i, state):
        b, g = state
        k = planes - 1 - i
        r = ratio[rows_of(k), :]
        b = beta[rows_of(k), :] - r * b
        g = -r * g
        beta[rows_of(k), :] = b
        gamma[rows_of(k), :] = g
        return b, g

    b0, g0 = lax.fori_loop(0, planes, unfold, (zero, one_v))
    last = slice((planes - 1) * 8, planes * 8)
    mat_all[mz, 0] = b0
    mat_all[mz, 1] = g0
    mat_all[mz, 2] = beta[last, :]
    mat_all[mz, 3] = gamma[last, :]
    z_send(mat_all, m_ssem, m_rsem)
    z_wait_recv(mat_all, m_ssem, m_rsem)

    red_r[0] = zero
    red_e[0, 0] = zero
    red_e[0, 1] = zero

    def reduce_matrix(d, r):
        den = 1.0 / (1.0 - mat_all[d, 0] * r)
        psi = mat_all[d, 1] * den
        br = mat_all[d, 2] * r
        red_den[d] = den
        red_bden[d] = mat_all[d, 0] * den
        red_psi[d] = psi
        red_br[d] = br
        r = mat_all[d, 3] + br * psi
        red_r[d + 1] = r
        return r

    lax.fori_loop(0, gz, reduce_matrix, zero)

    copy_ft.wait()
    first_lane = lax.broadcasted_iota(jnp.int32, (planes, LANES), 1) == 0

    def forward(f):
        quarters = []
        for q in range(4):
            block = recv_f[f, 4 * q:4 * q + 4].reshape(LANES, LANES).T
            quarters.append(jnp.concatenate([block[:64], block[64:]], axis=1))
        a = quarters[0] + quarters[2]
        b = quarters[0] - quarters[2]
        c = quarters[1] + quarters[3]
        e = quarters[1] - quarters[3]
        turned = jnp.concatenate([e[planes:], -e[:planes]], axis=0)
        spectra = []
        for first, z in ((0, a + c), (256, a - c)):
            both = product(z, ftab[0, :, first:first + 256], ftab[1, :, first:first + 256])
            rc, rs = both[:planes, :128], both[:planes, 128:]
            ic, is_ = both[planes:, :128], both[planes:, 128:]
            if first == 0:
                rs0, is0 = jnp.where(first_lane, 0.0, rs), jnp.where(first_lane, 0.0, is_)
                spectra.append((rc + is0, ic - rs0))
                spectra.append((jnp.where(first_lane, rs, rc - is_), jnp.where(first_lane, is_, ic + rs)))
            else:
                spectra.append((rc + is_, ic - rs))
                spectra.append((rc - is_, ic + rs))
        both = product(jnp.concatenate([b + turned, b - turned], axis=0), ftab[0, :, 512:], ftab[1, :, 512:])
        for half in range(2):
            cos, sin = both[:, half * 128:half * 128 + 128], both[:, 256 + half * 128:384 + half * 128]
            spectra.append((cos[:planes] + sin[planes:2 * planes], cos[planes:2 * planes] - sin[:planes]))
        for half in range(2):
            cos, sin = both[:, half * 128:half * 128 + 128], both[:, 256 + half * 128:384 + half * 128]
            spectra.append((cos[2 * planes:3 * planes] - sin[3 * planes:], cos[3 * planes:] + sin[2 * planes:3 * planes]))
        return spectra

    y_wait_recv(send_f, recv_f, f_ssem, f_rsem, 1)
    for s, (re, im) in enumerate(forward(1)):
        ky_row = ky[s:s + 1, :]
        vhat[s, 0] = -ky_row * im
        vhat[s, 1] = ky_row * re
    y_wait_recv(send_f, recv_f, f_ssem, f_rsem, 0)
    for s, (re, im) in enumerate(forward(0)):
        field_re[pl.ds(s, planes, stride=8), :] = re + vhat[s, 0]
        field_im[pl.ds(s, planes, stride=8), :] = im + vhat[s, 1]

    def down(k, state):
        sr, si = state
        inverse, m = inv_piv[rows_of(k), :], mult[rows_of(k), :]
        sr = field_re[rows_of(k), :] * inverse - m * sr
        si = field_im[rows_of(k), :] * inverse - m * si
        field_re[rows_of(k), :] = sr
        field_im[rows_of(k), :] = si
        return sr, si

    lax.fori_loop(0, planes, down, (zero, zero), unroll=True)

    def back(i, state):
        ar, ai = state
        k = planes - 1 - i
        r = ratio[rows_of(k), :]
        ar = field_re[rows_of(k), :] - r * ar
        ai = field_im[rows_of(k), :] - r * ai
        field_re[rows_of(k), :] = ar
        field_im[rows_of(k), :] = ai
        return ar, ai

    ar, ai = lax.fori_loop(0, planes, back, (zero, zero), unroll=True)
    rhs_all[mz, 0] = ar
    rhs_all[mz, 1] = ai
    rhs_all[mz, 2] = field_re[last, :]
    rhs_all[mz, 3] = field_im[last, :]
    z_send(rhs_all, r_ssem, r_rsem)
    z_wait_recv(rhs_all, r_ssem, r_rsem)

    def reduce_rhs(d, state):
        er, ei = state
        den, bden, br, b31 = red_den[d], red_bden[d], red_br[d], mat_all[d, 2]
        pr = den * rhs_all[d, 0] + bden * er
        pi = den * rhs_all[d, 1] + bden * ei
        er = rhs_all[d, 2] + b31 * er + br * pr
        ei = rhs_all[d, 3] + b31 * ei + br * pi
        red_phi[d, 0] = pr
        red_phi[d, 1] = pi
        red_e[d + 1, 0] = er
        red_e[d + 1, 1] = ei
        return er, ei

    lax.fori_loop(0, gz, reduce_rhs, (zero, zero), unroll=True)
    red_f[gz, 0] = zero
    red_f[gz, 1] = zero

    def reduce_back(i, state):
        fr, fi = state
        d = gz - 1 - i
        psi = red_psi[d]
        fr = red_phi[d, 0] + psi * fr
        fi = red_phi[d, 1] + psi * fi
        red_f[d, 0] = fr
        red_f[d, 1] = fi
        return fr, fi

    lax.fori_loop(0, gz, reduce_back, (zero, zero), unroll=True)
    before = [red_e[mz, part] + red_r[mz] * red_f[mz, part] for part in range(2)]
    after = [red_f[mz + 1, part] for part in range(2)]

    def finish(k, _):
        b, g = beta[rows_of(k), :], gamma[rows_of(k), :]
        field_re[rows_of(k), :] = field_re[rows_of(k), :] + b * before[0] + g * after[0]
        field_im[rows_of(k), :] = field_im[rows_of(k), :] + b * before[1] + g * after[1]
        return 0

    lax.fori_loop(0, planes, finish, 0, unroll=True)

    copy_it.wait()

    def inverse(f, spectra):
        parts = []
        for first in (0, 256):
            (pr, pi), (nr, ni) = spectra[first // 128], spectra[first // 128 + 1]
            cr, sr, ci, si = pr + nr, ni - pi, pi + ni, pr - nr
            if first == 0:
                cr, sr = jnp.where(first_lane, pr, cr), jnp.where(first_lane, nr, sr)
                ci, si = jnp.where(first_lane, pi, ci), jnp.where(first_lane, ni, si)
            z = jnp.concatenate([jnp.concatenate([cr, sr], axis=1), jnp.concatenate([ci, si], axis=1)], axis=0)
            parts.append(product(z, itab[0, first:first + 256, :], itab[1, first:first + 256, :]))
        (ar, ai), (br, bi), (cr, ci), (dr, di) = spectra[4:]
        z = jnp.concatenate([
            jnp.concatenate([ar, br, -ai, -bi], axis=1),
            jnp.concatenate([ai, bi, ar, br], axis=1),
            jnp.concatenate([cr, dr, ci, di], axis=1),
            jnp.concatenate([ci, di, -cr, -dr], axis=1)], axis=0)
        odd = product(z, itab[0, 512:, :], itab[1, 512:, :])
        g1, g3 = odd[:64], odd[64:]
        s02, d02 = parts[0] + parts[1], parts[0] - parts[1]
        s13, d13 = g1 + g3, g1 - g3
        turned = jnp.concatenate([-d13[planes:], d13[:planes]], axis=0)
        for q, value in enumerate((s02 + s13, d02 + turned, s02 - s13, d02 - turned)):
            block = jnp.concatenate([value[:, :128], value[:, 128:]], axis=0).T
            send_b[f, 4 * q:4 * q + 4] = block.reshape(4, 32, LANES)

    tiles = [(field_re[pl.ds(s, planes, stride=8), :], field_im[pl.ds(s, planes, stride=8), :]) for s in range(8)]
    inverse(0, tiles)
    y_send(send_b, recv_b, b_ssem, b_rsem, 0)
    inverse(1, [(-ky[s:s + 1, :] * im, ky[s:s + 1, :] * re) for s, (re, im) in enumerate(tiles)])
    y_send(send_b, recv_b, b_ssem, b_rsem, 1)

    def unstage(f):
        for j in range(KX):
            rows_buf[pl.ds(j, 32, stride=16), :] = recv_b[f, j]
        for c in range(4):
            block = rows_buf[c * 128:(c + 1) * 128, :].T
            for h in range(2):
                for part in range(2):
                    first = h * 64 + part * 32
                    grad[part, :, h * 512 + c * 128:h * 512 + c * 128 + 128] = block[first:first + 32]

    y_wait_recv(send_b, recv_b, b_ssem, b_rsem, 0)
    unstage(0)
    for part in range(2):
        halo_send[1, 0, part:part + 1, :] = grad[part, planes - 1:planes, :]
        halo_send[1, 1, part:part + 1, :] = grad[part, 0:1, :]
    halo_p = halo_copies(1)
    halo_p[0].start()
    halo_p[1].start()
    out[0, 0] = vel[0, 0] + kx_lane * grad[1]
    out[0, 1] = vel[0, 1] - kx_lane * grad[0]
    copy_out[0].start()
    halo_p[0].wait_recv()
    halo_p[1].wait_recv()
    for part in range(2):
        out[2, part] = vel[2, part] - slope_diff(grad[part], 1, part, slope_wide)
    copy_out[2].start()
    y_wait_recv(send_b, recv_b, b_ssem, b_rsem, 1)
    unstage(1)
    for part in range(2):
        out[1, part] = vel[1, part] - grad[part]
    copy_out[1].start()

    for copy in (*halo_w, *halo_p):
        copy.wait_send()
    for f in range(2):
        y_wait_send(send_f, recv_f, f_ssem, f_rsem, f)
        y_wait_send(send_b, recv_b, b_ssem, b_rsem, f)
    z_wait_send(mat_all, m_ssem, m_rsem)
    z_wait_send(rhs_all, r_ssem, r_rsem)
    for copy in copy_out:
        copy.wait()


def shards(velocity, z_lower, z_upper, z_slope):
    gy, gz = lax.axis_size("gy"), lax.axis_size("gz")
    planes = velocity.shape[2]
    ftab, itab = (jnp.asarray(table) for table in fourier_tables())
    f32 = jnp.float32
    hbm = pl.BlockSpec(memory_space=pl.ANY)
    lines = (planes * 8, LANES)
    dma = pltpu.SemaphoreType.DMA
    return pl.pallas_call(
        functools.partial(kernel, planes, gy, gz),
        out_shape=jax.ShapeDtypeStruct(velocity.shape, f32),
        in_specs=[pl.BlockSpec(memory_space=pltpu.HBM)] * 6,
        out_specs=hbm,
        scratch_shapes=[
            pltpu.VMEM(velocity.shape, f32),
            pltpu.VMEM(velocity.shape, f32),
            pltpu.SMEM((planes,), f32),
            pltpu.SMEM((planes,), f32),
            pltpu.SMEM((planes,), f32),
            pltpu.VMEM(ftab.shape, jnp.bfloat16),
            pltpu.VMEM(itab.shape, jnp.bfloat16),
            pltpu.VMEM((512, LANES), f32),
            pltpu.VMEM((2, gy, 32, LANES), f32),
            pltpu.VMEM((2, gy, 32, LANES), f32),
            pltpu.VMEM((2, gy, 32, LANES), f32),
            pltpu.VMEM((2, gy, 32, LANES), f32),
            pltpu.VMEM((2, 2, 2, NY), f32),
            pltpu.VMEM((2, 2, 2, NY), f32),
            pltpu.VMEM((8, 2, planes, LANES), f32),
            pltpu.VMEM(lines, f32),
            pltpu.VMEM(lines, f32),
            pltpu.VMEM(lines, f32),
            pltpu.VMEM(lines, f32),
            pltpu.VMEM(lines, f32),
            pltpu.VMEM(lines, f32),
            pltpu.VMEM(lines, f32),
            pltpu.VMEM((gz, 4, 8, LANES), f32),
            pltpu.VMEM((gz, 4, 8, LANES), f32),
            pltpu.VMEM((gz, 8, LANES), f32),
            pltpu.VMEM((gz, 8, LANES), f32),
            pltpu.VMEM((gz, 8, LANES), f32),
            pltpu.VMEM((gz, 8, LANES), f32),
            pltpu.VMEM((gz, 8, LANES), f32),
            pltpu.VMEM((gz + 1, 8, LANES), f32),
            pltpu.VMEM((gz + 1, 2, 8, LANES), f32),
            pltpu.VMEM((gz, 2, 8, LANES), f32),
            pltpu.VMEM((gz + 1, 2, 8, LANES), f32),
            pltpu.VMEM((2, planes, NY), f32),
            dma((8,)), dma((3,)), dma((2, 2)), dma((2, 2)),
            dma((2, gy)), dma((2, gy)), dma((2, gy)), dma((2, gy)),
            dma((gz,)), dma((gz,)), dma((gz,)), dma((gz,)),
        ],
        compiler_params=pltpu.CompilerParams(
            collective_id=0, has_side_effects=True, vmem_limit_bytes=40 * 1024 * 1024
        ),
        name="project",
    )(*(pltpu.with_memory_space_constraint(a, pltpu.HBM) for a in (velocity, z_lower, z_upper, z_slope, ftab, itab)))


def solution(mesh):
    placed = (P(None, None, "gz", "gy"), P("gz"), P("gz"), P("gz"))
    return jax.shard_map(
        shards, mesh=mesh, in_specs=placed, out_specs=P(None, None, "gz", "gy"), check_vma=False
    )
```

```python
import functools

import jax
import jax.numpy as jnp
import ml_dtypes
import numpy as np
from jax import lax
from jax.experimental import pallas as pl
from jax.experimental.pallas import tpu as pltpu
from jax.sharding import PartitionSpec as P

NY = 1024
KX = 16
LANES = 128
MESH = pl.DeviceIdType.MESH
Y_ORDER = [(dz, c) for dz in (4, 3, -3, 2, -2, 1, -1) for c in (0, 1)] + [(0, 1)]
Z_ORDER = sorted(
    ((dx, dy) for dx in (2, 1, -1, 0) for dy in (2, 1, -1, 0) if (dx, dy) != (0, 0)),
    key=lambda pair: -abs(pair[0]) - abs(pair[1]),
)


def fourier_tables():
    place = np.arange(256)
    y = 64 * ((place % 128) // 32) + 32 * (place // 128) + place % 32

    def pair(m):
        phase = 2.0 * np.pi * ((y[:, None] * m[None, :]) % NY) / NY
        return np.cos(phase), np.sin(phase)

    c0, s0 = pair(4 * np.arange(128))
    s0[:, 0] = (-1.0) ** y
    c2, s2 = pair(4 * np.arange(128) + 2)
    c1, s1 = pair(4 * np.arange(256) + 1)
    table = np.concatenate([c0, s0, c2, s2, c1, s1], axis=1)

    def split(values):
        high = values.astype(ml_dtypes.bfloat16)
        low = (values - high.astype(np.float64)).astype(ml_dtypes.bfloat16)
        return np.stack([high, low])

    return split(table), split(table.T / NY)


def dot(a, b):
    return jnp.dot(a, b, preferred_element_type=jnp.float32)


def product(values, high, low):
    top = values.astype(jnp.bfloat16)
    rest = (values - top.astype(jnp.float32)).astype(jnp.bfloat16)
    rows = values.shape[0]
    both = dot(jnp.concatenate([top, rest], axis=0), high)
    return both[:rows] + both[rows:] + dot(top, low)


def kernel(
    planes, gy, gz,
    vel_hbm, zl_hbm, zu_hbm, zs_hbm, ftab_hbm, itab_hbm, out_hbm,
    vel, out, zl, zu, zs, ftab, itab, rows_buf, send_f, recv_f, send_b, recv_b,
    halo_send, halo_recv, vhat, field_re, field_im,
    inv_piv, mult, ratio, beta, gamma,
    mat_all, rhs_all, red_den, red_bden, red_psi, red_b31, red_br, red_r, red_e, red_phi, red_f,
    grad,
    in_sem, out_sem, halo_ssem, halo_rsem, f_ssem, f_rsem, b_ssem, b_rsem, m_ssem, m_rsem, r_ssem, r_rsem,
):
    me = lax.axis_index("gy")
    mz = lax.axis_index("gz")
    f32 = jnp.float32

    copy_in = [pltpu.make_async_copy(vel_hbm.at[c], vel.at[c], in_sem.at[c]) for c in range(3)]
    copy_z = [
        pltpu.make_async_copy(src, dst, in_sem.at[3 + i])
        for i, (src, dst) in enumerate(((zl_hbm, zl), (zu_hbm, zu), (zs_hbm, zs)))
    ]
    copy_ft = pltpu.make_async_copy(ftab_hbm, ftab, in_sem.at[6])
    copy_it = pltpu.make_async_copy(itab_hbm, itab, in_sem.at[7])
    copy_out = [pltpu.make_async_copy(out.at[c], out_hbm.at[c], out_sem.at[c]) for c in range(3)]
    copy_in[1].start()
    copy_in[2].start()
    barrier = pltpu.get_barrier_semaphore()

    def y_partner(o, sign):
        dz, c = Y_ORDER[o]
        return lax.rem(me // 2 + sign * dz + gy // 2, gy // 2) * 2 + lax.rem(me + c, 2)

    def z_partner(o, sign):
        dx, dy = Z_ORDER[o]
        return lax.rem(mz // 4 + sign * dx + 4, 4) * 4 + lax.rem(mz + sign * dy + 4, 4)

    y_all, z_all = range(len(Y_ORDER)), range(len(Z_ORDER))
    for o in y_all:
        pl.semaphore_signal(barrier, inc=1, device_id={"gy": y_partner(o, 1)}, device_id_type=MESH)
    for o in z_all:
        pl.semaphore_signal(barrier, inc=1, device_id={"gz": z_partner(o, 1)}, device_id_type=MESH)
    for copy in (copy_z[2], copy_in[0], copy_z[0], copy_z[1], copy_ft, copy_it):
        copy.start()

    def stage(f, re, im):
        for c in range(4):
            a = slice(c * 128, c * 128 + 128)
            b = slice(512 + c * 128, 512 + c * 128 + 128)
            block = jnp.concatenate([re[:, a], im[:, a], re[:, b], im[:, b]], axis=0)
            rows_buf[c * 128:(c + 1) * 128, :] = block.T
        for j in range(KX):
            send_f[f, j] = rows_buf[pl.ds(j, 32, stride=16), :]

    def y_copy(src, dst, ssem, rsem, f, o, slot_src, slot_dst):
        return pltpu.make_async_remote_copy(
            src_ref=src.at[f, slot_src], dst_ref=dst.at[f, slot_dst],
            send_sem=ssem.at[f, o], recv_sem=rsem.at[f, o],
            device_id={"gy": y_partner(o, 1)}, device_id_type=MESH)

    def y_send(src, dst, ssem, rsem, f):
        for o in y_all:
            y_copy(src, dst, ssem, rsem, f, o, y_partner(o, 1), me).start()
        dst[f, me] = src[f, me]

    def y_wait_recv(src, dst, ssem, rsem, f):
        for o in y_all:
            d = y_partner(o, -1)
            y_copy(src, dst, ssem, rsem, f, o, d, d).wait_recv()

    def y_wait_send(src, dst, ssem, rsem, f):
        for o in y_all:
            y_copy(src, dst, ssem, rsem, f, o, y_partner(o, 1), me).wait_send()

    def z_copy(buf, ssem, rsem, o, slot):
        return pltpu.make_async_remote_copy(
            src_ref=buf.at[slot], dst_ref=buf.at[slot],
            send_sem=ssem.at[o], recv_sem=rsem.at[o],
            device_id={"gz": z_partner(o, 1)}, device_id_type=MESH)

    def z_send(buf, ssem, rsem):
        for o in z_all:
            z_copy(buf, ssem, rsem, o, mz).start()

    def z_wait_recv(buf, ssem, rsem):
        for o in z_all:
            z_copy(buf, ssem, rsem, o, z_partner(o, -1)).wait_recv()

    def z_wait_send(buf, ssem, rsem):
        for o in z_all:
            z_copy(buf, ssem, rsem, o, mz).wait_send()

    def halo_copies(f):
        up = pltpu.make_async_remote_copy(
            src_ref=halo_send.at[f, 0], dst_ref=halo_recv.at[f, 0],
            send_sem=halo_ssem.at[f, 0], recv_sem=halo_rsem.at[f, 0],
            device_id={"gz": lax.rem(mz + 1, gz)}, device_id_type=MESH)
        down = pltpu.make_async_remote_copy(
            src_ref=halo_send.at[f, 1], dst_ref=halo_recv.at[f, 1],
            send_sem=halo_ssem.at[f, 1], recv_sem=halo_rsem.at[f, 1],
            device_id={"gz": lax.rem(mz + gz - 1, gz)}, device_id_type=MESH)
        return up, down

    plane_id = lax.broadcasted_iota(jnp.int32, (planes, LANES), 0)

    def column(ref):
        def one(k, col):
            return jnp.where(plane_id == k, ref[k], col)

        return lax.fori_loop(0, planes, one, jnp.zeros((planes, LANES), f32))

    kx_lane = (lax.broadcasted_iota(jnp.int32, (1, NY), 1) % KX + 1).astype(f32)

    def slope_diff(values, f, part, slope_wide):
        low = jnp.where(mz > 0, halo_recv[f, 0, part:part + 1, :], 0.0)
        high = jnp.where(mz < gz - 1, halo_recv[f, 1, part:part + 1, :], 0.0)
        above = jnp.concatenate([values[1:], high], axis=0)
        below = jnp.concatenate([low, values[:-1]], axis=0)
        return slope_wide * (above - below)

    copy_in[1].wait()
    stage(1, vel[1, 0], vel[1, 1])
    copy_in[2].wait()
    for part in range(2):
        halo_send[0, 0, part:part + 1, :] = vel[2, part, planes - 1:planes, :]
        halo_send[0, 1, part:part + 1, :] = vel[2, part, 0:1, :]
    pl.semaphore_wait(barrier, len(Y_ORDER) + len(Z_ORDER))
    halo_w = halo_copies(0)
    halo_w[0].start()
    halo_w[1].start()
    y_send(send_f, recv_f, f_ssem, f_rsem, 1)

    copy_z[2].wait()
    slope = column(zs)
    slope_wide = jnp.concatenate([slope] * 8, axis=1)
    copy_in[0].wait()
    halo_w[0].wait_recv()
    halo_w[1].wait_recv()
    stage(0, slope_diff(vel[2, 0], 0, 0, slope_wide) - kx_lane * vel[0, 1], slope_diff(vel[2, 1], 0, 1, slope_wide) + kx_lane * vel[0, 0])
    y_send(send_f, recv_f, f_ssem, f_rsem, 0)

    copy_z[0].wait()
    copy_z[1].wait()
    row = lax.broadcasted_iota(jnp.int32, (8, LANES), 0)
    lane = lax.broadcasted_iota(jnp.int32, (8, LANES), 1)
    offset = jnp.where(row < 2, 0, jnp.where(row < 4, 2, jnp.where((row == 4) | (row == 6), 1, -511)))
    ky_int = 4 * lane + offset
    ky_int = jnp.where((row == 1) | (row == 3) | (row >= 6), -ky_int, ky_int)
    ky_int = jnp.where((row == 1) & (lane == 0), -512, ky_int)
    ky = ky_int.astype(f32)
    kx = (me + 1).astype(f32)
    square = kx * kx + ky * ky

    def rows_of(k):
        return pl.ds(pl.multiple_of(k * 8, 8), 8)

    def factor(k, state):
        r, g = state
        low, up = zl[k], zu[k]
        inverse = 1.0 / (-(low + up) - square - low * r)
        m = low * inverse
        r = up * inverse
        g = -m * g
        inv_piv[rows_of(k), :] = inverse
        mult[rows_of(k), :] = m
        ratio[rows_of(k), :] = r
        beta[rows_of(k), :] = g
        return r, g

    zero = jnp.zeros((8, LANES), f32)
    one_v = jnp.ones((8, LANES), f32)
    lax.fori_loop(0, planes, factor, (zero, one_v))

    def unfold(i, state):
        b, g = state
        k = planes - 1 - i
        r = ratio[rows_of(k), :]
        b = beta[rows_of(k), :] - r * b
        g = -r * g
        beta[rows_of(k), :] = b
        gamma[rows_of(k), :] = g
        return b, g

    b0, g0 = lax.fori_loop(0, planes, unfold, (zero, one_v))
    last = slice((planes - 1) * 8, planes * 8)
    mat_all[mz, 0] = b0
    mat_all[mz, 1] = g0
    mat_all[mz, 2] = beta[last, :]
    mat_all[mz, 3] = gamma[last, :]
    z_send(mat_all, m_ssem, m_rsem)
    z_wait_recv(mat_all, m_ssem, m_rsem)

    red_r[0] = zero
    red_e[0, 0] = zero
    red_e[0, 1] = zero

    def reduce_matrix(d, r):
        den = 1.0 / (1.0 - mat_all[d, 0] * r)
        psi = mat_all[d, 1] * den
        br = mat_all[d, 2] * r
        red_den[d] = den
        red_bden[d] = mat_all[d, 0] * den
        red_psi[d] = psi
        red_br[d] = br
        r = mat_all[d, 3] + br * psi
        red_r[d + 1] = r
        return r

    lax.fori_loop(0, gz, reduce_matrix, zero)

    copy_ft.wait()
    first_lane = lax.broadcasted_iota(jnp.int32, (planes, LANES), 1) == 0

    def forward(f):
        quarters = []
        for q in range(4):
            block = recv_f[f, 4 * q:4 * q + 4].reshape(LANES, LANES).T
            quarters.append(jnp.concatenate([block[:64], block[64:]], axis=1))
        a = quarters[0] + quarters[2]
        b = quarters[0] - quarters[2]
        c = quarters[1] + quarters[3]
        e = quarters[1] - quarters[3]
        turned = jnp.concatenate([e[planes:], -e[:planes]], axis=0)
        spectra = []
        for first, z in ((0, a + c), (256, a - c)):
            both = product(z, ftab[0, :, first:first + 256], ftab[1, :, first:first + 256])
            rc, rs = both[:planes, :128], both[:planes, 128:]
            ic, is_ = both[planes:, :128], both[planes:, 128:]
            if first == 0:
                rs0, is0 = jnp.where(first_lane, 0.0, rs), jnp.where(first_lane, 0.0, is_)
                spectra.append((rc + is0, ic - rs0))
                spectra.append((jnp.where(first_lane, rs, rc - is_), jnp.where(first_lane, is_, ic + rs)))
            else:
                spectra.append((rc + is_, ic - rs))
                spectra.append((rc - is_, ic + rs))
        both = product(jnp.concatenate([b + turned, b - turned], axis=0), ftab[0, :, 512:], ftab[1, :, 512:])
        for half in range(2):
            cos, sin = both[:, half * 128:half * 128 + 128], both[:, 256 + half * 128:384 + half * 128]
            spectra.append((cos[:planes] + sin[planes:2 * planes], cos[planes:2 * planes] - sin[:planes]))
        for half in range(2):
            cos, sin = both[:, half * 128:half * 128 + 128], both[:, 256 + half * 128:384 + half * 128]
            spectra.append((cos[2 * planes:3 * planes] - sin[3 * planes:], cos[3 * planes:] + sin[2 * planes:3 * planes]))
        return spectra

    y_wait_recv(send_f, recv_f, f_ssem, f_rsem, 1)
    for s, (re, im) in enumerate(forward(1)):
        ky_row = ky[s:s + 1, :]
        vhat[s, 0] = -ky_row * im
        vhat[s, 1] = ky_row * re
    y_wait_recv(send_f, recv_f, f_ssem, f_rsem, 0)
    for s, (re, im) in enumerate(forward(0)):
        field_re[pl.ds(s, planes, stride=8), :] = re + vhat[s, 0]
        field_im[pl.ds(s, planes, stride=8), :] = im + vhat[s, 1]

    def down(k, state):
        sr, si = state
        inverse, m = inv_piv[rows_of(k), :], mult[rows_of(k), :]
        sr = field_re[rows_of(k), :] * inverse - m * sr
        si = field_im[rows_of(k), :] * inverse - m * si
        field_re[rows_of(k), :] = sr
        field_im[rows_of(k), :] = si
        return sr, si

    lax.fori_loop(0, planes, down, (zero, zero), unroll=True)

    def back(i, state):
        ar, ai = state
        k = planes - 1 - i
        r = ratio[rows_of(k), :]
        ar = field_re[rows_of(k), :] - r * ar
        ai = field_im[rows_of(k), :] - r * ai
        field_re[rows_of(k), :] = ar
        field_im[rows_of(k), :] = ai
        return ar, ai

    ar, ai = lax.fori_loop(0, planes, back, (zero, zero), unroll=True)
    rhs_all[mz, 0] = ar
    rhs_all[mz, 1] = ai
    rhs_all[mz, 2] = field_re[last, :]
    rhs_all[mz, 3] = field_im[last, :]
    z_send(rhs_all, r_ssem, r_rsem)
    z_wait_recv(rhs_all, r_ssem, r_rsem)

    def reduce_rhs(d, state):
        er, ei = state
        den, bden, br, b31 = red_den[d], red_bden[d], red_br[d], mat_all[d, 2]
        pr = den * rhs_all[d, 0] + bden * er
        pi = den * rhs_all[d, 1] + bden * ei
        er = rhs_all[d, 2] + b31 * er + br * pr
        ei = rhs_all[d, 3] + b31 * ei + br * pi
        red_phi[d, 0] = pr
        red_phi[d, 1] = pi
        red_e[d + 1, 0] = er
        red_e[d + 1, 1] = ei
        return er, ei

    lax.fori_loop(0, gz, reduce_rhs, (zero, zero), unroll=True)
    red_f[gz, 0] = zero
    red_f[gz, 1] = zero

    def reduce_back(i, state):
        fr, fi = state
        d = gz - 1 - i
        psi = red_psi[d]
        fr = red_phi[d, 0] + psi * fr
        fi = red_phi[d, 1] + psi * fi
        red_f[d, 0] = fr
        red_f[d, 1] = fi
        return fr, fi

    lax.fori_loop(0, gz, reduce_back, (zero, zero), unroll=True)
    before = [red_e[mz, part] + red_r[mz] * red_f[mz, part] for part in range(2)]
    after = [red_f[mz + 1, part] for part in range(2)]

    def finish(k, _):
        b, g = beta[rows_of(k), :], gamma[rows_of(k), :]
        field_re[rows_of(k), :] = field_re[rows_of(k), :] + b * before[0] + g * after[0]
        field_im[rows_of(k), :] = field_im[rows_of(k), :] + b * before[1] + g * after[1]
        return 0

    lax.fori_loop(0, planes, finish, 0, unroll=True)

    copy_it.wait()

    def inverse(f, spectra):
        parts = []
        for first in (0, 256):
            (pr, pi), (nr, ni) = spectra[first // 128], spectra[first // 128 + 1]
            cr, sr, ci, si = pr + nr, ni - pi, pi + ni, pr - nr
            if first == 0:
                cr, sr = jnp.where(first_lane, pr, cr), jnp.where(first_lane, nr, sr)
                ci, si = jnp.where(first_lane, pi, ci), jnp.where(first_lane, ni, si)
            z = jnp.concatenate([jnp.concatenate([cr, sr], axis=1), jnp.concatenate([ci, si], axis=1)], axis=0)
            parts.append(product(z, itab[0, first:first + 256, :], itab[1, first:first + 256, :]))
        (ar, ai), (br, bi), (cr, ci), (dr, di) = spectra[4:]
        z = jnp.concatenate([
            jnp.concatenate([ar, br, -ai, -bi], axis=1),
            jnp.concatenate([ai, bi, ar, br], axis=1),
            jnp.concatenate([cr, dr, ci, di], axis=1),
            jnp.concatenate([ci, di, -cr, -dr], axis=1)], axis=0)
        odd = product(z, itab[0, 512:, :], itab[1, 512:, :])
        g1, g3 = odd[:64], odd[64:]
        s02, d02 = parts[0] + parts[1], parts[0] - parts[1]
        s13, d13 = g1 + g3, g1 - g3
        turned = jnp.concatenate([-d13[planes:], d13[:planes]], axis=0)
        for q, value in enumerate((s02 + s13, d02 + turned, s02 - s13, d02 - turned)):
            block = jnp.concatenate([value[:, :128], value[:, 128:]], axis=0).T
            send_b[f, 4 * q:4 * q + 4] = block.reshape(4, 32, LANES)

    tiles = [(field_re[pl.ds(s, planes, stride=8), :], field_im[pl.ds(s, planes, stride=8), :]) for s in range(8)]
    inverse(0, tiles)
    y_send(send_b, recv_b, b_ssem, b_rsem, 0)
    inverse(1, [(-ky[s:s + 1, :] * im, ky[s:s + 1, :] * re) for s, (re, im) in enumerate(tiles)])
    y_send(send_b, recv_b, b_ssem, b_rsem, 1)

    def unstage(f):
        for j in range(KX):
            rows_buf[pl.ds(j, 32, stride=16), :] = recv_b[f, j]
        for c in range(4):
            block = rows_buf[c * 128:(c + 1) * 128, :].T
            for h in range(2):
                for part in range(2):
                    first = h * 64 + part * 32
                    grad[part, :, h * 512 + c * 128:h * 512 + c * 128 + 128] = block[first:first + 32]

    y_wait_recv(send_b, recv_b, b_ssem, b_rsem, 0)
    unstage(0)
    for part in range(2):
        halo_send[1, 0, part:part + 1, :] = grad[part, planes - 1:planes, :]
        halo_send[1, 1, part:part + 1, :] = grad[part, 0:1, :]
    halo_p = halo_copies(1)
    halo_p[0].start()
    halo_p[1].start()
    out[0, 0] = vel[0, 0] + kx_lane * grad[1]
    out[0, 1] = vel[0, 1] - kx_lane * grad[0]
    copy_out[0].start()
    halo_p[0].wait_recv()
    halo_p[1].wait_recv()
    for part in range(2):
        out[2, part] = vel[2, part] - slope_diff(grad[part], 1, part, slope_wide)
    copy_out[2].start()
    y_wait_recv(send_b, recv_b, b_ssem, b_rsem, 1)
    unstage(1)
    for part in range(2):
        out[1, part] = vel[1, part] - grad[part]
    copy_out[1].start()

    for copy in (*halo_w, *halo_p):
        copy.wait_send()
    for f in range(2):
        y_wait_send(send_f, recv_f, f_ssem, f_rsem, f)
        y_wait_send(send_b, recv_b, b_ssem, b_rsem, f)
    z_wait_send(mat_all, m_ssem, m_rsem)
    z_wait_send(rhs_all, r_ssem, r_rsem)
    for copy in copy_out:
        copy.wait()


def shards(velocity, z_lower, z_upper, z_slope):
    gy, gz = lax.axis_size("gy"), lax.axis_size("gz")
    planes = velocity.shape[2]
    ftab, itab = (jnp.asarray(table) for table in fourier_tables())
    f32 = jnp.float32
    hbm = pl.BlockSpec(memory_space=pl.ANY)
    lines = (planes * 8, LANES)
    dma = pltpu.SemaphoreType.DMA
    return pl.pallas_call(
        functools.partial(kernel, planes, gy, gz),
        out_shape=jax.ShapeDtypeStruct(velocity.shape, f32),
        in_specs=[pl.BlockSpec(memory_space=pltpu.HBM)] * 6,
        out_specs=hbm,
        scratch_shapes=[
            pltpu.VMEM(velocity.shape, f32),
            pltpu.VMEM(velocity.shape, f32),
            pltpu.SMEM((planes,), f32),
            pltpu.SMEM((planes,), f32),
            pltpu.SMEM((planes,), f32),
            pltpu.VMEM(ftab.shape, jnp.bfloat16),
            pltpu.VMEM(itab.shape, jnp.bfloat16),
            pltpu.VMEM((512, LANES), f32),
            pltpu.VMEM((2, gy, 32, LANES), f32),
            pltpu.VMEM((2, gy, 32, LANES), f32),
            pltpu.VMEM((2, gy, 32, LANES), f32),
            pltpu.VMEM((2, gy, 32, LANES), f32),
            pltpu.VMEM((2, 2, 2, NY), f32),
            pltpu.VMEM((2, 2, 2, NY), f32),
            pltpu.VMEM((8, 2, planes, LANES), f32),
            pltpu.VMEM(lines, f32),
            pltpu.VMEM(lines, f32),
            pltpu.VMEM(lines, f32),
            pltpu.VMEM(lines, f32),
            pltpu.VMEM(lines, f32),
            pltpu.VMEM(lines, f32),
            pltpu.VMEM(lines, f32),
            pltpu.VMEM((gz, 4, 8, LANES), f32),
            pltpu.VMEM((gz, 4, 8, LANES), f32),
            pltpu.VMEM((gz, 8, LANES), f32),
            pltpu.VMEM((gz, 8, LANES), f32),
            pltpu.VMEM((gz, 8, LANES), f32),
            pltpu.VMEM((gz, 8, LANES), f32),
            pltpu.VMEM((gz, 8, LANES), f32),
            pltpu.VMEM((gz + 1, 8, LANES), f32),
            pltpu.VMEM((gz + 1, 2, 8, LANES), f32),
            pltpu.VMEM((gz, 2, 8, LANES), f32),
            pltpu.VMEM((gz + 1, 2, 8, LANES), f32),
            pltpu.VMEM((2, planes, NY), f32),
            dma((8,)), dma((3,)), dma((2, 2)), dma((2, 2)),
            dma((2, gy)), dma((2, gy)), dma((2, gy)), dma((2, gy)),
            dma((gz,)), dma((gz,)), dma((gz,)), dma((gz,)),
        ],
        compiler_params=pltpu.CompilerParams(
            collective_id=0, has_side_effects=True, vmem_limit_bytes=40 * 1024 * 1024
        ),
        name="project",
    )(*(pltpu.with_memory_space_constraint(a, pltpu.HBM) for a in (velocity, z_lower, z_upper, z_slope, ftab, itab)))


def solution(mesh):
    placed = (P(None, None, "gz", "gy"), P("gz"), P("gz"), P("gz"))
    return jax.shard_map(
        shards, mesh=mesh, in_specs=placed, out_specs=P(None, None, "gz", "gy"), check_vma=False
    )
```

```python
import functools

import jax
import jax.numpy as jnp
import ml_dtypes
import numpy as np
from jax import lax
from jax.experimental import pallas as pl
from jax.experimental.pallas import tpu as pltpu
from jax.sharding import PartitionSpec as P

NY = 1024
KX = 16
LANES = 128
MESH = pl.DeviceIdType.MESH
Y_ORDER = (4, 3, -3, 2, -2, 1, -1)
Z_ORDER = sorted(
    ((dx, dy) for dx in (2, 1, -1, 0) for dy in (2, 1, -1, 0) if (dx, dy) != (0, 0)),
    key=lambda pair: -abs(pair[0]) - abs(pair[1]),
)


def fourier_tables():
    place = np.arange(256)
    y = 64 * ((place % 128) // 32) + 32 * (place // 128) + place % 32

    def pair(m):
        phase = 2.0 * np.pi * ((y[:, None] * m[None, :]) % NY) / NY
        return np.cos(phase), np.sin(phase)

    c0, s0 = pair(4 * np.arange(128))
    s0[:, 0] = (-1.0) ** y
    c2, s2 = pair(4 * np.arange(128) + 2)
    c1, s1 = pair(4 * np.arange(256) + 1)
    table = np.concatenate([c0, s0, c2, s2, c1, s1], axis=1)

    def split(values):
        high = values.astype(ml_dtypes.bfloat16)
        low = (values - high.astype(np.float64)).astype(ml_dtypes.bfloat16)
        return np.stack([high, low])

    return split(table), split(table.T / NY)


def dot(a, b):
    return jnp.dot(a, b, preferred_element_type=jnp.float32)


def product(values, high, low):
    top = values.astype(jnp.bfloat16)
    rest = (values - top.astype(jnp.float32)).astype(jnp.bfloat16)
    rows = values.shape[0]
    both = dot(jnp.concatenate([top, rest], axis=0), high)
    return both[:rows] + both[rows:] + dot(top, low)


def kernel(
    planes, gy, gz,
    vel_hbm, zl_hbm, zu_hbm, zs_hbm, ftab_hbm, itab_hbm, out,
    vel, zl, zu, zs, ftab, itab, rows_buf, send_f, recv_f, send_b, recv_b,
    halo_send, halo_recv, vhat, field_re, field_im,
    inv_piv, mult, ratio, beta, gamma,
    mat_all, rhs_all, red_den, red_bden, red_psi, red_b31, red_br, red_r, red_e, red_phi, red_f,
    grad, grad_q,
    in_sem, halo_ssem, halo_rsem, f_ssem, f_rsem, b_ssem, b_rsem, m_ssem, m_rsem, r_ssem, r_rsem,
):
    me = lax.axis_index("gy")
    mz = lax.axis_index("gz")
    f32 = jnp.float32

    copy_in = [pltpu.make_async_copy(vel_hbm.at[c], vel.at[c], in_sem.at[c]) for c in range(3)]
    copy_z = [
        pltpu.make_async_copy(src, dst, in_sem.at[3 + i])
        for i, (src, dst) in enumerate(((zl_hbm, zl), (zu_hbm, zu), (zs_hbm, zs)))
    ]
    copy_ft = pltpu.make_async_copy(ftab_hbm, ftab, in_sem.at[6])
    copy_it = pltpu.make_async_copy(itab_hbm, itab, in_sem.at[7])
    copy_in[1].start()
    copy_in[2].start()
    barrier = pltpu.get_barrier_semaphore()

    chips, chip, core = gy // 2, me // 2, lax.rem(me, 2)
    mate = me + 1 - 2 * core

    def y_partner(dz, c):
        return lax.rem(chip + dz + chips, chips) * 2 + c

    def z_partner(o, sign):
        dx, dy = Z_ORDER[o]
        return lax.rem(mz // 4 + sign * dx + 4, 4) * 4 + lax.rem(mz + sign * dy + 4, 4)

    z_all = range(len(Z_ORDER))
    y_all = [y_partner(dz, c) for dz in Y_ORDER for c in range(2)] + [mate]
    for g in y_all:
        pl.semaphore_signal(barrier, inc=1, device_id={"gy": g}, device_id_type=MESH)
    for o in z_all:
        pl.semaphore_signal(barrier, inc=1, device_id={"gz": z_partner(o, 1)}, device_id_type=MESH)
    for copy in (copy_z[2], copy_in[0], copy_z[0], copy_z[1], copy_ft, copy_it):
        copy.start()

    def stage(f, re, im):
        for c in range(4):
            a = slice(c * 128, c * 128 + 128)
            b = slice(512 + c * 128, 512 + c * 128 + 128)
            block = jnp.concatenate([re[:, a], im[:, a], re[:, b], im[:, b]], axis=0)
            rows_buf[c * 128:(c + 1) * 128, :] = block.T
        for j in range(KX):
            send_f[f, j] = rows_buf[pl.ds(j, 32, stride=16), :]

    def y_copy(src, dst, ssem, rsem, f, g):
        return pltpu.make_async_remote_copy(
            src_ref=src.at[f, g], dst_ref=dst.at[f, me],
            send_sem=ssem.at[f, g], recv_sem=rsem.at[f, me],
            device_id={"gy": g}, device_id_type=MESH)

    def y_send(src, dst, ssem, rsem, f, partners):
        for g in partners:
            y_copy(src, dst, ssem, rsem, f, g).start()

    def y_wait_recv(src, dst, ssem, rsem, f):
        for g in y_all:
            pltpu.make_async_remote_copy(
                src_ref=src.at[f, g], dst_ref=dst.at[f, g],
                send_sem=ssem.at[f, g], recv_sem=rsem.at[f, g],
                device_id={"gy": g}, device_id_type=MESH).wait_recv()

    def y_wait_send(src, dst, ssem, rsem, f):
        for g in y_all:
            y_copy(src, dst, ssem, rsem, f, g).wait_send()

    def z_copy(buf, ssem, rsem, o, slot):
        return pltpu.make_async_remote_copy(
            src_ref=buf.at[slot], dst_ref=buf.at[slot],
            send_sem=ssem.at[o], recv_sem=rsem.at[o],
            device_id={"gz": z_partner(o, 1)}, device_id_type=MESH)

    def z_send(buf, ssem, rsem):
        for o in z_all:
            z_copy(buf, ssem, rsem, o, mz).start()

    def z_wait_recv(buf, ssem, rsem):
        for o in z_all:
            z_copy(buf, ssem, rsem, o, z_partner(o, -1)).wait_recv()

    def z_wait_send(buf, ssem, rsem):
        for o in z_all:
            z_copy(buf, ssem, rsem, o, mz).wait_send()

    def halo_copies(f):
        up = pltpu.make_async_remote_copy(
            src_ref=halo_send.at[f, 0], dst_ref=halo_recv.at[f, 0],
            send_sem=halo_ssem.at[f, 0], recv_sem=halo_rsem.at[f, 0],
            device_id={"gz": lax.rem(mz + 1, gz)}, device_id_type=MESH)
        down = pltpu.make_async_remote_copy(
            src_ref=halo_send.at[f, 1], dst_ref=halo_recv.at[f, 1],
            send_sem=halo_ssem.at[f, 1], recv_sem=halo_rsem.at[f, 1],
            device_id={"gz": lax.rem(mz + gz - 1, gz)}, device_id_type=MESH)
        return up, down

    plane_id = lax.broadcasted_iota(jnp.int32, (planes, LANES), 0)

    def column(ref):
        def one(k, col):
            return jnp.where(plane_id == k, ref[k], col)

        return lax.fori_loop(0, planes, one, jnp.zeros((planes, LANES), f32))

    kx_lane = (lax.broadcasted_iota(jnp.int32, (1, NY), 1) % KX + 1).astype(f32)

    def slope_diff(values, f, part, slope_wide):
        low = jnp.where(mz > 0, halo_recv[f, 0, part:part + 1, :], 0.0)
        high = jnp.where(mz < gz - 1, halo_recv[f, 1, part:part + 1, :], 0.0)
        above = jnp.concatenate([values[1:], high], axis=0)
        below = jnp.concatenate([low, values[:-1]], axis=0)
        return slope_wide * (above - below)

    copy_in[1].wait()
    stage(1, vel[1, 0], vel[1, 1])
    copy_in[2].wait()
    for part in range(2):
        halo_send[0, 0, part:part + 1, :] = vel[2, part, planes - 1:planes, :]
        halo_send[0, 1, part:part + 1, :] = vel[2, part, 0:1, :]
    pl.semaphore_wait(barrier, len(y_all) + len(Z_ORDER))
    halo_w = halo_copies(0)
    halo_w[0].start()
    halo_w[1].start()
    to_core = [[y_partner(dz, c) for dz in Y_ORDER] for c in range(2)]
    y_send(send_f, recv_f, f_ssem, f_rsem, 1, to_core[0] + [mate] + to_core[1][:4])
    recv_f[1, me] = send_f[1, me]

    copy_z[2].wait()
    slope = column(zs)
    slope_wide = jnp.concatenate([slope] * 8, axis=1)
    copy_in[0].wait()
    halo_w[0].wait_recv()
    halo_w[1].wait_recv()
    stage(0, slope_diff(vel[2, 0], 0, 0, slope_wide) - kx_lane * vel[0, 1], slope_diff(vel[2, 1], 0, 1, slope_wide) + kx_lane * vel[0, 0])
    y_send(send_f, recv_f, f_ssem, f_rsem, 0, to_core[0] + [mate])
    y_send(send_f, recv_f, f_ssem, f_rsem, 1, to_core[1][4:])
    y_send(send_f, recv_f, f_ssem, f_rsem, 0, to_core[1])
    recv_f[0, me] = send_f[0, me]

    copy_z[0].wait()
    copy_z[1].wait()
    row = lax.broadcasted_iota(jnp.int32, (8, LANES), 0)
    lane = lax.broadcasted_iota(jnp.int32, (8, LANES), 1)
    offset = jnp.where(row < 2, 0, jnp.where(row < 4, 2, jnp.where((row == 4) | (row == 6), 1, -511)))
    ky_int = 4 * lane + offset
    ky_int = jnp.where((row == 1) | (row == 3) | (row >= 6), -ky_int, ky_int)
    ky_int = jnp.where((row == 1) & (lane == 0), -512, ky_int)
    ky = ky_int.astype(f32)
    kx = (me + 1).astype(f32)
    square = kx * kx + ky * ky

    def rows_of(k):
        return pl.ds(pl.multiple_of(k * 8, 8), 8)

    def factor(k, state):
        r, g = state
        low, up = zl[k], zu[k]
        inverse = 1.0 / (-(low + up) - square - low * r)
        m = low * inverse
        r = up * inverse
        g = -m * g
        inv_piv[rows_of(k), :] = inverse
        mult[rows_of(k), :] = m
        ratio[rows_of(k), :] = r
        beta[rows_of(k), :] = g
        return r, g

    zero = jnp.zeros((8, LANES), f32)
    one_v = jnp.ones((8, LANES), f32)
    lax.fori_loop(0, planes, factor, (zero, one_v))

    def unfold(i, state):
        b, g = state
        k = planes - 1 - i
        r = ratio[rows_of(k), :]
        b = beta[rows_of(k), :] - r * b
        g = -r * g
        beta[rows_of(k), :] = b
        gamma[rows_of(k), :] = g
        return b, g

    b0, g0 = lax.fori_loop(0, planes, unfold, (zero, one_v))
    last = slice((planes - 1) * 8, planes * 8)
    mat_all[mz, 0] = b0
    mat_all[mz, 1] = g0
    mat_all[mz, 2] = beta[last, :]
    mat_all[mz, 3] = gamma[last, :]
    z_send(mat_all, m_ssem, m_rsem)

    copy_ft.wait()
    first_lane = lax.broadcasted_iota(jnp.int32, (planes, LANES), 1) == 0

    def forward(f):
        quarters = []
        for q in range(4):
            block = recv_f[f, 4 * q:4 * q + 4].reshape(LANES, LANES).T
            quarters.append(jnp.concatenate([block[:64], block[64:]], axis=1))
        a = quarters[0] + quarters[2]
        b = quarters[0] - quarters[2]
        c = quarters[1] + quarters[3]
        e = quarters[1] - quarters[3]
        turned = jnp.concatenate([e[planes:], -e[:planes]], axis=0)
        spectra = []
        for first, z in ((0, a + c), (256, a - c)):
            both = product(z, ftab[0, :, first:first + 256], ftab[1, :, first:first + 256])
            rc, rs = both[:planes, :128], both[:planes, 128:]
            ic, is_ = both[planes:, :128], both[planes:, 128:]
            if first == 0:
                rs0, is0 = jnp.where(first_lane, 0.0, rs), jnp.where(first_lane, 0.0, is_)
                spectra.append((rc + is0, ic - rs0))
                spectra.append((jnp.where(first_lane, rs, rc - is_), jnp.where(first_lane, is_, ic + rs)))
            else:
                spectra.append((rc + is_, ic - rs))
                spectra.append((rc - is_, ic + rs))
        both = product(jnp.concatenate([b + turned, b - turned], axis=0), ftab[0, :, 512:], ftab[1, :, 512:])
        for half in range(2):
            cos, sin = both[:, half * 128:half * 128 + 128], both[:, 256 + half * 128:384 + half * 128]
            spectra.append((cos[:planes] + sin[planes:2 * planes], cos[planes:2 * planes] - sin[:planes]))
        for half in range(2):
            cos, sin = both[:, half * 128:half * 128 + 128], both[:, 256 + half * 128:384 + half * 128]
            spectra.append((cos[2 * planes:3 * planes] - sin[3 * planes:], cos[3 * planes:] + sin[2 * planes:3 * planes]))
        return spectra

    y_wait_recv(send_f, recv_f, f_ssem, f_rsem, 1)
    for s, (re, im) in enumerate(forward(1)):
        ky_row = ky[s:s + 1, :]
        vhat[s, 0] = -ky_row * im
        vhat[s, 1] = ky_row * re
    y_wait_recv(send_f, recv_f, f_ssem, f_rsem, 0)
    for s, (re, im) in enumerate(forward(0)):
        field_re[pl.ds(s, planes, stride=8), :] = re + vhat[s, 0]
        field_im[pl.ds(s, planes, stride=8), :] = im + vhat[s, 1]

    def down(k, state):
        sr, si = state
        inverse, m = inv_piv[rows_of(k), :], mult[rows_of(k), :]
        sr = field_re[rows_of(k), :] * inverse - m * sr
        si = field_im[rows_of(k), :] * inverse - m * si
        field_re[rows_of(k), :] = sr
        field_im[rows_of(k), :] = si
        return sr, si

    lax.fori_loop(0, planes, down, (zero, zero), unroll=True)

    def back(i, state):
        ar, ai = state
        k = planes - 1 - i
        r = ratio[rows_of(k), :]
        ar = field_re[rows_of(k), :] - r * ar
        ai = field_im[rows_of(k), :] - r * ai
        field_re[rows_of(k), :] = ar
        field_im[rows_of(k), :] = ai
        return ar, ai

    ar, ai = lax.fori_loop(0, planes, back, (zero, zero), unroll=True)
    rhs_all[mz, 0] = ar
    rhs_all[mz, 1] = ai
    rhs_all[mz, 2] = field_re[last, :]
    rhs_all[mz, 3] = field_im[last, :]
    z_send(rhs_all, r_ssem, r_rsem)

    z_wait_recv(mat_all, m_ssem, m_rsem)
    red_r[0] = zero
    red_e[0, 0] = zero
    red_e[0, 1] = zero

    def reduce_matrix(d, r):
        den = 1.0 / (1.0 - mat_all[d, 0] * r)
        psi = mat_all[d, 1] * den
        br = mat_all[d, 2] * r
        red_den[d] = den
        red_bden[d] = mat_all[d, 0] * den
        red_psi[d] = psi
        red_br[d] = br
        r = mat_all[d, 3] + br * psi
        red_r[d + 1] = r
        return r

    lax.fori_loop(0, gz, reduce_matrix, zero)
    z_wait_recv(rhs_all, r_ssem, r_rsem)

    def reduce_rhs(d, state):
        er, ei = state
        den, bden, br, b31 = red_den[d], red_bden[d], red_br[d], mat_all[d, 2]
        pr = den * rhs_all[d, 0] + bden * er
        pi = den * rhs_all[d, 1] + bden * ei
        er = rhs_all[d, 2] + b31 * er + br * pr
        ei = rhs_all[d, 3] + b31 * ei + br * pi
        red_phi[d, 0] = pr
        red_phi[d, 1] = pi
        red_e[d + 1, 0] = er
        red_e[d + 1, 1] = ei
        return er, ei

    lax.fori_loop(0, gz, reduce_rhs, (zero, zero), unroll=True)
    red_f[gz, 0] = zero
    red_f[gz, 1] = zero

    def reduce_back(i, state):
        fr, fi = state
        d = gz - 1 - i
        psi = red_psi[d]
        fr = red_phi[d, 0] + psi * fr
        fi = red_phi[d, 1] + psi * fi
        red_f[d, 0] = fr
        red_f[d, 1] = fi
        return fr, fi

    lax.fori_loop(0, gz, reduce_back, (zero, zero), unroll=True)
    before = [red_e[mz, part] + red_r[mz] * red_f[mz, part] for part in range(2)]
    after = [red_f[mz + 1, part] for part in range(2)]

    def finish(k, _):
        b, g = beta[rows_of(k), :], gamma[rows_of(k), :]
        field_re[rows_of(k), :] = field_re[rows_of(k), :] + b * before[0] + g * after[0]
        field_im[rows_of(k), :] = field_im[rows_of(k), :] + b * before[1] + g * after[1]
        return 0

    lax.fori_loop(0, planes, finish, 0, unroll=True)

    copy_it.wait()

    def inverse(f, spectra):
        parts = []
        for first in (0, 256):
            (pr, pi), (nr, ni) = spectra[first // 128], spectra[first // 128 + 1]
            cr, sr, ci, si = pr + nr, ni - pi, pi + ni, pr - nr
            if first == 0:
                cr, sr = jnp.where(first_lane, pr, cr), jnp.where(first_lane, nr, sr)
                ci, si = jnp.where(first_lane, pi, ci), jnp.where(first_lane, ni, si)
            z = jnp.concatenate([jnp.concatenate([cr, sr], axis=1), jnp.concatenate([ci, si], axis=1)], axis=0)
            parts.append(product(z, itab[0, first:first + 256, :], itab[1, first:first + 256, :]))
        (ar, ai), (br, bi), (cr, ci), (dr, di) = spectra[4:]
        z = jnp.concatenate([
            jnp.concatenate([ar, br, -ai, -bi], axis=1),
            jnp.concatenate([ai, bi, ar, br], axis=1),
            jnp.concatenate([cr, dr, ci, di], axis=1),
            jnp.concatenate([ci, di, -cr, -dr], axis=1)], axis=0)
        odd = product(z, itab[0, 512:, :], itab[1, 512:, :])
        g1, g3 = odd[:64], odd[64:]
        s02, d02 = parts[0] + parts[1], parts[0] - parts[1]
        s13, d13 = g1 + g3, g1 - g3
        turned = jnp.concatenate([-d13[planes:], d13[:planes]], axis=0)
        for q, value in enumerate((s02 + s13, d02 + turned, s02 - s13, d02 - turned)):
            block = jnp.concatenate([value[:, :128], value[:, 128:]], axis=0).T
            send_b[f, 4 * q:4 * q + 4] = block.reshape(4, 32, LANES)

    tiles = [(field_re[pl.ds(s, planes, stride=8), :], field_im[pl.ds(s, planes, stride=8), :]) for s in range(8)]
    inverse(0, tiles)
    y_send(send_b, recv_b, b_ssem, b_rsem, 0, y_all)
    recv_b[0, me] = send_b[0, me]
    inverse(1, [(-ky[s:s + 1, :] * im, ky[s:s + 1, :] * re) for s, (re, im) in enumerate(tiles)])
    y_send(send_b, recv_b, b_ssem, b_rsem, 1, y_all)
    recv_b[1, me] = send_b[1, me]

    def unstage(f, grad):
        for j in range(KX):
            rows_buf[pl.ds(j, 32, stride=16), :] = recv_b[f, j]
        for c in range(4):
            block = rows_buf[c * 128:(c + 1) * 128, :].T
            for h in range(2):
                for part in range(2):
                    first = h * 64 + part * 32
                    grad[part, :, h * 512 + c * 128:h * 512 + c * 128 + 128] = block[first:first + 32]

    for copy in halo_w:
        copy.wait_send()
    for f in range(2):
        y_wait_send(send_f, recv_f, f_ssem, f_rsem, f)
    z_wait_send(mat_all, m_ssem, m_rsem)
    z_wait_send(rhs_all, r_ssem, r_rsem)
    y_wait_recv(send_b, recv_b, b_ssem, b_rsem, 0)
    unstage(0, grad)
    for part in range(2):
        halo_send[1, 0, part:part + 1, :] = grad[part, planes - 1:planes, :]
        halo_send[1, 1, part:part + 1, :] = grad[part, 0:1, :]
    halo_p = halo_copies(1)
    halo_p[0].start()
    halo_p[1].start()
    out[0, 0] = vel[0, 0] + kx_lane * grad[1]
    out[0, 1] = vel[0, 1] - kx_lane * grad[0]
    y_wait_send(send_b, recv_b, b_ssem, b_rsem, 0)
    y_wait_recv(send_b, recv_b, b_ssem, b_rsem, 1)
    unstage(1, grad_q)
    for part in range(2):
        out[1, part] = vel[1, part] - grad_q[part]
    halo_p[0].wait_recv()
    halo_p[1].wait_recv()
    for part in range(2):
        out[2, part] = vel[2, part] - slope_diff(grad[part], 1, part, slope_wide)

    for copy in halo_p:
        copy.wait_send()
    y_wait_send(send_b, recv_b, b_ssem, b_rsem, 1)


def shards(velocity, z_lower, z_upper, z_slope):
    gy, gz = lax.axis_size("gy"), lax.axis_size("gz")
    planes = velocity.shape[2]
    ftab, itab = (jnp.asarray(table) for table in fourier_tables())
    f32 = jnp.float32
    hbm = pl.BlockSpec(memory_space=pl.ANY)
    lines = (planes * 8, LANES)
    dma = pltpu.SemaphoreType.DMA
    return pl.pallas_call(
        functools.partial(kernel, planes, gy, gz),
        out_shape=jax.ShapeDtypeStruct(velocity.shape, f32),
        in_specs=[pl.BlockSpec(memory_space=pltpu.HBM)] * 6,
        out_specs=pl.BlockSpec(memory_space=pltpu.VMEM),
        scratch_shapes=[
            pltpu.VMEM(velocity.shape, f32),
            pltpu.SMEM((planes,), f32),
            pltpu.SMEM((planes,), f32),
            pltpu.SMEM((planes,), f32),
            pltpu.VMEM(ftab.shape, jnp.bfloat16),
            pltpu.VMEM(itab.shape, jnp.bfloat16),
            pltpu.VMEM((512, LANES), f32),
            pltpu.VMEM((2, gy, 32, LANES), f32),
            pltpu.VMEM((2, gy, 32, LANES), f32),
            pltpu.VMEM((2, gy, 32, LANES), f32),
            pltpu.VMEM((2, gy, 32, LANES), f32),
            pltpu.VMEM((2, 2, 2, NY), f32),
            pltpu.VMEM((2, 2, 2, NY), f32),
            pltpu.VMEM((8, 2, planes, LANES), f32),
            pltpu.VMEM(lines, f32),
            pltpu.VMEM(lines, f32),
            pltpu.VMEM(lines, f32),
            pltpu.VMEM(lines, f32),
            pltpu.VMEM(lines, f32),
            pltpu.VMEM(lines, f32),
            pltpu.VMEM(lines, f32),
            pltpu.VMEM((gz, 4, 8, LANES), f32),
            pltpu.VMEM((gz, 4, 8, LANES), f32),
            pltpu.VMEM((gz, 8, LANES), f32),
            pltpu.VMEM((gz, 8, LANES), f32),
            pltpu.VMEM((gz, 8, LANES), f32),
            pltpu.VMEM((gz, 8, LANES), f32),
            pltpu.VMEM((gz, 8, LANES), f32),
            pltpu.VMEM((gz + 1, 8, LANES), f32),
            pltpu.VMEM((gz + 1, 2, 8, LANES), f32),
            pltpu.VMEM((gz, 2, 8, LANES), f32),
            pltpu.VMEM((gz + 1, 2, 8, LANES), f32),
            pltpu.VMEM((2, planes, NY), f32),
            pltpu.VMEM((2, planes, NY), f32),
            dma((8,)), dma((2, 2)), dma((2, 2)),
            dma((2, gy)), dma((2, gy)), dma((2, gy)), dma((2, gy)),
            dma((gz,)), dma((gz,)), dma((gz,)), dma((gz,)),
        ],
        compiler_params=pltpu.CompilerParams(
            collective_id=0, has_side_effects=True, vmem_limit_bytes=40 * 1024 * 1024
        ),
        name="project",
    )(*(pltpu.with_memory_space_constraint(a, pltpu.HBM) for a in (velocity, z_lower, z_upper, z_slope, ftab, itab)))


def solution(mesh):
    placed = (P(None, None, "gz", "gy"), P("gz"), P("gz"), P("gz"))
    return jax.shard_map(
        shards, mesh=mesh, in_specs=placed, out_specs=P(None, None, "gz", "gy"), check_vma=False
    )
```

```python
import functools

import jax
import jax.numpy as jnp
import ml_dtypes
import numpy as np
from jax import lax
from jax.experimental import pallas as pl
from jax.experimental.pallas import tpu as pltpu
from jax.sharding import PartitionSpec as P

NY = 1024
KX = 16
LANES = 128
MESH = pl.DeviceIdType.MESH
Y_ORDER = (4, 3, -3, 2, -2, 1, -1)
Z_ORDER = sorted(
    ((dx, dy) for dx in (2, 1, -1, 0) for dy in (2, 1, -1, 0) if (dx, dy) != (0, 0)),
    key=lambda pair: -abs(pair[0]) - abs(pair[1]),
)


def fourier_tables():
    place = np.arange(256)
    y = 64 * ((place % 128) // 32) + 32 * (place // 128) + place % 32

    def pair(m):
        phase = 2.0 * np.pi * ((y[:, None] * m[None, :]) % NY) / NY
        return np.cos(phase), np.sin(phase)

    c0, s0 = pair(4 * np.arange(128))
    s0[:, 0] = (-1.0) ** y
    c2, s2 = pair(4 * np.arange(128) + 2)
    c1, s1 = pair(4 * np.arange(256) + 1)
    table = np.concatenate([c0, s0, c2, s2, c1, s1], axis=1)

    def split(values):
        high = values.astype(ml_dtypes.bfloat16)
        low = (values - high.astype(np.float64)).astype(ml_dtypes.bfloat16)
        return np.stack([high, low])

    return split(table), split(table.T / NY)


def dot(a, b):
    return jnp.dot(a, b, preferred_element_type=jnp.float32)


def product(values, high, low):
    top = values.astype(jnp.bfloat16)
    rest = (values - top.astype(jnp.float32)).astype(jnp.bfloat16)
    rows = values.shape[0]
    both = dot(jnp.concatenate([top, rest], axis=0), high)
    return both[:rows] + both[rows:] + dot(top, low)


def kernel(
    planes, gy, gz,
    vel_hbm, zl_hbm, zu_hbm, zs_hbm, ftab_hbm, itab_hbm, out,
    vel, zl, zu, zs, ftab, itab, rows_buf, send_f, recv_f, send_b, recv_b,
    halo_send, halo_recv, vhat, field_re, field_im,
    inv_piv, mult, ratio, beta, gamma,
    mat_all, rhs_all, red_den, red_bden, red_psi, red_b31, red_br, red_r, red_e, red_phi, red_f,
    grad, grad_q,
    in_sem, halo_ssem, halo_rsem, f_ssem, f_rsem, b_ssem, b_rsem, m_ssem, m_rsem, r_ssem, r_rsem,
):
    me = lax.axis_index("gy")
    mz = lax.axis_index("gz")
    f32 = jnp.float32

    copy_in = [pltpu.make_async_copy(vel_hbm.at[c], vel.at[c], in_sem.at[c]) for c in range(3)]
    copy_z = [
        pltpu.make_async_copy(src, dst, in_sem.at[3 + i])
        for i, (src, dst) in enumerate(((zl_hbm, zl), (zu_hbm, zu), (zs_hbm, zs)))
    ]
    copy_ft = pltpu.make_async_copy(ftab_hbm, ftab, in_sem.at[6])
    copy_it = pltpu.make_async_copy(itab_hbm, itab, in_sem.at[7])
    copy_in[1].start()
    copy_in[2].start()
    barrier = pltpu.get_barrier_semaphore()

    chips, chip, core = gy // 2, me // 2, lax.rem(me, 2)
    mate = me + 1 - 2 * core

    def y_partner(dz, c):
        return lax.rem(chip + dz + chips, chips) * 2 + c

    def z_partner(o, sign):
        dx, dy = Z_ORDER[o]
        return lax.rem(mz // 4 + sign * dx + 4, 4) * 4 + lax.rem(mz + sign * dy + 4, 4)

    z_all = range(len(Z_ORDER))
    y_all = [y_partner(dz, c) for dz in Y_ORDER for c in range(2)] + [mate]
    for g in y_all:
        pl.semaphore_signal(barrier, inc=1, device_id={"gy": g}, device_id_type=MESH)
    for o in z_all:
        pl.semaphore_signal(barrier, inc=1, device_id={"gz": z_partner(o, 1)}, device_id_type=MESH)
    for copy in (copy_z[2], copy_in[0], copy_z[0], copy_z[1], copy_ft, copy_it):
        copy.start()

    def stage(f, re, im):
        for c in range(4):
            a = slice(c * 128, c * 128 + 128)
            b = slice(512 + c * 128, 512 + c * 128 + 128)
            block = jnp.concatenate([re[:, a], im[:, a], re[:, b], im[:, b]], axis=0)
            rows_buf[c * 128:(c + 1) * 128, :] = block.T
        for j in range(KX):
            send_f[f, j] = rows_buf[pl.ds(j, 32, stride=16), :]

    def y_copy(src, dst, ssem, rsem, f, g):
        return pltpu.make_async_remote_copy(
            src_ref=src.at[f, g], dst_ref=dst.at[f, me],
            send_sem=ssem.at[f, g], recv_sem=rsem.at[f, me],
            device_id={"gy": g}, device_id_type=MESH)

    def y_send(src, dst, ssem, rsem, f, partners):
        for g in partners:
            y_copy(src, dst, ssem, rsem, f, g).start()

    def y_send_first(src, dst, ssem, rsem, f, first):
        for t in first:
            @pl.when(chip != t)
            def _():
                y_send(src, dst, ssem, rsem, f, [2 * t, 2 * t + 1])


    def y_wait_recv(src, dst, ssem, rsem, f):
        for g in y_all:
            pltpu.make_async_remote_copy(
                src_ref=src.at[f, g], dst_ref=dst.at[f, g],
                send_sem=ssem.at[f, g], recv_sem=rsem.at[f, g],
                device_id={"gy": g}, device_id_type=MESH).wait_recv()

    def y_wait_send(src, dst, ssem, rsem, f):
        for g in y_all:
            y_copy(src, dst, ssem, rsem, f, g).wait_send()

    def z_copy(buf, ssem, rsem, o, slot):
        return pltpu.make_async_remote_copy(
            src_ref=buf.at[slot], dst_ref=buf.at[slot],
            send_sem=ssem.at[o], recv_sem=rsem.at[o],
            device_id={"gz": z_partner(o, 1)}, device_id_type=MESH)

    def z_send(buf, ssem, rsem):
        for o in z_all:
            z_copy(buf, ssem, rsem, o, mz).start()

    def z_wait_recv(buf, ssem, rsem):
        for o in z_all:
            z_copy(buf, ssem, rsem, o, z_partner(o, -1)).wait_recv()

    def z_wait_send(buf, ssem, rsem):
        for o in z_all:
            z_copy(buf, ssem, rsem, o, mz).wait_send()

    def halo_copies(f):
        up = pltpu.make_async_remote_copy(
            src_ref=halo_send.at[f, 0], dst_ref=halo_recv.at[f, 0],
            send_sem=halo_ssem.at[f, 0], recv_sem=halo_rsem.at[f, 0],
            device_id={"gz": lax.rem(mz + 1, gz)}, device_id_type=MESH)
        down = pltpu.make_async_remote_copy(
            src_ref=halo_send.at[f, 1], dst_ref=halo_recv.at[f, 1],
            send_sem=halo_ssem.at[f, 1], recv_sem=halo_rsem.at[f, 1],
            device_id={"gz": lax.rem(mz + gz - 1, gz)}, device_id_type=MESH)
        return up, down

    plane_id = lax.broadcasted_iota(jnp.int32, (planes, LANES), 0)

    def column(ref):
        def one(k, col):
            return jnp.where(plane_id == k, ref[k], col)

        return lax.fori_loop(0, planes, one, jnp.zeros((planes, LANES), f32))

    kx_lane = (lax.broadcasted_iota(jnp.int32, (1, NY), 1) % KX + 1).astype(f32)

    def slope_diff(values, f, part, slope_wide):
        low = jnp.where(mz > 0, halo_recv[f, 0, part:part + 1, :], 0.0)
        high = jnp.where(mz < gz - 1, halo_recv[f, 1, part:part + 1, :], 0.0)
        above = jnp.concatenate([values[1:], high], axis=0)
        below = jnp.concatenate([low, values[:-1]], axis=0)
        return slope_wide * (above - below)

    copy_in[1].wait()
    stage(1, vel[1, 0], vel[1, 1])
    copy_in[2].wait()
    for part in range(2):
        halo_send[0, 0, part:part + 1, :] = vel[2, part, planes - 1:planes, :]
        halo_send[0, 1, part:part + 1, :] = vel[2, part, 0:1, :]
    pl.semaphore_wait(barrier, len(y_all) + len(Z_ORDER))
    halo_w = halo_copies(0)
    halo_w[0].start()
    halo_w[1].start()
    to_core = [[y_partner(dz, c) for dz in Y_ORDER] for c in range(2)]
    y_send(send_f, recv_f, f_ssem, f_rsem, 1, to_core[0] + [mate] + to_core[1][:4])
    recv_f[1, me] = send_f[1, me]

    copy_z[2].wait()
    slope = column(zs)
    slope_wide = jnp.concatenate([slope] * 8, axis=1)
    copy_in[0].wait()
    halo_w[0].wait_recv()
    halo_w[1].wait_recv()
    stage(0, slope_diff(vel[2, 0], 0, 0, slope_wide) - kx_lane * vel[0, 1], slope_diff(vel[2, 1], 0, 1, slope_wide) + kx_lane * vel[0, 0])
    y_send(send_f, recv_f, f_ssem, f_rsem, 0, to_core[0] + [mate])
    y_send(send_f, recv_f, f_ssem, f_rsem, 1, to_core[1][4:])
    y_send(send_f, recv_f, f_ssem, f_rsem, 0, to_core[1])
    recv_f[0, me] = send_f[0, me]

    copy_z[0].wait()
    copy_z[1].wait()
    row = lax.broadcasted_iota(jnp.int32, (8, LANES), 0)
    lane = lax.broadcasted_iota(jnp.int32, (8, LANES), 1)
    offset = jnp.where(row < 2, 0, jnp.where(row < 4, 2, jnp.where((row == 4) | (row == 6), 1, -511)))
    ky_int = 4 * lane + offset
    ky_int = jnp.where((row == 1) | (row == 3) | (row >= 6), -ky_int, ky_int)
    ky_int = jnp.where((row == 1) & (lane == 0), -512, ky_int)
    ky = ky_int.astype(f32)
    kx = (me + 1).astype(f32)
    square = kx * kx + ky * ky

    def rows_of(k):
        return pl.ds(pl.multiple_of(k * 8, 8), 8)

    def factor(k, state):
        r, g = state
        low, up = zl[k], zu[k]
        inverse = 1.0 / (-(low + up) - square - low * r)
        m = low * inverse
        r = up * inverse
        g = -m * g
        inv_piv[rows_of(k), :] = inverse
        mult[rows_of(k), :] = m
        ratio[rows_of(k), :] = r
        beta[rows_of(k), :] = g
        return r, g

    zero = jnp.zeros((8, LANES), f32)
    one_v = jnp.ones((8, LANES), f32)
    lax.fori_loop(0, planes, factor, (zero, one_v))

    def unfold(i, state):
        b, g = state
        k = planes - 1 - i
        r = ratio[rows_of(k), :]
        b = beta[rows_of(k), :] - r * b
        g = -r * g
        beta[rows_of(k), :] = b
        gamma[rows_of(k), :] = g
        return b, g

    b0, g0 = lax.fori_loop(0, planes, unfold, (zero, one_v))
    last = slice((planes - 1) * 8, planes * 8)
    mat_all[mz, 0] = b0
    mat_all[mz, 1] = g0
    mat_all[mz, 2] = beta[last, :]
    mat_all[mz, 3] = gamma[last, :]
    z_send(mat_all, m_ssem, m_rsem)

    copy_ft.wait()
    first_lane = lax.broadcasted_iota(jnp.int32, (planes, LANES), 1) == 0

    def forward(f):
        quarters = []
        for q in range(4):
            block = recv_f[f, 4 * q:4 * q + 4].reshape(LANES, LANES).T
            quarters.append(jnp.concatenate([block[:64], block[64:]], axis=1))
        a = quarters[0] + quarters[2]
        b = quarters[0] - quarters[2]
        c = quarters[1] + quarters[3]
        e = quarters[1] - quarters[3]
        turned = jnp.concatenate([e[planes:], -e[:planes]], axis=0)
        spectra = []
        for first, z in ((0, a + c), (256, a - c)):
            both = product(z, ftab[0, :, first:first + 256], ftab[1, :, first:first + 256])
            rc, rs = both[:planes, :128], both[:planes, 128:]
            ic, is_ = both[planes:, :128], both[planes:, 128:]
            if first == 0:
                rs0, is0 = jnp.where(first_lane, 0.0, rs), jnp.where(first_lane, 0.0, is_)
                spectra.append((rc + is0, ic - rs0))
                spectra.append((jnp.where(first_lane, rs, rc - is_), jnp.where(first_lane, is_, ic + rs)))
            else:
                spectra.append((rc + is_, ic - rs))
                spectra.append((rc - is_, ic + rs))
        both = product(jnp.concatenate([b + turned, b - turned], axis=0), ftab[0, :, 512:], ftab[1, :, 512:])
        for half in range(2):
            cos, sin = both[:, half * 128:half * 128 + 128], both[:, 256 + half * 128:384 + half * 128]
            spectra.append((cos[:planes] + sin[planes:2 * planes], cos[planes:2 * planes] - sin[:planes]))
        for half in range(2):
            cos, sin = both[:, half * 128:half * 128 + 128], both[:, 256 + half * 128:384 + half * 128]
            spectra.append((cos[2 * planes:3 * planes] - sin[3 * planes:], cos[3 * planes:] + sin[2 * planes:3 * planes]))
        return spectra

    y_wait_recv(send_f, recv_f, f_ssem, f_rsem, 1)
    for s, (re, im) in enumerate(forward(1)):
        ky_row = ky[s:s + 1, :]
        vhat[s, 0] = -ky_row * im
        vhat[s, 1] = ky_row * re
    y_wait_recv(send_f, recv_f, f_ssem, f_rsem, 0)
    for s, (re, im) in enumerate(forward(0)):
        field_re[pl.ds(s, planes, stride=8), :] = re + vhat[s, 0]
        field_im[pl.ds(s, planes, stride=8), :] = im + vhat[s, 1]

    def down(k, state):
        sr, si = state
        inverse, m = inv_piv[rows_of(k), :], mult[rows_of(k), :]
        sr = field_re[rows_of(k), :] * inverse - m * sr
        si = field_im[rows_of(k), :] * inverse - m * si
        field_re[rows_of(k), :] = sr
        field_im[rows_of(k), :] = si
        return sr, si

    lax.fori_loop(0, planes, down, (zero, zero), unroll=True)

    def back(i, state):
        ar, ai = state
        k = planes - 1 - i
        r = ratio[rows_of(k), :]
        ar = field_re[rows_of(k), :] - r * ar
        ai = field_im[rows_of(k), :] - r * ai
        field_re[rows_of(k), :] = ar
        field_im[rows_of(k), :] = ai
        return ar, ai

    ar, ai = lax.fori_loop(0, planes, back, (zero, zero), unroll=True)
    rhs_all[mz, 0] = ar
    rhs_all[mz, 1] = ai
    rhs_all[mz, 2] = field_re[last, :]
    rhs_all[mz, 3] = field_im[last, :]
    z_send(rhs_all, r_ssem, r_rsem)

    z_wait_recv(mat_all, m_ssem, m_rsem)
    red_r[0] = zero
    red_e[0, 0] = zero
    red_e[0, 1] = zero

    def reduce_matrix(d, r):
        den = 1.0 / (1.0 - mat_all[d, 0] * r)
        psi = mat_all[d, 1] * den
        br = mat_all[d, 2] * r
        red_den[d] = den
        red_bden[d] = mat_all[d, 0] * den
        red_psi[d] = psi
        red_br[d] = br
        r = mat_all[d, 3] + br * psi
        red_r[d + 1] = r
        return r

    lax.fori_loop(0, gz, reduce_matrix, zero)
    z_wait_recv(rhs_all, r_ssem, r_rsem)

    def reduce_rhs(d, state):
        er, ei = state
        den, bden, br, b31 = red_den[d], red_bden[d], red_br[d], mat_all[d, 2]
        pr = den * rhs_all[d, 0] + bden * er
        pi = den * rhs_all[d, 1] + bden * ei
        er = rhs_all[d, 2] + b31 * er + br * pr
        ei = rhs_all[d, 3] + b31 * ei + br * pi
        red_phi[d, 0] = pr
        red_phi[d, 1] = pi
        red_e[d + 1, 0] = er
        red_e[d + 1, 1] = ei
        return er, ei

    lax.fori_loop(0, gz, reduce_rhs, (zero, zero), unroll=True)
    red_f[gz, 0] = zero
    red_f[gz, 1] = zero

    def reduce_back(i, state):
        fr, fi = state
        d = gz - 1 - i
        psi = red_psi[d]
        fr = red_phi[d, 0] + psi * fr
        fi = red_phi[d, 1] + psi * fi
        red_f[d, 0] = fr
        red_f[d, 1] = fi
        return fr, fi

    lax.fori_loop(0, gz, reduce_back, (zero, zero), unroll=True)
    before = [red_e[mz, part] + red_r[mz] * red_f[mz, part] for part in range(2)]
    after = [red_f[mz + 1, part] for part in range(2)]

    def finish(k, _):
        b, g = beta[rows_of(k), :], gamma[rows_of(k), :]
        field_re[rows_of(k), :] = field_re[rows_of(k), :] + b * before[0] + g * after[0]
        field_im[rows_of(k), :] = field_im[rows_of(k), :] + b * before[1] + g * after[1]
        return 0

    lax.fori_loop(0, planes, finish, 0, unroll=True)

    copy_it.wait()

    def inverse(f, spectra):
        parts = []
        for first in (0, 256):
            (pr, pi), (nr, ni) = spectra[first // 128], spectra[first // 128 + 1]
            cr, sr, ci, si = pr + nr, ni - pi, pi + ni, pr - nr
            if first == 0:
                cr, sr = jnp.where(first_lane, pr, cr), jnp.where(first_lane, nr, sr)
                ci, si = jnp.where(first_lane, pi, ci), jnp.where(first_lane, ni, si)
            z = jnp.concatenate([jnp.concatenate([cr, sr], axis=1), jnp.concatenate([ci, si], axis=1)], axis=0)
            parts.append(product(z, itab[0, first:first + 256, :], itab[1, first:first + 256, :]))
        (ar, ai), (br, bi), (cr, ci), (dr, di) = spectra[4:]
        z = jnp.concatenate([
            jnp.concatenate([ar, br, -ai, -bi], axis=1),
            jnp.concatenate([ai, bi, ar, br], axis=1),
            jnp.concatenate([cr, dr, ci, di], axis=1),
            jnp.concatenate([ci, di, -cr, -dr], axis=1)], axis=0)
        odd = product(z, itab[0, 512:, :], itab[1, 512:, :])
        g1, g3 = odd[:64], odd[64:]
        s02, d02 = parts[0] + parts[1], parts[0] - parts[1]
        s13, d13 = g1 + g3, g1 - g3
        turned = jnp.concatenate([-d13[planes:], d13[:planes]], axis=0)
        for q, value in enumerate((s02 + s13, d02 + turned, s02 - s13, d02 - turned)):
            block = jnp.concatenate([value[:, :128], value[:, 128:]], axis=0).T
            send_b[f, 4 * q:4 * q + 4] = block.reshape(4, 32, LANES)

    tiles = [(field_re[pl.ds(s, planes, stride=8), :], field_im[pl.ds(s, planes, stride=8), :]) for s in range(8)]
    inverse(0, tiles)
    y_send_first(send_b, recv_b, b_ssem, b_rsem, 0, [0])
    y_send_first(send_b, recv_b, b_ssem, b_rsem, 0, [1])
    y_send_first(send_b, recv_b, b_ssem, b_rsem, 0, [2])
    y_send_first(send_b, recv_b, b_ssem, b_rsem, 0, [3])
    y_send_first(send_b, recv_b, b_ssem, b_rsem, 0, [4])
    y_send_first(send_b, recv_b, b_ssem, b_rsem, 0, [5])
    y_send_first(send_b, recv_b, b_ssem, b_rsem, 0, [6])
    y_send_first(send_b, recv_b, b_ssem, b_rsem, 0, [7])
    y_send(send_b, recv_b, b_ssem, b_rsem, 0, [mate])
    recv_b[0, me] = send_b[0, me]
    inverse(1, [(-ky[s:s + 1, :] * im, ky[s:s + 1, :] * re) for s, (re, im) in enumerate(tiles)])
    y_send_first(send_b, recv_b, b_ssem, b_rsem, 1, [0])
    y_send_first(send_b, recv_b, b_ssem, b_rsem, 1, [1])
    y_send_first(send_b, recv_b, b_ssem, b_rsem, 1, [2])
    y_send_first(send_b, recv_b, b_ssem, b_rsem, 1, [3])
    y_send_first(send_b, recv_b, b_ssem, b_rsem, 1, [4])
    y_send_first(send_b, recv_b, b_ssem, b_rsem, 1, [5])
    y_send_first(send_b, recv_b, b_ssem, b_rsem, 1, [6])
    y_send_first(send_b, recv_b, b_ssem, b_rsem, 1, [7])
    y_send(send_b, recv_b, b_ssem, b_rsem, 1, [mate])
    recv_b[1, me] = send_b[1, me]

    def unstage(f, grad):
        for j in range(KX):
            rows_buf[pl.ds(j, 32, stride=16), :] = recv_b[f, j]
        for c in range(4):
            block = rows_buf[c * 128:(c + 1) * 128, :].T
            for h in range(2):
                for part in range(2):
                    first = h * 64 + part * 32
                    grad[part, :, h * 512 + c * 128:h * 512 + c * 128 + 128] = block[first:first + 32]

    for copy in halo_w:
        copy.wait_send()
    for f in range(2):
        y_wait_send(send_f, recv_f, f_ssem, f_rsem, f)
    z_wait_send(mat_all, m_ssem, m_rsem)
    z_wait_send(rhs_all, r_ssem, r_rsem)
    y_wait_recv(send_b, recv_b, b_ssem, b_rsem, 0)
    unstage(0, grad)
    for part in range(2):
        halo_send[1, 0, part:part + 1, :] = grad[part, planes - 1:planes, :]
        halo_send[1, 1, part:part + 1, :] = grad[part, 0:1, :]
    halo_p = halo_copies(1)
    halo_p[0].start()
    halo_p[1].start()
    out[0, 0] = vel[0, 0] + kx_lane * grad[1]
    out[0, 1] = vel[0, 1] - kx_lane * grad[0]
    y_wait_send(send_b, recv_b, b_ssem, b_rsem, 0)
    y_wait_recv(send_b, recv_b, b_ssem, b_rsem, 1)
    unstage(1, grad_q)
    for part in range(2):
        out[1, part] = vel[1, part] - grad_q[part]
    halo_p[0].wait_recv()
    halo_p[1].wait_recv()
    for part in range(2):
        out[2, part] = vel[2, part] - slope_diff(grad[part], 1, part, slope_wide)

    for copy in halo_p:
        copy.wait_send()
    y_wait_send(send_b, recv_b, b_ssem, b_rsem, 1)


def shards(velocity, z_lower, z_upper, z_slope):
    gy, gz = lax.axis_size("gy"), lax.axis_size("gz")
    planes = velocity.shape[2]
    ftab, itab = (jnp.asarray(table) for table in fourier_tables())
    f32 = jnp.float32
    hbm = pl.BlockSpec(memory_space=pl.ANY)
    lines = (planes * 8, LANES)
    dma = pltpu.SemaphoreType.DMA
    return pl.pallas_call(
        functools.partial(kernel, planes, gy, gz),
        out_shape=jax.ShapeDtypeStruct(velocity.shape, f32),
        in_specs=[pl.BlockSpec(memory_space=pltpu.HBM)] * 6,
        out_specs=pl.BlockSpec(memory_space=pltpu.VMEM),
        scratch_shapes=[
            pltpu.VMEM(velocity.shape, f32),
            pltpu.SMEM((planes,), f32),
            pltpu.SMEM((planes,), f32),
            pltpu.SMEM((planes,), f32),
            pltpu.VMEM(ftab.shape, jnp.bfloat16),
            pltpu.VMEM(itab.shape, jnp.bfloat16),
            pltpu.VMEM((512, LANES), f32),
            pltpu.VMEM((2, gy, 32, LANES), f32),
            pltpu.VMEM((2, gy, 32, LANES), f32),
            pltpu.VMEM((2, gy, 32, LANES), f32),
            pltpu.VMEM((2, gy, 32, LANES), f32),
            pltpu.VMEM((2, 2, 2, NY), f32),
            pltpu.VMEM((2, 2, 2, NY), f32),
            pltpu.VMEM((8, 2, planes, LANES), f32),
            pltpu.VMEM(lines, f32),
            pltpu.VMEM(lines, f32),
            pltpu.VMEM(lines, f32),
            pltpu.VMEM(lines, f32),
            pltpu.VMEM(lines, f32),
            pltpu.VMEM(lines, f32),
            pltpu.VMEM(lines, f32),
            pltpu.VMEM((gz, 4, 8, LANES), f32),
            pltpu.VMEM((gz, 4, 8, LANES), f32),
            pltpu.VMEM((gz, 8, LANES), f32),
            pltpu.VMEM((gz, 8, LANES), f32),
            pltpu.VMEM((gz, 8, LANES), f32),
            pltpu.VMEM((gz, 8, LANES), f32),
            pltpu.VMEM((gz, 8, LANES), f32),
            pltpu.VMEM((gz + 1, 8, LANES), f32),
            pltpu.VMEM((gz + 1, 2, 8, LANES), f32),
            pltpu.VMEM((gz, 2, 8, LANES), f32),
            pltpu.VMEM((gz + 1, 2, 8, LANES), f32),
            pltpu.VMEM((2, planes, NY), f32),
            pltpu.VMEM((2, planes, NY), f32),
            dma((8,)), dma((2, 2)), dma((2, 2)),
            dma((2, gy)), dma((2, gy)), dma((2, gy)), dma((2, gy)),
            dma((gz,)), dma((gz,)), dma((gz,)), dma((gz,)),
        ],
        compiler_params=pltpu.CompilerParams(
            collective_id=0, has_side_effects=True, vmem_limit_bytes=40 * 1024 * 1024
        ),
        name="project",
    )(*(pltpu.with_memory_space_constraint(a, pltpu.HBM) for a in (velocity, z_lower, z_upper, z_slope, ftab, itab)))


def solution(mesh):
    placed = (P(None, None, "gz", "gy"), P("gz"), P("gz"), P("gz"))
    return jax.shard_map(
        shards, mesh=mesh, in_specs=placed, out_specs=P(None, None, "gz", "gy"), check_vma=False
    )
```

```python
import functools

import jax
import jax.numpy as jnp
import ml_dtypes
import numpy as np
from jax import lax
from jax.experimental import pallas as pl
from jax.experimental.pallas import tpu as pltpu
from jax.sharding import PartitionSpec as P

NY = 1024
KX = 16
LANES = 128
MESH = pl.DeviceIdType.MESH
Y_ORDER = (4, 3, -3, 2, -2, 1, -1)
Z_ORDER = sorted(
    ((dx, dy) for dx in (2, 1, -1, 0) for dy in (2, 1, -1, 0) if (dx, dy) != (0, 0)),
    key=lambda pair: -abs(pair[0]) - abs(pair[1]),
)


def fourier_tables():
    place = np.arange(256)
    y = 64 * ((place % 128) // 32) + 32 * (place // 128) + place % 32

    def pair(m):
        phase = 2.0 * np.pi * ((y[:, None] * m[None, :]) % NY) / NY
        return np.cos(phase), np.sin(phase)

    c0, s0 = pair(4 * np.arange(128))
    s0[:, 0] = (-1.0) ** y
    c2, s2 = pair(4 * np.arange(128) + 2)
    c1, s1 = pair(4 * np.arange(256) + 1)
    table = np.concatenate([c0, s0, c2, s2, c1, s1], axis=1)

    def split(values):
        high = values.astype(ml_dtypes.bfloat16)
        low = (values - high.astype(np.float64)).astype(ml_dtypes.bfloat16)
        return np.stack([high, low])

    t, u = np.arange(128), np.arange(256)
    half = 4 * t
    half[0] = NY // 2
    m = np.concatenate([4 * t, -half, 4 * t + 2, -4 * t - 2, 4 * u + 1, -4 * u - 1]) % NY

    def both(y):
        phase = 2.0 * np.pi * ((y[:, None] * m[None, :]) % NY) / NY
        return np.cos(phase), np.sin(phase)

    r = np.arange(32)
    edge = np.concatenate(both(64 * (r // 2) + r % 2), axis=1)
    turn = np.stack(both(8 * (r % 8) + 2 * (r // 8))).astype(np.float32)
    return split(table), split(table.T / NY), split(edge), turn


def dot(a, b):
    return jnp.dot(a, b, preferred_element_type=jnp.float32)


def product(values, high, low):
    top = values.astype(jnp.bfloat16)
    rest = (values - top.astype(jnp.float32)).astype(jnp.bfloat16)
    rows = values.shape[0]
    both = dot(jnp.concatenate([top, rest], axis=0), high)
    return both[:rows] + both[rows:] + dot(top, low)


def kernel(
    planes, gy, gz,
    vel_hbm, zl_hbm, zu_hbm, zs_hbm, ftab_hbm, itab_hbm, etab_hbm, turn_hbm, out,
    vel, zl, zu, zs, ftab, itab, etab, turn, edge_buf, edge_rows, edge_send, edge_recv, edge_sum, edge, rows_buf, send_f, recv_f, send_b, recv_b,
    halo_send, halo_recv, vhat, field_re, field_im,
    inv_piv, mult, ratio, beta, gamma,
    mat_all, rhs_all, red_den, red_bden, red_psi, red_b31, red_br, red_r, red_e, red_phi, red_f,
    grad, grad_q,
    in_sem, e_ssem, e_rsem, halo_ssem, halo_rsem, f_ssem, f_rsem, b_ssem, b_rsem, m_ssem, m_rsem, r_ssem, r_rsem,
):
    me = lax.axis_index("gy")
    mz = lax.axis_index("gz")
    f32 = jnp.float32

    copy_in = [pltpu.make_async_copy(vel_hbm.at[c], vel.at[c], in_sem.at[c]) for c in range(3)]
    copy_z = [
        pltpu.make_async_copy(src, dst, in_sem.at[3 + i])
        for i, (src, dst) in enumerate(((zl_hbm, zl), (zu_hbm, zu), (zs_hbm, zs)))
    ]
    copy_ft = pltpu.make_async_copy(ftab_hbm, ftab, in_sem.at[6])
    copy_it = pltpu.make_async_copy(itab_hbm, itab, in_sem.at[7])
    copy_et = pltpu.make_async_copy(etab_hbm, etab, in_sem.at[8])
    copy_tt = pltpu.make_async_copy(turn_hbm, turn, in_sem.at[9])
    copy_in[1].start()
    copy_in[2].start()
    barrier = pltpu.get_barrier_semaphore()

    chips, chip, core = gy // 2, me // 2, lax.rem(me, 2)
    mate = me + 1 - 2 * core

    def y_partner(dz, c):
        return lax.rem(chip + dz + chips, chips) * 2 + c

    def z_partner(o, sign):
        dx, dy = Z_ORDER[o]
        return lax.rem(mz // 4 + sign * dx + 4, 4) * 4 + lax.rem(mz + sign * dy + 4, 4)

    z_all = range(len(Z_ORDER))
    y_all = [y_partner(dz, c) for dz in Y_ORDER for c in range(2)] + [mate]
    for g in y_all:
        pl.semaphore_signal(barrier, inc=1, device_id={"gy": g}, device_id_type=MESH)
    for o in z_all:
        pl.semaphore_signal(barrier, inc=1, device_id={"gz": z_partner(o, 1)}, device_id_type=MESH)
    for copy in (copy_z[2], copy_in[0], copy_z[0], copy_z[1], copy_et, copy_tt, copy_ft, copy_it):
        copy.start()

    def stage(f, re, im):
        for c in range(4):
            a = slice(c * 128, c * 128 + 128)
            b = slice(512 + c * 128, 512 + c * 128 + 128)
            block = jnp.concatenate([re[:, a], im[:, a], re[:, b], im[:, b]], axis=0)
            rows_buf[c * 128:(c + 1) * 128, :] = block.T
        for j in range(KX):
            send_f[f, j] = rows_buf[pl.ds(j, 32, stride=16), :]

    def y_copy(src, dst, ssem, rsem, f, g):
        return pltpu.make_async_remote_copy(
            src_ref=src.at[f, g], dst_ref=dst.at[f, me],
            send_sem=ssem.at[f, g], recv_sem=rsem.at[f, me],
            device_id={"gy": g}, device_id_type=MESH)

    def y_send(src, dst, ssem, rsem, f, partners):
        for g in partners:
            y_copy(src, dst, ssem, rsem, f, g).start()

    def y_send_first(src, dst, ssem, rsem, f, first):
        for t in first:
            @pl.when(chip != t)
            def _():
                y_send(src, dst, ssem, rsem, f, [2 * t, 2 * t + 1])
        for dz in Y_ORDER:
            g = y_partner(dz, 0)
            other = g >= 0
            for t in first:
                other = other & (g != 2 * t)

            @pl.when(other)
            def _():
                y_send(src, dst, ssem, rsem, f, [g, g + 1])

    def y_wait_recv(src, dst, ssem, rsem, f):
        for g in y_all:
            pltpu.make_async_remote_copy(
                src_ref=src.at[f, g], dst_ref=dst.at[f, g],
                send_sem=ssem.at[f, g], recv_sem=rsem.at[f, g],
                device_id={"gy": g}, device_id_type=MESH).wait_recv()

    def y_wait_send(src, dst, ssem, rsem, f):
        for g in y_all:
            y_copy(src, dst, ssem, rsem, f, g).wait_send()

    def z_copy(buf, ssem, rsem, o, slot):
        return pltpu.make_async_remote_copy(
            src_ref=buf.at[slot], dst_ref=buf.at[slot],
            send_sem=ssem.at[o], recv_sem=rsem.at[o],
            device_id={"gz": z_partner(o, 1)}, device_id_type=MESH)

    def z_send(buf, ssem, rsem):
        for o in z_all:
            z_copy(buf, ssem, rsem, o, mz).start()

    def z_wait_recv(buf, ssem, rsem):
        for o in z_all:
            z_copy(buf, ssem, rsem, o, z_partner(o, -1)).wait_recv()

    def z_wait_send(buf, ssem, rsem):
        for o in z_all:
            z_copy(buf, ssem, rsem, o, mz).wait_send()

    def edge_copy(g):
        return pltpu.make_async_remote_copy(
            src_ref=edge_send.at[g], dst_ref=edge_recv.at[me],
            send_sem=e_ssem.at[g], recv_sem=e_rsem.at[me],
            device_id={"gy": g}, device_id_type=MESH)

    def halo_copies():
        up = pltpu.make_async_remote_copy(
            src_ref=halo_send.at[0], dst_ref=halo_recv.at[0],
            send_sem=halo_ssem.at[0], recv_sem=halo_rsem.at[0],
            device_id={"gz": lax.rem(mz + 1, gz)}, device_id_type=MESH)
        down = pltpu.make_async_remote_copy(
            src_ref=halo_send.at[1], dst_ref=halo_recv.at[1],
            send_sem=halo_ssem.at[1], recv_sem=halo_rsem.at[1],
            device_id={"gz": lax.rem(mz + gz - 1, gz)}, device_id_type=MESH)
        return up, down

    plane_id = lax.broadcasted_iota(jnp.int32, (planes, LANES), 0)

    def column(ref):
        def one(k, col):
            return jnp.where(plane_id == k, ref[k], col)

        return lax.fori_loop(0, planes, one, jnp.zeros((planes, LANES), f32))

    kx_lane = (lax.broadcasted_iota(jnp.int32, (1, NY), 1) % KX + 1).astype(f32)

    def slope_diff(values, low, high):
        above = jnp.concatenate([values[1:], high], axis=0)
        below = jnp.concatenate([low, values[:-1]], axis=0)
        return slope_wide * (above - below)

    copy_z[2].wait()
    slope = column(zs)
    slope_wide = jnp.concatenate([slope] * 8, axis=1)
    nothing = jnp.zeros((1, NY), f32)
    copy_in[1].wait()
    stage(1, vel[1, 0], vel[1, 1])
    copy_in[2].wait()
    for t in range(8):
        for part in range(2):
            for e, k in enumerate((0, planes - 1)):
                r = 4 * t + 2 * part + e
                edge_rows[r:r + 1, :] = vel[2, part, k:k + 1, t * 128:t * 128 + 128]
    edge_buf[...] = jnp.zeros((LANES, LANES), f32)
    for q in range(4):
        edge_buf[q * 32:q * 32 + 32, :32] = edge_rows[:, q * 32:q * 32 + 32]
    edge_rows[...] = edge_buf[...].T[:32]
    for j in range(KX):
        edge_send[j] = edge_rows[pl.ds(j, 2, stride=16), :]
    copy_in[0].wait()
    stage(
        0,
        slope_diff(vel[2, 0], nothing, nothing) - kx_lane * vel[0, 1],
        slope_diff(vel[2, 1], nothing, nothing) + kx_lane * vel[0, 0],
    )
    pl.semaphore_wait(barrier, len(y_all) + len(Z_ORDER))
    to_core = [[y_partner(dz, c) for dz in Y_ORDER] for c in range(2)]
    for partners in (to_core[0] + [mate], to_core[1]):
        for g in partners:
            edge_copy(g).start()
        y_send(send_f, recv_f, f_ssem, f_rsem, 1, partners)
        y_send(send_f, recv_f, f_ssem, f_rsem, 0, partners)
    for f in range(2):
        recv_f[f, me] = send_f[f, me]
    edge_recv[me] = edge_send[me]

    copy_z[0].wait()
    copy_z[1].wait()
    row = lax.broadcasted_iota(jnp.int32, (8, LANES), 0)
    lane = lax.broadcasted_iota(jnp.int32, (8, LANES), 1)
    offset = jnp.where(row < 2, 0, jnp.where(row < 4, 2, jnp.where((row == 4) | (row == 6), 1, -511)))
    ky_int = 4 * lane + offset
    ky_int = jnp.where((row == 1) | (row == 3) | (row >= 6), -ky_int, ky_int)
    ky_int = jnp.where((row == 1) & (lane == 0), -512, ky_int)
    ky = ky_int.astype(f32)
    kx = (me + 1).astype(f32)
    square = kx * kx + ky * ky

    def rows_of(k):
        return pl.ds(pl.multiple_of(k * 8, 8), 8)

    def factor(k, state):
        r, g = state
        low, up = zl[k], zu[k]
        inverse = 1.0 / (-(low + up) - square - low * r)
        m = low * inverse
        r = up * inverse
        g = -m * g
        inv_piv[rows_of(k), :] = inverse
        mult[rows_of(k), :] = m
        ratio[rows_of(k), :] = r
        beta[rows_of(k), :] = g
        return r, g

    zero = jnp.zeros((8, LANES), f32)
    one_v = jnp.ones((8, LANES), f32)
    lax.fori_loop(0, planes, factor, (zero, one_v))

    def unfold(i, state):
        b, g = state
        k = planes - 1 - i
        r = ratio[rows_of(k), :]
        b = beta[rows_of(k), :] - r * b
        g = -r * g
        beta[rows_of(k), :] = b
        gamma[rows_of(k), :] = g
        return b, g

    b0, g0 = lax.fori_loop(0, planes, unfold, (zero, one_v))
    last = slice((planes - 1) * 8, planes * 8)
    mat_all[mz, 0] = b0
    mat_all[mz, 1] = g0
    mat_all[mz, 2] = beta[last, :]
    mat_all[mz, 3] = gamma[last, :]
    z_send(mat_all, m_ssem, m_rsem)

    copy_ft.wait()
    first_lane = lax.broadcasted_iota(jnp.int32, (planes, LANES), 1) == 0

    def forward(f):
        quarters = []
        for q in range(4):
            block = recv_f[f, 4 * q:4 * q + 4].reshape(LANES, LANES).T
            quarters.append(jnp.concatenate([block[:64], block[64:]], axis=1))
        a = quarters[0] + quarters[2]
        b = quarters[0] - quarters[2]
        c = quarters[1] + quarters[3]
        e = quarters[1] - quarters[3]
        turned = jnp.concatenate([e[planes:], -e[:planes]], axis=0)
        spectra = []
        for first, z in ((0, a + c), (256, a - c)):
            both = product(z, ftab[0, :, first:first + 256], ftab[1, :, first:first + 256])
            rc, rs = both[:planes, :128], both[:planes, 128:]
            ic, is_ = both[planes:, :128], both[planes:, 128:]
            if first == 0:
                rs0, is0 = jnp.where(first_lane, 0.0, rs), jnp.where(first_lane, 0.0, is_)
                spectra.append((rc + is0, ic - rs0))
                spectra.append((jnp.where(first_lane, rs, rc - is_), jnp.where(first_lane, is_, ic + rs)))
            else:
                spectra.append((rc + is_, ic - rs))
                spectra.append((rc - is_, ic + rs))
        both = product(jnp.concatenate([b + turned, b - turned], axis=0), ftab[0, :, 512:], ftab[1, :, 512:])
        for half in range(2):
            cos, sin = both[:, half * 128:half * 128 + 128], both[:, 256 + half * 128:384 + half * 128]
            spectra.append((cos[:planes] + sin[planes:2 * planes], cos[planes:2 * planes] - sin[:planes]))
        for half in range(2):
            cos, sin = both[:, half * 128:half * 128 + 128], both[:, 256 + half * 128:384 + half * 128]
            spectra.append((cos[2 * planes:3 * planes] - sin[3 * planes:], cos[3 * planes:] + sin[2 * planes:3 * planes]))
        return spectra

    y_wait_recv(send_f, recv_f, f_ssem, f_rsem, 1)
    for s, (re, im) in enumerate(forward(1)):
        ky_row = ky[s:s + 1, :]
        vhat[s, 0] = -ky_row * im
        vhat[s, 1] = ky_row * re
    copy_et.wait()
    copy_tt.wait()
    for g in y_all:
        pltpu.make_async_remote_copy(
            src_ref=edge_send.at[g], dst_ref=edge_recv.at[g],
            send_sem=e_ssem.at[g], recv_sem=e_rsem.at[g],
            device_id={"gy": g}, device_id_type=MESH).wait_recv()
    for d in range(gy):
        edge_buf[2 * d:2 * d + 2, :] = edge_recv[d]
    partial = product(edge_buf[...].T[:, :32], etab[0], etab[1])
    for s in range(16):
        edge_sum[s] = partial[:, s * 128:s * 128 + 128]
    for s in range(8):
        cos, sin = turn[0, :, s * 128:s * 128 + 128], turn[1, :, s * 128:s * 128 + 128]
        for e in range(2):
            rc, rs, ic, is_ = (
                edge_sum[s + off, pl.ds(part + e, 32, stride=4), :] for part in (0, 2) for off in (0, 8))
            re, im = rc + is_, ic - rs
            edge[e, 0, s:s + 1, :] = jnp.sum(re * cos + im * sin, axis=0, keepdims=True)
            edge[e, 1, s:s + 1, :] = jnp.sum(im * cos - re * sin, axis=0, keepdims=True)
    below = jnp.full((8, LANES), zs[0]) / jnp.full((8, LANES), zl[0])
    above = jnp.full((8, LANES), zs[planes - 1]) / jnp.full((8, LANES), zu[planes - 1])
    y_wait_recv(send_f, recv_f, f_ssem, f_rsem, 0)
    for s, (re, im) in enumerate(forward(0)):
        field_re[pl.ds(s, planes, stride=8), :] = re + vhat[s, 0]
        field_im[pl.ds(s, planes, stride=8), :] = im + vhat[s, 1]

    def down(k, state):
        sr, si = state
        inverse, m = inv_piv[rows_of(k), :], mult[rows_of(k), :]
        sr = field_re[rows_of(k), :] * inverse - m * sr
        si = field_im[rows_of(k), :] * inverse - m * si
        field_re[rows_of(k), :] = sr
        field_im[rows_of(k), :] = si
        return sr, si

    lax.fori_loop(0, planes, down, (zero, zero), unroll=True)

    def back(i, state):
        ar, ai = state
        k = planes - 1 - i
        r = ratio[rows_of(k), :]
        ar = field_re[rows_of(k), :] - r * ar
        ai = field_im[rows_of(k), :] - r * ai
        field_re[rows_of(k), :] = ar
        field_im[rows_of(k), :] = ai
        return ar, ai

    ar, ai = lax.fori_loop(0, planes, back, (zero, zero), unroll=True)
    rhs_all[mz, 0] = ar - below * edge[0, 0]
    rhs_all[mz, 1] = ai - below * edge[0, 1]
    rhs_all[mz, 2] = field_re[last, :] + above * edge[1, 0]
    rhs_all[mz, 3] = field_im[last, :] + above * edge[1, 1]
    z_send(rhs_all, r_ssem, r_rsem)

    z_wait_recv(mat_all, m_ssem, m_rsem)
    red_r[0] = zero
    red_e[0, 0] = zero
    red_e[0, 1] = zero

    def reduce_matrix(d, r):
        den = 1.0 / (1.0 - mat_all[d, 0] * r)
        psi = mat_all[d, 1] * den
        br = mat_all[d, 2] * r
        red_den[d] = den
        red_bden[d] = mat_all[d, 0] * den
        red_psi[d] = psi
        red_br[d] = br
        r = mat_all[d, 3] + br * psi
        red_r[d + 1] = r
        return r

    lax.fori_loop(0, gz, reduce_matrix, zero)
    z_wait_recv(rhs_all, r_ssem, r_rsem)

    def reduce_rhs(d, state):
        er, ei = state
        den, bden, br, b31 = red_den[d], red_bden[d], red_br[d], mat_all[d, 2]
        pr = den * rhs_all[d, 0] + bden * er
        pi = den * rhs_all[d, 1] + bden * ei
        er = rhs_all[d, 2] + b31 * er + br * pr
        ei = rhs_all[d, 3] + b31 * ei + br * pi
        red_phi[d, 0] = pr
        red_phi[d, 1] = pi
        red_e[d + 1, 0] = er
        red_e[d + 1, 1] = ei
        return er, ei

    lax.fori_loop(0, gz, reduce_rhs, (zero, zero), unroll=True)
    red_f[gz, 0] = zero
    red_f[gz, 1] = zero

    def reduce_back(i, state):
        fr, fi = state
        d = gz - 1 - i
        psi = red_psi[d]
        fr = red_phi[d, 0] + psi * fr
        fi = red_phi[d, 1] + psi * fi
        red_f[d, 0] = fr
        red_f[d, 1] = fi
        return fr, fi

    lax.fori_loop(0, gz, reduce_back, (zero, zero), unroll=True)
    before = [red_e[mz, part] + red_r[mz] * red_f[mz, part] for part in range(2)]
    after = [red_f[mz + 1, part] for part in range(2)]

    def finish(k, _):
        b, g = beta[rows_of(k), :], gamma[rows_of(k), :]
        field_re[rows_of(k), :] = field_re[rows_of(k), :] + b * before[0] + g * after[0]
        field_im[rows_of(k), :] = field_im[rows_of(k), :] + b * before[1] + g * after[1]
        return 0

    lax.fori_loop(0, planes, finish, 0, unroll=True)

    copy_it.wait()

    def inverse(f, spectra):
        parts = []
        for first in (0, 256):
            (pr, pi), (nr, ni) = spectra[first // 128], spectra[first // 128 + 1]
            cr, sr, ci, si = pr + nr, ni - pi, pi + ni, pr - nr
            if first == 0:
                cr, sr = jnp.where(first_lane, pr, cr), jnp.where(first_lane, nr, sr)
                ci, si = jnp.where(first_lane, pi, ci), jnp.where(first_lane, ni, si)
            z = jnp.concatenate([jnp.concatenate([cr, sr], axis=1), jnp.concatenate([ci, si], axis=1)], axis=0)
            parts.append(product(z, itab[0, first:first + 256, :], itab[1, first:first + 256, :]))
        (ar, ai), (br, bi), (cr, ci), (dr, di) = spectra[4:]
        z = jnp.concatenate([
            jnp.concatenate([ar, br, -ai, -bi], axis=1),
            jnp.concatenate([ai, bi, ar, br], axis=1),
            jnp.concatenate([cr, dr, ci, di], axis=1),
            jnp.concatenate([ci, di, -cr, -dr], axis=1)], axis=0)
        odd = product(z, itab[0, 512:, :], itab[1, 512:, :])
        g1, g3 = odd[:64], odd[64:]
        s02, d02 = parts[0] + parts[1], parts[0] - parts[1]
        s13, d13 = g1 + g3, g1 - g3
        turned = jnp.concatenate([-d13[planes:], d13[:planes]], axis=0)
        for q, value in enumerate((s02 + s13, d02 + turned, s02 - s13, d02 - turned)):
            block = jnp.concatenate([value[:, :128], value[:, 128:]], axis=0).T
            send_b[f, 4 * q:4 * q + 4] = block.reshape(4, 32, LANES)

    tiles = [(field_re[pl.ds(s, planes, stride=8), :], field_im[pl.ds(s, planes, stride=8), :]) for s in range(8)]
    inverse(0, tiles)
    y_send_first(send_b, recv_b, b_ssem, b_rsem, 0, (0, 1, 2))
    y_send(send_b, recv_b, b_ssem, b_rsem, 0, [mate])
    recv_b[0, me] = send_b[0, me]
    inverse(1, [(-ky[s:s + 1, :] * im, ky[s:s + 1, :] * re) for s, (re, im) in enumerate(tiles)])
    y_send_first(send_b, recv_b, b_ssem, b_rsem, 1, (0, 1, 2))
    y_send(send_b, recv_b, b_ssem, b_rsem, 1, [mate])
    recv_b[1, me] = send_b[1, me]

    def unstage(f, grad):
        for j in range(KX):
            rows_buf[pl.ds(j, 32, stride=16), :] = recv_b[f, j]
        for c in range(4):
            block = rows_buf[c * 128:(c + 1) * 128, :].T
            for h in range(2):
                for part in range(2):
                    first = h * 64 + part * 32
                    grad[part, :, h * 512 + c * 128:h * 512 + c * 128 + 128] = block[first:first + 32]

    for g in y_all:
        edge_copy(g).wait_send()
    for f in range(2):
        y_wait_send(send_f, recv_f, f_ssem, f_rsem, f)
    z_wait_send(mat_all, m_ssem, m_rsem)
    z_wait_send(rhs_all, r_ssem, r_rsem)
    y_wait_recv(send_b, recv_b, b_ssem, b_rsem, 0)
    unstage(0, grad)
    for part in range(2):
        halo_send[0, part:part + 1, :] = grad[part, planes - 1:planes, :]
        halo_send[1, part:part + 1, :] = grad[part, 0:1, :]
    halo_p = halo_copies()
    halo_p[0].start()
    halo_p[1].start()
    out[0, 0] = vel[0, 0] + kx_lane * grad[1]
    out[0, 1] = vel[0, 1] - kx_lane * grad[0]
    y_wait_send(send_b, recv_b, b_ssem, b_rsem, 0)
    y_wait_recv(send_b, recv_b, b_ssem, b_rsem, 1)
    unstage(1, grad_q)
    for part in range(2):
        out[1, part] = vel[1, part] - grad_q[part]
    halo_p[0].wait_recv()
    halo_p[1].wait_recv()
    for part in range(2):
        low = jnp.where(mz > 0, halo_recv[0, part:part + 1, :], 0.0)
        high = jnp.where(mz < gz - 1, halo_recv[1, part:part + 1, :], 0.0)
        out[2, part] = vel[2, part] - slope_diff(grad[part], low, high)

    for copy in halo_p:
        copy.wait_send()
    y_wait_send(send_b, recv_b, b_ssem, b_rsem, 1)


def shards(velocity, z_lower, z_upper, z_slope):
    gy, gz = lax.axis_size("gy"), lax.axis_size("gz")
    planes = velocity.shape[2]
    ftab, itab, etab, turn = (jnp.asarray(table) for table in fourier_tables())
    f32 = jnp.float32
    hbm = pl.BlockSpec(memory_space=pl.ANY)
    lines = (planes * 8, LANES)
    dma = pltpu.SemaphoreType.DMA
    return pl.pallas_call(
        functools.partial(kernel, planes, gy, gz),
        out_shape=jax.ShapeDtypeStruct(velocity.shape, f32),
        in_specs=[pl.BlockSpec(memory_space=pltpu.HBM)] * 8,
        out_specs=pl.BlockSpec(memory_space=pltpu.VMEM),
        scratch_shapes=[
            pltpu.VMEM(velocity.shape, f32),
            pltpu.SMEM((planes,), f32),
            pltpu.SMEM((planes,), f32),
            pltpu.SMEM((planes,), f32),
            pltpu.VMEM(ftab.shape, jnp.bfloat16),
            pltpu.VMEM(itab.shape, jnp.bfloat16),
            pltpu.VMEM(etab.shape, jnp.bfloat16),
            pltpu.VMEM(turn.shape, f32),
            pltpu.VMEM((LANES, LANES), f32),
            pltpu.VMEM((32, LANES), f32),
            pltpu.VMEM((gy, 2, LANES), f32),
            pltpu.VMEM((gy, 2, LANES), f32),
            pltpu.VMEM((16, LANES, LANES), f32),
            pltpu.VMEM((2, 2, 8, LANES), f32),
            pltpu.VMEM((512, LANES), f32),
            pltpu.VMEM((2, gy, 32, LANES), f32),
            pltpu.VMEM((2, gy, 32, LANES), f32),
            pltpu.VMEM((2, gy, 32, LANES), f32),
            pltpu.VMEM((2, gy, 32, LANES), f32),
            pltpu.VMEM((2, 2, NY), f32),
            pltpu.VMEM((2, 2, NY), f32),
            pltpu.VMEM((8, 2, planes, LANES), f32),
            pltpu.VMEM(lines, f32),
            pltpu.VMEM(lines, f32),
            pltpu.VMEM(lines, f32),
            pltpu.VMEM(lines, f32),
            pltpu.VMEM(lines, f32),
            pltpu.VMEM(lines, f32),
            pltpu.VMEM(lines, f32),
            pltpu.VMEM((gz, 4, 8, LANES), f32),
            pltpu.VMEM((gz, 4, 8, LANES), f32),
            pltpu.VMEM((gz, 8, LANES), f32),
            pltpu.VMEM((gz, 8, LANES), f32),
            pltpu.VMEM((gz, 8, LANES), f32),
            pltpu.VMEM((gz, 8, LANES), f32),
            pltpu.VMEM((gz, 8, LANES), f32),
            pltpu.VMEM((gz + 1, 8, LANES), f32),
            pltpu.VMEM((gz + 1, 2, 8, LANES), f32),
            pltpu.VMEM((gz, 2, 8, LANES), f32),
            pltpu.VMEM((gz + 1, 2, 8, LANES), f32),
            pltpu.VMEM((2, planes, NY), f32),
            pltpu.VMEM((2, planes, NY), f32),
            dma((10,)), dma((gy,)), dma((gy,)), dma((2,)), dma((2,)),
            dma((2, gy)), dma((2, gy)), dma((2, gy)), dma((2, gy)),
            dma((gz,)), dma((gz,)), dma((gz,)), dma((gz,)),
        ],
        compiler_params=pltpu.CompilerParams(
            collective_id=0, has_side_effects=True, vmem_limit_bytes=40 * 1024 * 1024
        ),
        name="project",
    )(*(pltpu.with_memory_space_constraint(a, pltpu.HBM) for a in (velocity, z_lower, z_upper, z_slope, ftab, itab, etab, turn)))


def solution(mesh):
    placed = (P(None, None, "gz", "gy"), P("gz"), P("gz"), P("gz"))
    return jax.shard_map(
        shards, mesh=mesh, in_specs=placed, out_specs=P(None, None, "gz", "gy"), check_vma=False
    )
```

```python
import functools

import jax
import jax.numpy as jnp
import ml_dtypes
import numpy as np
from jax import lax
from jax.experimental import pallas as pl
from jax.experimental.pallas import tpu as pltpu
from jax.sharding import PartitionSpec as P

NY = 1024
KX = 16
LANES = 128
MESH = pl.DeviceIdType.MESH
Y_ORDER = (4, 3, -3, 2, -2, 1, -1)
Z_ORDER = sorted(
    ((dx, dy) for dx in (2, 1, -1, 0) for dy in (2, 1, -1, 0) if (dx, dy) != (0, 0)),
    key=lambda pair: -abs(pair[0]) - abs(pair[1]),
)


def fourier_tables():
    place = np.arange(256)
    y = 64 * ((place % 128) // 32) + 32 * (place // 128) + place % 32

    def pair(m):
        phase = 2.0 * np.pi * ((y[:, None] * m[None, :]) % NY) / NY
        return np.cos(phase), np.sin(phase)

    c0, s0 = pair(4 * np.arange(128))
    s0[:, 0] = (-1.0) ** y
    c2, s2 = pair(4 * np.arange(128) + 2)
    c1, s1 = pair(4 * np.arange(256) + 1)
    table = np.concatenate([c0, s0, c2, s2, c1, s1], axis=1)

    def split(values):
        high = values.astype(ml_dtypes.bfloat16)
        low = (values - high.astype(np.float64)).astype(ml_dtypes.bfloat16)
        return np.stack([high, low])

    t, u = np.arange(128), np.arange(256)
    half = 4 * t
    half[0] = NY // 2
    m = np.concatenate([4 * t, -half, 4 * t + 2, -4 * t - 2, 4 * u + 1, -4 * u - 1]) % NY

    def both(y):
        phase = 2.0 * np.pi * ((y[:, None] * m[None, :]) % NY) / NY
        return np.cos(phase), np.sin(phase)

    r = np.arange(32)
    edge = np.concatenate(both(64 * (r // 2) + r % 2), axis=1)
    turn = np.stack(both(8 * (r % 8) + 2 * (r // 8))).astype(np.float32)
    return split(table), split(table.T / NY), split(edge), turn


def dot(a, b):
    return jnp.dot(a, b, preferred_element_type=jnp.float32)


def product(values, high, low):
    top = values.astype(jnp.bfloat16)
    rest = (values - top.astype(jnp.float32)).astype(jnp.bfloat16)
    rows = values.shape[0]
    both = dot(jnp.concatenate([top, rest], axis=0), high)
    return both[:rows] + both[rows:] + dot(top, low)


def kernel(
    planes, gy, gz,
    vel_hbm, zl_hbm, zu_hbm, zs_hbm, ftab_hbm, itab_hbm, etab_hbm, turn_hbm, out,
    vel, zl, zu, zs, ftab, itab, etab, turn, edge_buf, edge_rows, edge_send, edge_recv, edge_sum, edge, rows_buf, send_f, recv_f, send_b, recv_b,
    halo_send, halo_recv, vhat, field_re, field_im,
    inv_piv, mult, ratio, beta, gamma, low_row, high_row,
    mat_all, rhs_all, red_den, red_bden, red_psi, red_b31, red_br, red_r, red_e, red_phi, red_f,
    grad, grad_q,
    in_sem, e_ssem, e_rsem, halo_ssem, halo_rsem, f_ssem, f_rsem, b_ssem, b_rsem, m_ssem, m_rsem, r_ssem, r_rsem,
):
    me = lax.axis_index("gy")
    mz = lax.axis_index("gz")
    f32 = jnp.float32

    copy_in = [pltpu.make_async_copy(vel_hbm.at[c], vel.at[c], in_sem.at[c]) for c in range(3)]
    copy_z = [
        pltpu.make_async_copy(src, dst, in_sem.at[3 + i])
        for i, (src, dst) in enumerate(((zl_hbm, zl), (zu_hbm, zu), (zs_hbm, zs)))
    ]
    copy_ft = pltpu.make_async_copy(ftab_hbm, ftab, in_sem.at[6])
    copy_it = pltpu.make_async_copy(itab_hbm, itab, in_sem.at[7])
    copy_et = pltpu.make_async_copy(etab_hbm, etab, in_sem.at[8])
    copy_tt = pltpu.make_async_copy(turn_hbm, turn, in_sem.at[9])
    copy_in[1].start()
    copy_in[2].start()
    barrier = pltpu.get_barrier_semaphore()

    chips, chip, core = gy // 2, me // 2, lax.rem(me, 2)
    mate = me + 1 - 2 * core

    def y_partner(dz, c):
        return lax.rem(chip + dz + chips, chips) * 2 + c

    def z_partner(o, sign):
        dx, dy = Z_ORDER[o]
        return lax.rem(mz // 4 + sign * dx + 4, 4) * 4 + lax.rem(mz + sign * dy + 4, 4)

    z_all = range(len(Z_ORDER))
    y_all = [y_partner(dz, c) for dz in Y_ORDER for c in range(2)] + [mate]
    for g in y_all:
        pl.semaphore_signal(barrier, inc=1, device_id={"gy": g}, device_id_type=MESH)
    for o in z_all:
        pl.semaphore_signal(barrier, inc=1, device_id={"gz": z_partner(o, 1)}, device_id_type=MESH)
    for copy in (copy_z[2], copy_in[0], copy_z[0], copy_z[1], copy_et, copy_tt, copy_ft, copy_it):
        copy.start()

    def stage(f, re, im):
        for c in range(4):
            a = slice(c * 128, c * 128 + 128)
            b = slice(512 + c * 128, 512 + c * 128 + 128)
            block = jnp.concatenate([re[:, a], im[:, a], re[:, b], im[:, b]], axis=0)
            rows_buf[c * 128:(c + 1) * 128, :] = block.T
        for j in range(KX):
            send_f[f, j] = rows_buf[pl.ds(j, 32, stride=16), :]

    def y_copy(src, dst, ssem, rsem, f, g):
        return pltpu.make_async_remote_copy(
            src_ref=src.at[f, g], dst_ref=dst.at[f, me],
            send_sem=ssem.at[f, g], recv_sem=rsem.at[f, me],
            device_id={"gy": g}, device_id_type=MESH)

    def y_send(src, dst, ssem, rsem, f, partners):
        for g in partners:
            y_copy(src, dst, ssem, rsem, f, g).start()

    def y_send_first(src, dst, ssem, rsem, f, first):
        for t in first:
            @pl.when(chip != t)
            def _():
                y_send(src, dst, ssem, rsem, f, [2 * t, 2 * t + 1])
        for dz in Y_ORDER:
            g = y_partner(dz, 0)
            other = g >= 0
            for t in first:
                other = other & (g != 2 * t)

            @pl.when(other)
            def _():
                y_send(src, dst, ssem, rsem, f, [g, g + 1])

    def y_wait_recv(src, dst, ssem, rsem, f):
        for g in y_all:
            pltpu.make_async_remote_copy(
                src_ref=src.at[f, g], dst_ref=dst.at[f, g],
                send_sem=ssem.at[f, g], recv_sem=rsem.at[f, g],
                device_id={"gy": g}, device_id_type=MESH).wait_recv()

    def y_wait_send(src, dst, ssem, rsem, f):
        for g in y_all:
            y_copy(src, dst, ssem, rsem, f, g).wait_send()

    def z_copy(buf, ssem, rsem, o, slot):
        return pltpu.make_async_remote_copy(
            src_ref=buf.at[slot], dst_ref=buf.at[slot],
            send_sem=ssem.at[o], recv_sem=rsem.at[o],
            device_id={"gz": z_partner(o, 1)}, device_id_type=MESH)

    def z_send(buf, ssem, rsem):
        for o in z_all:
            z_copy(buf, ssem, rsem, o, mz).start()

    def z_wait_recv(buf, ssem, rsem):
        for o in z_all:
            z_copy(buf, ssem, rsem, o, z_partner(o, -1)).wait_recv()

    def z_wait_send(buf, ssem, rsem):
        for o in z_all:
            z_copy(buf, ssem, rsem, o, mz).wait_send()

    def edge_copy(g):
        return pltpu.make_async_remote_copy(
            src_ref=edge_send.at[g], dst_ref=edge_recv.at[me],
            send_sem=e_ssem.at[g], recv_sem=e_rsem.at[me],
            device_id={"gy": g}, device_id_type=MESH)

    def halo_copies():
        up = pltpu.make_async_remote_copy(
            src_ref=halo_send.at[0], dst_ref=halo_recv.at[0],
            send_sem=halo_ssem.at[0], recv_sem=halo_rsem.at[0],
            device_id={"gz": lax.rem(mz + 1, gz)}, device_id_type=MESH)
        down = pltpu.make_async_remote_copy(
            src_ref=halo_send.at[1], dst_ref=halo_recv.at[1],
            send_sem=halo_ssem.at[1], recv_sem=halo_rsem.at[1],
            device_id={"gz": lax.rem(mz + gz - 1, gz)}, device_id_type=MESH)
        return up, down

    plane_id = lax.broadcasted_iota(jnp.int32, (planes, LANES), 0)

    def column(ref):
        def one(k, col):
            return jnp.where(plane_id == k, ref[k], col)

        return lax.fori_loop(0, planes, one, jnp.zeros((planes, LANES), f32))

    kx_lane = (lax.broadcasted_iota(jnp.int32, (1, NY), 1) % KX + 1).astype(f32)

    def slope_diff(values, low, high):
        above = jnp.concatenate([values[1:], high], axis=0)
        below = jnp.concatenate([low, values[:-1]], axis=0)
        return slope_wide * (above - below)

    copy_z[2].wait()
    slope = column(zs)
    slope_wide = jnp.concatenate([slope] * 8, axis=1)
    nothing = jnp.zeros((1, NY), f32)
    copy_in[1].wait()
    stage(1, vel[1, 0], vel[1, 1])
    copy_in[2].wait()
    for t in range(8):
        for part in range(2):
            for e, k in enumerate((0, planes - 1)):
                r = 4 * t + 2 * part + e
                edge_rows[r:r + 1, :] = vel[2, part, k:k + 1, t * 128:t * 128 + 128]
    edge_buf[...] = jnp.zeros((LANES, LANES), f32)
    for q in range(4):
        edge_buf[q * 32:q * 32 + 32, :32] = edge_rows[:32, q * 32:q * 32 + 32]
    edge_rows[:32, :] = edge_buf[...].T[:32]
    for j in range(KX):
        edge_send[j] = edge_rows[pl.ds(j, 2, stride=16), :]
    copy_in[0].wait()
    stage(
        0,
        slope_diff(vel[2, 0], nothing, nothing) - kx_lane * vel[0, 1],
        slope_diff(vel[2, 1], nothing, nothing) + kx_lane * vel[0, 0],
    )
    pl.semaphore_wait(barrier, len(y_all) + len(Z_ORDER))
    to_core = [[y_partner(dz, c) for dz in Y_ORDER] for c in range(2)]
    for partners in (to_core[0] + [mate], to_core[1]):
        for g in partners:
            edge_copy(g).start()
        y_send(send_f, recv_f, f_ssem, f_rsem, 1, partners)
        y_send(send_f, recv_f, f_ssem, f_rsem, 0, partners)
    for f in range(2):
        recv_f[f, me] = send_f[f, me]
    edge_recv[me] = edge_send[me]

    copy_z[0].wait()
    copy_z[1].wait()
    row = lax.broadcasted_iota(jnp.int32, (8, LANES), 0)
    lane = lax.broadcasted_iota(jnp.int32, (8, LANES), 1)
    offset = jnp.where(row < 2, 0, jnp.where(row < 4, 2, jnp.where((row == 4) | (row == 6), 1, -511)))
    ky_int = 4 * lane + offset
    ky_int = jnp.where((row == 1) | (row == 3) | (row >= 6), -ky_int, ky_int)
    ky_int = jnp.where((row == 1) & (lane == 0), -512, ky_int)
    ky = ky_int.astype(f32)
    kx = (me + 1).astype(f32)
    square = kx * kx + ky * ky

    def rows_of(k):
        return pl.ds(pl.multiple_of(k * 8, 8), 8)

    def factor(k, state):
        r, g = state
        low, up = zl[k], zu[k]
        inverse = 1.0 / (-(low + up) - square - low * r)
        m = low * inverse
        r = up * inverse
        g = -m * g
        inv_piv[rows_of(k), :] = inverse
        mult[rows_of(k), :] = m
        ratio[rows_of(k), :] = r
        beta[rows_of(k), :] = g
        return r, g

    zero = jnp.zeros((8, LANES), f32)
    one_v = jnp.ones((8, LANES), f32)
    lax.fori_loop(0, planes, factor, (zero, one_v))

    def unfold(i, state):
        b, g, width = state
        k = planes - 1 - i
        r = ratio[rows_of(k), :]
        b = beta[rows_of(k), :] - r * b
        g = -r * g
        beta[rows_of(k), :] = b
        gamma[rows_of(k), :] = g
        low_row[rows_of(k), :] = b * width
        high_row[rows_of(k), :] = g * width
        before = jnp.maximum(k - 1, 0)
        wider = width * (jnp.full((8, LANES), zl[k]) / jnp.full((8, LANES), zu[before]))
        return b, g, jnp.where(k > 0, wider, width)

    b0, g0, first_width = lax.fori_loop(0, planes, unfold, (zero, one_v, one_v))
    low_scale = -1.0 / (jnp.full((8, LANES), zl[0]) * first_width)
    high_scale = -1.0 / jnp.full((8, LANES), zu[planes - 1])
    last = slice((planes - 1) * 8, planes * 8)
    mat_all[mz, 0] = b0
    mat_all[mz, 1] = g0
    mat_all[mz, 2] = beta[last, :]
    mat_all[mz, 3] = gamma[last, :]
    z_send(mat_all, m_ssem, m_rsem)

    copy_ft.wait()
    first_lane = lax.broadcasted_iota(jnp.int32, (planes, LANES), 1) == 0

    def forward(f):
        quarters = []
        for q in range(4):
            block = recv_f[f, 4 * q:4 * q + 4].reshape(LANES, LANES).T
            quarters.append(jnp.concatenate([block[:64], block[64:]], axis=1))
        a = quarters[0] + quarters[2]
        b = quarters[0] - quarters[2]
        c = quarters[1] + quarters[3]
        e = quarters[1] - quarters[3]
        turned = jnp.concatenate([e[planes:], -e[:planes]], axis=0)
        spectra = []
        for first, z in ((0, a + c), (256, a - c)):
            both = product(z, ftab[0, :, first:first + 256], ftab[1, :, first:first + 256])
            rc, rs = both[:planes, :128], both[:planes, 128:]
            ic, is_ = both[planes:, :128], both[planes:, 128:]
            if first == 0:
                rs0, is0 = jnp.where(first_lane, 0.0, rs), jnp.where(first_lane, 0.0, is_)
                spectra.append((rc + is0, ic - rs0))
                spectra.append((jnp.where(first_lane, rs, rc - is_), jnp.where(first_lane, is_, ic + rs)))
            else:
                spectra.append((rc + is_, ic - rs))
                spectra.append((rc - is_, ic + rs))
        both = product(jnp.concatenate([b + turned, b - turned], axis=0), ftab[0, :, 512:], ftab[1, :, 512:])
        for half in range(2):
            cos, sin = both[:, half * 128:half * 128 + 128], both[:, 256 + half * 128:384 + half * 128]
            spectra.append((cos[:planes] + sin[planes:2 * planes], cos[planes:2 * planes] - sin[:planes]))
        for half in range(2):
            cos, sin = both[:, half * 128:half * 128 + 128], both[:, 256 + half * 128:384 + half * 128]
            spectra.append((cos[2 * planes:3 * planes] - sin[3 * planes:], cos[3 * planes:] + sin[2 * planes:3 * planes]))
        return spectra

    y_wait_recv(send_f, recv_f, f_ssem, f_rsem, 1)
    for s, (re, im) in enumerate(forward(1)):
        ky_row = ky[s:s + 1, :]
        vhat[s, 0] = -ky_row * im
        vhat[s, 1] = ky_row * re
    copy_et.wait()
    copy_tt.wait()
    for g in y_all:
        pltpu.make_async_remote_copy(
            src_ref=edge_send.at[g], dst_ref=edge_recv.at[g],
            send_sem=e_ssem.at[g], recv_sem=e_rsem.at[g],
            device_id={"gy": g}, device_id_type=MESH).wait_recv()
    for d in range(gy):
        edge_buf[2 * d:2 * d + 2, :] = edge_recv[d]
    partial = product(edge_buf[...].T[:, :32], etab[0], etab[1])
    for s in range(16):
        edge_sum[s] = partial[:, s * 128:s * 128 + 128]
    for s in range(8):
        cos, sin = turn[0, :, s * 128:s * 128 + 128], turn[1, :, s * 128:s * 128 + 128]
        for e in range(2):
            rc, rs, ic, is_ = (
                edge_sum[s + off, pl.ds(part + e, 32, stride=4), :] for part in (0, 2) for off in (0, 8))
            re, im = rc + is_, ic - rs
            edge[e, 0, s:s + 1, :] = jnp.sum(re * cos + im * sin, axis=0, keepdims=True)
            edge[e, 1, s:s + 1, :] = jnp.sum(im * cos - re * sin, axis=0, keepdims=True)
    below = jnp.full((8, LANES), zs[0]) / jnp.full((8, LANES), zl[0])
    above = jnp.full((8, LANES), zs[planes - 1]) / jnp.full((8, LANES), zu[planes - 1])
    y_wait_recv(send_f, recv_f, f_ssem, f_rsem, 0)
    for s, (re, im) in enumerate(forward(0)):
        field_re[pl.ds(s, planes, stride=8), :] = re + vhat[s, 0]
        field_im[pl.ds(s, planes, stride=8), :] = im + vhat[s, 1]

    sums = [[zero] * 4 for _ in range(4)]
    for k in range(planes):
        rows = slice(k * 8, k * 8 + 8)
        re, im, low, high = field_re[rows, :], field_im[rows, :], low_row[rows, :], high_row[rows, :]
        for n, term in enumerate((low * re, low * im, high * re, high * im)):
            sums[n][k % 4] = sums[n][k % 4] + term
    lr, li, hr, hi = ((t[0] + t[1]) + (t[2] + t[3]) for t in sums)
    rhs_all[mz, 0] = low_scale * lr - below * edge[0, 0]
    rhs_all[mz, 1] = low_scale * li - below * edge[0, 1]
    rhs_all[mz, 2] = high_scale * hr + above * edge[1, 0]
    rhs_all[mz, 3] = high_scale * hi + above * edge[1, 1]
    z_send(rhs_all, r_ssem, r_rsem)

    def down(k, state):
        sr, si = state
        inverse, m = inv_piv[rows_of(k), :], mult[rows_of(k), :]
        sr = field_re[rows_of(k), :] * inverse - m * sr
        si = field_im[rows_of(k), :] * inverse - m * si
        field_re[rows_of(k), :] = sr
        field_im[rows_of(k), :] = si
        return sr, si

    lax.fori_loop(0, planes, down, (zero, zero), unroll=True)

    def back(i, state):
        ar, ai = state
        k = planes - 1 - i
        r = ratio[rows_of(k), :]
        ar = field_re[rows_of(k), :] - r * ar
        ai = field_im[rows_of(k), :] - r * ai
        field_re[rows_of(k), :] = ar
        field_im[rows_of(k), :] = ai
        return ar, ai

    lax.fori_loop(0, planes, back, (zero, zero), unroll=True)

    z_wait_recv(mat_all, m_ssem, m_rsem)
    red_r[0] = zero
    red_e[0, 0] = zero
    red_e[0, 1] = zero

    def reduce_matrix(d, r):
        den = 1.0 / (1.0 - mat_all[d, 0] * r)
        psi = mat_all[d, 1] * den
        br = mat_all[d, 2] * r
        red_den[d] = den
        red_bden[d] = mat_all[d, 0] * den
        red_psi[d] = psi
        red_b31[d] = mat_all[d, 2] + br * (mat_all[d, 0] * den)
        red_br[d] = br * den
        r = mat_all[d, 3] + br * psi
        red_r[d + 1] = r
        return r

    lax.fori_loop(0, gz, reduce_matrix, zero)
    z_wait_recv(rhs_all, r_ssem, r_rsem)

    def reduce_rhs(d, state):
        er, ei = state
        den, bden, brden, step = red_den[d], red_bden[d], red_br[d], red_b31[d]
        red_phi[d, 0] = den * rhs_all[d, 0] + bden * er
        red_phi[d, 1] = den * rhs_all[d, 1] + bden * ei
        er = (rhs_all[d, 2] + brden * rhs_all[d, 0]) + step * er
        ei = (rhs_all[d, 3] + brden * rhs_all[d, 1]) + step * ei
        red_e[d + 1, 0] = er
        red_e[d + 1, 1] = ei
        return er, ei

    lax.fori_loop(0, gz, reduce_rhs, (zero, zero), unroll=True)
    red_f[gz, 0] = zero
    red_f[gz, 1] = zero

    def reduce_back(i, state):
        fr, fi = state
        d = gz - 1 - i
        psi = red_psi[d]
        fr = red_phi[d, 0] + psi * fr
        fi = red_phi[d, 1] + psi * fi
        red_f[d, 0] = fr
        red_f[d, 1] = fi
        return fr, fi

    lax.fori_loop(0, gz, reduce_back, (zero, zero), unroll=True)
    before = [red_e[mz, part] + red_r[mz] * red_f[mz, part] for part in range(2)]
    after = [red_f[mz + 1, part] for part in range(2)]

    def finish(k, _):
        b, g = beta[rows_of(k), :], gamma[rows_of(k), :]
        field_re[rows_of(k), :] = field_re[rows_of(k), :] + b * before[0] + g * after[0]
        field_im[rows_of(k), :] = field_im[rows_of(k), :] + b * before[1] + g * after[1]
        return 0

    lax.fori_loop(0, planes, finish, 0, unroll=True)

    copy_it.wait()

    def inverse(f, spectra):
        parts = []
        for first in (0, 256):
            (pr, pi), (nr, ni) = spectra[first // 128], spectra[first // 128 + 1]
            cr, sr, ci, si = pr + nr, ni - pi, pi + ni, pr - nr
            if first == 0:
                cr, sr = jnp.where(first_lane, pr, cr), jnp.where(first_lane, nr, sr)
                ci, si = jnp.where(first_lane, pi, ci), jnp.where(first_lane, ni, si)
            z = jnp.concatenate([jnp.concatenate([cr, sr], axis=1), jnp.concatenate([ci, si], axis=1)], axis=0)
            parts.append(product(z, itab[0, first:first + 256, :], itab[1, first:first + 256, :]))
        (ar, ai), (br, bi), (cr, ci), (dr, di) = spectra[4:]
        z = jnp.concatenate([
            jnp.concatenate([ar, br, -ai, -bi], axis=1),
            jnp.concatenate([ai, bi, ar, br], axis=1),
            jnp.concatenate([cr, dr, ci, di], axis=1),
            jnp.concatenate([ci, di, -cr, -dr], axis=1)], axis=0)
        odd = product(z, itab[0, 512:, :], itab[1, 512:, :])
        g1, g3 = odd[:64], odd[64:]
        s02, d02 = parts[0] + parts[1], parts[0] - parts[1]
        s13, d13 = g1 + g3, g1 - g3
        turned = jnp.concatenate([-d13[planes:], d13[:planes]], axis=0)
        for q, value in enumerate((s02 + s13, d02 + turned, s02 - s13, d02 - turned)):
            block = jnp.concatenate([value[:, :128], value[:, 128:]], axis=0).T
            send_b[f, 4 * q:4 * q + 4] = block.reshape(4, 32, LANES)

    tiles = [(field_re[pl.ds(s, planes, stride=8), :], field_im[pl.ds(s, planes, stride=8), :]) for s in range(8)]
    inverse(0, tiles)
    y_send_first(send_b, recv_b, b_ssem, b_rsem, 0, (0, 1, 2))
    y_send(send_b, recv_b, b_ssem, b_rsem, 0, [mate])
    recv_b[0, me] = send_b[0, me]
    inverse(1, [(-ky[s:s + 1, :] * im, ky[s:s + 1, :] * re) for s, (re, im) in enumerate(tiles)])
    y_send_first(send_b, recv_b, b_ssem, b_rsem, 1, (0, 1, 2))
    y_send(send_b, recv_b, b_ssem, b_rsem, 1, [mate])
    recv_b[1, me] = send_b[1, me]

    def unstage(f, grad):
        for j in range(KX):
            rows_buf[pl.ds(j, 32, stride=16), :] = recv_b[f, j]
        for c in range(4):
            block = rows_buf[c * 128:(c + 1) * 128, :].T
            for h in range(2):
                for part in range(2):
                    first = h * 64 + part * 32
                    grad[part, :, h * 512 + c * 128:h * 512 + c * 128 + 128] = block[first:first + 32]

    for g in y_all:
        edge_copy(g).wait_send()
    for f in range(2):
        y_wait_send(send_f, recv_f, f_ssem, f_rsem, f)
    z_wait_send(mat_all, m_ssem, m_rsem)
    z_wait_send(rhs_all, r_ssem, r_rsem)
    y_wait_recv(send_b, recv_b, b_ssem, b_rsem, 0)
    unstage(0, grad)
    for part in range(2):
        halo_send[0, part:part + 1, :] = grad[part, planes - 1:planes, :]
        halo_send[1, part:part + 1, :] = grad[part, 0:1, :]
    halo_p = halo_copies()
    halo_p[0].start()
    halo_p[1].start()
    out[0, 0] = vel[0, 0] + kx_lane * grad[1]
    out[0, 1] = vel[0, 1] - kx_lane * grad[0]
    y_wait_send(send_b, recv_b, b_ssem, b_rsem, 0)
    y_wait_recv(send_b, recv_b, b_ssem, b_rsem, 1)
    unstage(1, grad_q)
    for part in range(2):
        out[1, part] = vel[1, part] - grad_q[part]
    halo_p[0].wait_recv()
    halo_p[1].wait_recv()
    for part in range(2):
        low = jnp.where(mz > 0, halo_recv[0, part:part + 1, :], 0.0)
        high = jnp.where(mz < gz - 1, halo_recv[1, part:part + 1, :], 0.0)
        out[2, part] = vel[2, part] - slope_diff(grad[part], low, high)

    for copy in halo_p:
        copy.wait_send()
    y_wait_send(send_b, recv_b, b_ssem, b_rsem, 1)


def shards(velocity, z_lower, z_upper, z_slope):
    gy, gz = lax.axis_size("gy"), lax.axis_size("gz")
    planes = velocity.shape[2]
    ftab, itab, etab, turn = (jnp.asarray(table) for table in fourier_tables())
    f32 = jnp.float32
    hbm = pl.BlockSpec(memory_space=pl.ANY)
    lines = (planes * 8 + 8, LANES)
    dma = pltpu.SemaphoreType.DMA
    return pl.pallas_call(
        functools.partial(kernel, planes, gy, gz),
        out_shape=jax.ShapeDtypeStruct(velocity.shape, f32),
        in_specs=[pl.BlockSpec(memory_space=pltpu.HBM)] * 8,
        out_specs=pl.BlockSpec(memory_space=pltpu.VMEM),
        scratch_shapes=[
            pltpu.VMEM(velocity.shape, f32),
            pltpu.SMEM((planes,), f32),
            pltpu.SMEM((planes,), f32),
            pltpu.SMEM((planes,), f32),
            pltpu.VMEM(ftab.shape, jnp.bfloat16),
            pltpu.VMEM(itab.shape, jnp.bfloat16),
            pltpu.VMEM(etab.shape, jnp.bfloat16),
            pltpu.VMEM(turn.shape, f32),
            pltpu.VMEM((LANES, LANES), f32),
            pltpu.VMEM((160, LANES), f32),
            pltpu.VMEM((gy, 2, LANES), f32),
            pltpu.VMEM((gy, 2, LANES), f32),
            pltpu.VMEM((16, LANES, LANES), f32),
            pltpu.VMEM((3, 2, 8, LANES), f32),
            pltpu.VMEM((528, LANES), f32),
            pltpu.VMEM((2, gy, 32, LANES), f32),
            pltpu.VMEM((2, gy, 32, LANES), f32),
            pltpu.VMEM((2, gy, 32, LANES), f32),
            pltpu.VMEM((2, gy, 32, LANES), f32),
            pltpu.VMEM((4, 2, NY), f32),
            pltpu.VMEM((4, 2, NY), f32),
            pltpu.VMEM((8, 2, planes, LANES), f32),
            pltpu.VMEM(lines, f32),
            pltpu.VMEM(lines, f32),
            pltpu.VMEM(lines, f32),
            pltpu.VMEM(lines, f32),
            pltpu.VMEM(lines, f32),
            pltpu.VMEM(lines, f32),
            pltpu.VMEM(lines, f32),
            pltpu.VMEM(lines, f32),
            pltpu.VMEM(lines, f32),
            pltpu.VMEM((gz, 4, 8, LANES), f32),
            pltpu.VMEM((gz, 4, 8, LANES), f32),
            pltpu.VMEM((gz, 8, LANES), f32),
            pltpu.VMEM((gz, 8, LANES), f32),
            pltpu.VMEM((gz, 8, LANES), f32),
            pltpu.VMEM((gz, 8, LANES), f32),
            pltpu.VMEM((gz, 8, LANES), f32),
            pltpu.VMEM((gz + 1, 8, LANES), f32),
            pltpu.VMEM((gz + 1, 2, 8, LANES), f32),
            pltpu.VMEM((gz, 2, 8, LANES), f32),
            pltpu.VMEM((gz + 1, 2, 8, LANES), f32),
            pltpu.VMEM((2, planes, NY), f32),
            pltpu.VMEM((2, planes, NY), f32),
            dma((10,)), dma((gy,)), dma((gy,)), dma((2,)), dma((2,)),
            dma((2, gy)), dma((2, gy)), dma((2, gy)), dma((2, gy)),
            dma((gz,)), dma((gz,)), dma((gz,)), dma((gz,)),
        ],
        compiler_params=pltpu.CompilerParams(
            collective_id=0, has_side_effects=True, vmem_limit_bytes=40 * 1024 * 1024
        ),
        name="project",
    )(*(pltpu.with_memory_space_constraint(a, pltpu.HBM) for a in (velocity, z_lower, z_upper, z_slope, ftab, itab, etab, turn)))


def solution(mesh):
    placed = (P(None, None, "gz", "gy"), P("gz"), P("gz"), P("gz"))
    return jax.shard_map(
        shards, mesh=mesh, in_specs=placed, out_specs=P(None, None, "gz", "gy"), check_vma=False
    )
```

```python
import functools

import jax
import jax.numpy as jnp
import ml_dtypes
import numpy as np
from jax import lax
from jax.experimental import pallas as pl
from jax.experimental.pallas import tpu as pltpu
from jax.sharding import PartitionSpec as P

NY = 1024
KX = 16
LANES = 128
MESH = pl.DeviceIdType.MESH
Y_ORDER = (4, 3, -3, 2, -2, 1, -1)
Z_ORDER = sorted(
    ((dx, dy) for dx in (2, 1, -1, 0) for dy in (2, 1, -1, 0) if (dx, dy) != (0, 0)),
    key=lambda pair: -abs(pair[0]) - abs(pair[1]),
)


def fourier_tables():
    place = np.arange(256)
    y = 64 * ((place % 128) // 32) + 32 * (place // 128) + place % 32

    def pair(m):
        phase = 2.0 * np.pi * ((y[:, None] * m[None, :]) % NY) / NY
        return np.cos(phase), np.sin(phase)

    c0, s0 = pair(4 * np.arange(128))
    s0[:, 0] = (-1.0) ** y
    c2, s2 = pair(4 * np.arange(128) + 2)
    c1, s1 = pair(4 * np.arange(256) + 1)
    table = np.concatenate([c0, s0, c2, s2, c1, s1], axis=1)

    def split(values):
        high = values.astype(ml_dtypes.bfloat16)
        low = (values - high.astype(np.float64)).astype(ml_dtypes.bfloat16)
        return np.stack([high, low])

    t, u = np.arange(128), np.arange(256)
    half = 4 * t
    half[0] = NY // 2
    m = np.concatenate([4 * t, -half, 4 * t + 2, -4 * t - 2, 4 * u + 1, -4 * u - 1]) % NY

    def both(y):
        phase = 2.0 * np.pi * ((y[:, None] * m[None, :]) % NY) / NY
        return np.cos(phase), np.sin(phase)

    r = np.arange(32)
    edge = np.concatenate(both(64 * (r // 2) + r % 2), axis=1)
    turn = np.stack(both(8 * (r % 8) + 2 * (r // 8))).astype(np.float32)
    return split(table), split(table.T / NY), split(edge), turn


def dot(a, b):
    return jnp.dot(a, b, preferred_element_type=jnp.float32)


def product(values, high, low):
    top = values.astype(jnp.bfloat16)
    rest = (values - top.astype(jnp.float32)).astype(jnp.bfloat16)
    rows = values.shape[0]
    both = dot(jnp.concatenate([top, rest], axis=0), high)
    return both[:rows] + both[rows:] + dot(top, low)


def kernel(
    planes, gy, gz,
    vel_hbm, zl_hbm, zu_hbm, zs_hbm, ftab_hbm, itab_hbm, etab_hbm, turn_hbm, out,
    vel, zl, zu, zs, ftab, itab, etab, turn, edge_buf, edge_rows, edge_send, edge_recv, edge_sum, edge, rows_buf, send_f, recv_f, send_b, recv_b,
    halo_send, halo_recv, vhat, field_re, field_im,
    inv_piv, mult, ratio, beta, gamma, low_row, high_row,
    mat_all, rhs_all, red_den, red_bden, red_psi, red_b31, red_br, red_r, red_e, red_phi, red_f,
    grad, grad_q,
    in_sem, e_ssem, e_rsem, halo_ssem, halo_rsem, f_ssem, f_rsem, b_ssem, b_rsem, m_ssem, m_rsem, r_ssem, r_rsem,
):
    me = lax.axis_index("gy")
    mz = lax.axis_index("gz")
    f32 = jnp.float32

    copy_in = [pltpu.make_async_copy(vel_hbm.at[c], vel.at[c], in_sem.at[c]) for c in range(3)]
    copy_z = [
        pltpu.make_async_copy(src, dst, in_sem.at[3 + i])
        for i, (src, dst) in enumerate(((zl_hbm, zl), (zu_hbm, zu), (zs_hbm, zs)))
    ]
    copy_ft = pltpu.make_async_copy(ftab_hbm, ftab, in_sem.at[6])
    copy_it = pltpu.make_async_copy(itab_hbm, itab, in_sem.at[7])
    copy_et = pltpu.make_async_copy(etab_hbm, etab, in_sem.at[8])
    copy_tt = pltpu.make_async_copy(turn_hbm, turn, in_sem.at[9])
    copy_in[1].start()
    copy_in[2].start()
    barrier = pltpu.get_barrier_semaphore()

    chips, chip, core = gy // 2, me // 2, lax.rem(me, 2)
    mate = me + 1 - 2 * core

    def y_partner(dz, c):
        return lax.rem(chip + dz + chips, chips) * 2 + c

    def z_partner(o, sign):
        dx, dy = Z_ORDER[o]
        return lax.rem(mz // 4 + sign * dx + 4, 4) * 4 + lax.rem(mz + sign * dy + 4, 4)

    z_all = range(len(Z_ORDER))
    y_all = [y_partner(dz, c) for dz in Y_ORDER for c in range(2)] + [mate]
    for g in y_all:
        pl.semaphore_signal(barrier, inc=1, device_id={"gy": g}, device_id_type=MESH)
    for o in z_all:
        pl.semaphore_signal(barrier, inc=1, device_id={"gz": z_partner(o, 1)}, device_id_type=MESH)
    for copy in (copy_z[2], copy_in[0], copy_z[0], copy_z[1], copy_et, copy_tt, copy_ft, copy_it):
        copy.start()

    def stage(f, re, im):
        for c in range(4):
            a = slice(c * 128, c * 128 + 128)
            b = slice(512 + c * 128, 512 + c * 128 + 128)
            block = jnp.concatenate([re[:, a], im[:, a], re[:, b], im[:, b]], axis=0)
            rows_buf[c * 128:(c + 1) * 128, :] = block.T
        for j in range(KX):
            send_f[f, j] = rows_buf[pl.ds(j, 32, stride=16), :]

    def y_copy(src, dst, ssem, rsem, f, g):
        return pltpu.make_async_remote_copy(
            src_ref=src.at[f, g], dst_ref=dst.at[f, me],
            send_sem=ssem.at[f], recv_sem=rsem.at[f],
            device_id={"gy": g}, device_id_type=MESH)

    def y_send(src, dst, ssem, rsem, f, partners):
        for g in partners:
            y_copy(src, dst, ssem, rsem, f, g).start()

    def y_send_first(src, dst, ssem, rsem, f, first):
        for t in first:
            @pl.when(chip != t)
            def _():
                y_send(src, dst, ssem, rsem, f, [2 * t, 2 * t + 1])
        for dz in Y_ORDER:
            g = y_partner(dz, 0)
            other = g >= 0
            for t in first:
                other = other & (g != 2 * t)

            @pl.when(other)
            def _():
                y_send(src, dst, ssem, rsem, f, [g, g + 1])

    def y_all_copy(src, dst, ssem, rsem, f):
        rest = pl.ds(0, gy - 1)
        return pltpu.make_async_remote_copy(
            src_ref=src.at[f, rest], dst_ref=dst.at[f, rest], send_sem=ssem.at[f], recv_sem=rsem.at[f],
            device_id={"gy": mate}, device_id_type=MESH)

    def y_wait_recv(src, dst, ssem, rsem, f):
        y_all_copy(src, dst, ssem, rsem, f).wait_recv()

    def y_wait_send(src, dst, ssem, rsem, f):
        y_all_copy(src, dst, ssem, rsem, f).wait_send()

    def z_copy(buf, ssem, rsem, g, slots):
        return pltpu.make_async_remote_copy(
            src_ref=buf.at[slots], dst_ref=buf.at[slots], send_sem=ssem, recv_sem=rsem,
            device_id={"gz": g}, device_id_type=MESH)

    def z_send(buf, ssem, rsem):
        for o in z_all:
            z_copy(buf, ssem, rsem, z_partner(o, 1), mz).start()

    def z_wait_recv(buf, ssem, rsem):
        z_copy(buf, ssem, rsem, z_partner(0, 1), pl.ds(0, gz - 1)).wait_recv()

    def z_wait_send(buf, ssem, rsem):
        z_copy(buf, ssem, rsem, z_partner(0, 1), pl.ds(0, gz - 1)).wait_send()

    def edge_copy(g):
        return pltpu.make_async_remote_copy(
            src_ref=edge_send.at[g], dst_ref=edge_recv.at[me], send_sem=e_ssem, recv_sem=e_rsem,
            device_id={"gy": g}, device_id_type=MESH)

    def edge_all_copy():
        rest = pl.ds(0, gy - 1)
        return pltpu.make_async_remote_copy(
            src_ref=edge_send.at[rest], dst_ref=edge_recv.at[rest], send_sem=e_ssem, recv_sem=e_rsem,
            device_id={"gy": mate}, device_id_type=MESH)

    def halo_copies():
        up = pltpu.make_async_remote_copy(
            src_ref=halo_send.at[0], dst_ref=halo_recv.at[0],
            send_sem=halo_ssem.at[0], recv_sem=halo_rsem.at[0],
            device_id={"gz": lax.rem(mz + 1, gz)}, device_id_type=MESH)
        down = pltpu.make_async_remote_copy(
            src_ref=halo_send.at[1], dst_ref=halo_recv.at[1],
            send_sem=halo_ssem.at[1], recv_sem=halo_rsem.at[1],
            device_id={"gz": lax.rem(mz + gz - 1, gz)}, device_id_type=MESH)
        return up, down

    plane_id = lax.broadcasted_iota(jnp.int32, (planes, LANES), 0)

    def column(ref):
        def one(k, col):
            return jnp.where(plane_id == k, ref[k], col)

        return lax.fori_loop(0, planes, one, jnp.zeros((planes, LANES), f32))

    kx_lane = (lax.broadcasted_iota(jnp.int32, (1, NY), 1) % KX + 1).astype(f32)

    def slope_diff(values, low, high):
        above = jnp.concatenate([values[1:], high], axis=0)
        below = jnp.concatenate([low, values[:-1]], axis=0)
        return slope_wide * (above - below)

    copy_z[2].wait()
    slope = column(zs)
    slope_wide = jnp.concatenate([slope] * 8, axis=1)
    nothing = jnp.zeros((1, NY), f32)
    copy_in[1].wait()
    stage(1, vel[1, 0], vel[1, 1])
    copy_in[2].wait()
    for t in range(8):
        for part in range(2):
            for e, k in enumerate((0, planes - 1)):
                r = 4 * t + 2 * part + e
                edge_rows[r:r + 1, :] = vel[2, part, k:k + 1, t * 128:t * 128 + 128]
    edge_buf[...] = jnp.zeros((LANES, LANES), f32)
    for q in range(4):
        edge_buf[q * 32:q * 32 + 32, :32] = edge_rows[:32, q * 32:q * 32 + 32]
    edge_rows[:32, :] = edge_buf[...].T[:32]
    for j in range(KX):
        edge_send[j] = edge_rows[pl.ds(j, 2, stride=16), :]
    copy_in[0].wait()
    stage(
        0,
        slope_diff(vel[2, 0], nothing, nothing) - kx_lane * vel[0, 1],
        slope_diff(vel[2, 1], nothing, nothing) + kx_lane * vel[0, 0],
    )
    pl.semaphore_wait(barrier, len(y_all) + len(Z_ORDER))
    to_core = [[y_partner(dz, c) for dz in Y_ORDER] for c in range(2)]
    for partners in (to_core[0] + [mate], to_core[1]):
        for g in partners:
            edge_copy(g).start()
        y_send(send_f, recv_f, f_ssem, f_rsem, 1, partners)
        y_send(send_f, recv_f, f_ssem, f_rsem, 0, partners)
    for f in range(2):
        recv_f[f, me] = send_f[f, me]
    edge_recv[me] = edge_send[me]

    copy_z[0].wait()
    copy_z[1].wait()
    row = lax.broadcasted_iota(jnp.int32, (8, LANES), 0)
    lane = lax.broadcasted_iota(jnp.int32, (8, LANES), 1)
    offset = jnp.where(row < 2, 0, jnp.where(row < 4, 2, jnp.where((row == 4) | (row == 6), 1, -511)))
    ky_int = 4 * lane + offset
    ky_int = jnp.where((row == 1) | (row == 3) | (row >= 6), -ky_int, ky_int)
    ky_int = jnp.where((row == 1) & (lane == 0), -512, ky_int)
    ky = ky_int.astype(f32)
    kx = (me + 1).astype(f32)
    square = kx * kx + ky * ky

    def rows_of(k):
        return pl.ds(pl.multiple_of(k * 8, 8), 8)

    def factor(k, state):
        r, g = state
        low, up = zl[k], zu[k]
        inverse = 1.0 / (-(low + up) - square - low * r)
        m = low * inverse
        r = up * inverse
        g = -m * g
        inv_piv[rows_of(k), :] = inverse
        mult[rows_of(k), :] = m
        ratio[rows_of(k), :] = r
        beta[rows_of(k), :] = g
        return r, g

    zero = jnp.zeros((8, LANES), f32)
    one_v = jnp.ones((8, LANES), f32)
    lax.fori_loop(0, planes, factor, (zero, one_v))

    def unfold(i, state):
        b, g, width = state
        k = planes - 1 - i
        r = ratio[rows_of(k), :]
        b = beta[rows_of(k), :] - r * b
        g = -r * g
        beta[rows_of(k), :] = b
        gamma[rows_of(k), :] = g
        low_row[rows_of(k), :] = b * width
        high_row[rows_of(k), :] = g * width
        before = jnp.maximum(k - 1, 0)
        wider = width * (jnp.full((8, LANES), zl[k]) / jnp.full((8, LANES), zu[before]))
        return b, g, jnp.where(k > 0, wider, width)

    b0, g0, first_width = lax.fori_loop(0, planes, unfold, (zero, one_v, one_v))
    low_scale = -1.0 / (jnp.full((8, LANES), zl[0]) * first_width)
    high_scale = -1.0 / jnp.full((8, LANES), zu[planes - 1])
    last = slice((planes - 1) * 8, planes * 8)
    mat_all[mz, 0] = b0
    mat_all[mz, 1] = g0
    mat_all[mz, 2] = beta[last, :]
    mat_all[mz, 3] = gamma[last, :]
    z_send(mat_all, m_ssem, m_rsem)

    copy_ft.wait()
    first_lane = lax.broadcasted_iota(jnp.int32, (planes, LANES), 1) == 0

    def forward(f):
        quarters = []
        for q in range(4):
            block = recv_f[f, 4 * q:4 * q + 4].reshape(LANES, LANES).T
            quarters.append(jnp.concatenate([block[:64], block[64:]], axis=1))
        a = quarters[0] + quarters[2]
        b = quarters[0] - quarters[2]
        c = quarters[1] + quarters[3]
        e = quarters[1] - quarters[3]
        turned = jnp.concatenate([e[planes:], -e[:planes]], axis=0)
        spectra = []
        for first, z in ((0, a + c), (256, a - c)):
            both = product(z, ftab[0, :, first:first + 256], ftab[1, :, first:first + 256])
            rc, rs = both[:planes, :128], both[:planes, 128:]
            ic, is_ = both[planes:, :128], both[planes:, 128:]
            if first == 0:
                rs0, is0 = jnp.where(first_lane, 0.0, rs), jnp.where(first_lane, 0.0, is_)
                spectra.append((rc + is0, ic - rs0))
                spectra.append((jnp.where(first_lane, rs, rc - is_), jnp.where(first_lane, is_, ic + rs)))
            else:
                spectra.append((rc + is_, ic - rs))
                spectra.append((rc - is_, ic + rs))
        both = product(jnp.concatenate([b + turned, b - turned], axis=0), ftab[0, :, 512:], ftab[1, :, 512:])
        for half in range(2):
            cos, sin = both[:, half * 128:half * 128 + 128], both[:, 256 + half * 128:384 + half * 128]
            spectra.append((cos[:planes] + sin[planes:2 * planes], cos[planes:2 * planes] - sin[:planes]))
        for half in range(2):
            cos, sin = both[:, half * 128:half * 128 + 128], both[:, 256 + half * 128:384 + half * 128]
            spectra.append((cos[2 * planes:3 * planes] - sin[3 * planes:], cos[3 * planes:] + sin[2 * planes:3 * planes]))
        return spectra

    y_wait_recv(send_f, recv_f, f_ssem, f_rsem, 1)
    for s, (re, im) in enumerate(forward(1)):
        ky_row = ky[s:s + 1, :]
        vhat[s, 0] = -ky_row * im
        vhat[s, 1] = ky_row * re
    copy_et.wait()
    copy_tt.wait()
    edge_all_copy().wait_recv()
    for d in range(gy):
        edge_buf[2 * d:2 * d + 2, :] = edge_recv[d]
    partial = product(edge_buf[...].T[:, :32], etab[0], etab[1])
    for s in range(16):
        edge_sum[s] = partial[:, s * 128:s * 128 + 128]
    for s in range(8):
        cos, sin = turn[0, :, s * 128:s * 128 + 128], turn[1, :, s * 128:s * 128 + 128]
        for e in range(2):
            rc, rs, ic, is_ = (
                edge_sum[s + off, pl.ds(part + e, 32, stride=4), :] for part in (0, 2) for off in (0, 8))
            re, im = rc + is_, ic - rs
            edge[e, 0, s:s + 1, :] = jnp.sum(re * cos + im * sin, axis=0, keepdims=True)
            edge[e, 1, s:s + 1, :] = jnp.sum(im * cos - re * sin, axis=0, keepdims=True)
    below = jnp.full((8, LANES), zs[0]) / jnp.full((8, LANES), zl[0])
    above = jnp.full((8, LANES), zs[planes - 1]) / jnp.full((8, LANES), zu[planes - 1])
    y_wait_recv(send_f, recv_f, f_ssem, f_rsem, 0)
    for s, (re, im) in enumerate(forward(0)):
        field_re[pl.ds(s, planes, stride=8), :] = re + vhat[s, 0]
        field_im[pl.ds(s, planes, stride=8), :] = im + vhat[s, 1]

    sums = [[zero] * 4 for _ in range(4)]
    for k in range(planes):
        rows = slice(k * 8, k * 8 + 8)
        re, im, low, high = field_re[rows, :], field_im[rows, :], low_row[rows, :], high_row[rows, :]
        for n, term in enumerate((low * re, low * im, high * re, high * im)):
            sums[n][k % 4] = sums[n][k % 4] + term
    lr, li, hr, hi = ((t[0] + t[1]) + (t[2] + t[3]) for t in sums)
    rhs_all[mz, 0] = low_scale * lr - below * edge[0, 0]
    rhs_all[mz, 1] = low_scale * li - below * edge[0, 1]
    rhs_all[mz, 2] = high_scale * hr + above * edge[1, 0]
    rhs_all[mz, 3] = high_scale * hi + above * edge[1, 1]
    z_send(rhs_all, r_ssem, r_rsem)

    def down(k, state):
        sr, si = state
        inverse, m = inv_piv[rows_of(k), :], mult[rows_of(k), :]
        sr = field_re[rows_of(k), :] * inverse - m * sr
        si = field_im[rows_of(k), :] * inverse - m * si
        field_re[rows_of(k), :] = sr
        field_im[rows_of(k), :] = si
        return sr, si

    lax.fori_loop(0, planes, down, (zero, zero), unroll=True)

    def back(i, state):
        ar, ai = state
        k = planes - 1 - i
        r = ratio[rows_of(k), :]
        ar = field_re[rows_of(k), :] - r * ar
        ai = field_im[rows_of(k), :] - r * ai
        field_re[rows_of(k), :] = ar
        field_im[rows_of(k), :] = ai
        return ar, ai

    lax.fori_loop(0, planes, back, (zero, zero), unroll=True)

    z_wait_recv(mat_all, m_ssem, m_rsem)
    red_r[0] = zero
    red_e[0, 0] = zero
    red_e[0, 1] = zero

    def reduce_matrix(d, r):
        den = 1.0 / (1.0 - mat_all[d, 0] * r)
        psi = mat_all[d, 1] * den
        br = mat_all[d, 2] * r
        red_den[d] = den
        red_bden[d] = mat_all[d, 0] * den
        red_psi[d] = psi
        red_b31[d] = mat_all[d, 2] + br * (mat_all[d, 0] * den)
        red_br[d] = br * den
        r = mat_all[d, 3] + br * psi
        red_r[d + 1] = r
        return r

    lax.fori_loop(0, gz, reduce_matrix, zero)
    z_wait_recv(rhs_all, r_ssem, r_rsem)

    def reduce_rhs(d, state):
        er, ei = state
        den, bden, brden, step = red_den[d], red_bden[d], red_br[d], red_b31[d]
        red_phi[d, 0] = den * rhs_all[d, 0] + bden * er
        red_phi[d, 1] = den * rhs_all[d, 1] + bden * ei
        er = (rhs_all[d, 2] + brden * rhs_all[d, 0]) + step * er
        ei = (rhs_all[d, 3] + brden * rhs_all[d, 1]) + step * ei
        red_e[d + 1, 0] = er
        red_e[d + 1, 1] = ei
        return er, ei

    lax.fori_loop(0, gz, reduce_rhs, (zero, zero), unroll=True)
    red_f[gz, 0] = zero
    red_f[gz, 1] = zero

    def reduce_back(i, state):
        fr, fi = state
        d = gz - 1 - i
        psi = red_psi[d]
        fr = red_phi[d, 0] + psi * fr
        fi = red_phi[d, 1] + psi * fi
        red_f[d, 0] = fr
        red_f[d, 1] = fi
        return fr, fi

    lax.fori_loop(0, gz, reduce_back, (zero, zero), unroll=True)
    before = [red_e[mz, part] + red_r[mz] * red_f[mz, part] for part in range(2)]
    after = [red_f[mz + 1, part] for part in range(2)]

    def finish(k, _):
        b, g = beta[rows_of(k), :], gamma[rows_of(k), :]
        field_re[rows_of(k), :] = field_re[rows_of(k), :] + b * before[0] + g * after[0]
        field_im[rows_of(k), :] = field_im[rows_of(k), :] + b * before[1] + g * after[1]
        return 0

    lax.fori_loop(0, planes, finish, 0, unroll=True)

    copy_it.wait()

    def inverse(f, spectra):
        parts = []
        for first in (0, 256):
            (pr, pi), (nr, ni) = spectra[first // 128], spectra[first // 128 + 1]
            cr, sr, ci, si = pr + nr, ni - pi, pi + ni, pr - nr
            if first == 0:
                cr, sr = jnp.where(first_lane, pr, cr), jnp.where(first_lane, nr, sr)
                ci, si = jnp.where(first_lane, pi, ci), jnp.where(first_lane, ni, si)
            z = jnp.concatenate([jnp.concatenate([cr, sr], axis=1), jnp.concatenate([ci, si], axis=1)], axis=0)
            parts.append(product(z, itab[0, first:first + 256, :], itab[1, first:first + 256, :]))
        (ar, ai), (br, bi), (cr, ci), (dr, di) = spectra[4:]
        z = jnp.concatenate([
            jnp.concatenate([ar, br, -ai, -bi], axis=1),
            jnp.concatenate([ai, bi, ar, br], axis=1),
            jnp.concatenate([cr, dr, ci, di], axis=1),
            jnp.concatenate([ci, di, -cr, -dr], axis=1)], axis=0)
        odd = product(z, itab[0, 512:, :], itab[1, 512:, :])
        g1, g3 = odd[:64], odd[64:]
        s02, d02 = parts[0] + parts[1], parts[0] - parts[1]
        s13, d13 = g1 + g3, g1 - g3
        turned = jnp.concatenate([-d13[planes:], d13[:planes]], axis=0)
        for q, value in enumerate((s02 + s13, d02 + turned, s02 - s13, d02 - turned)):
            block = jnp.concatenate([value[:, :128], value[:, 128:]], axis=0).T
            send_b[f, 4 * q:4 * q + 4] = block.reshape(4, 32, LANES)

    tiles = [(field_re[pl.ds(s, planes, stride=8), :], field_im[pl.ds(s, planes, stride=8), :]) for s in range(8)]
    inverse(0, tiles)
    y_send_first(send_b, recv_b, b_ssem, b_rsem, 0, (0, 1, 2))
    y_send(send_b, recv_b, b_ssem, b_rsem, 0, [mate])
    recv_b[0, me] = send_b[0, me]
    inverse(1, [(-ky[s:s + 1, :] * im, ky[s:s + 1, :] * re) for s, (re, im) in enumerate(tiles)])
    y_send_first(send_b, recv_b, b_ssem, b_rsem, 1, (0, 1, 2))
    y_send(send_b, recv_b, b_ssem, b_rsem, 1, [mate])
    recv_b[1, me] = send_b[1, me]

    def unstage(f, grad):
        for j in range(KX):
            rows_buf[pl.ds(j, 32, stride=16), :] = recv_b[f, j]
        for c in range(4):
            block = rows_buf[c * 128:(c + 1) * 128, :].T
            for h in range(2):
                for part in range(2):
                    first = h * 64 + part * 32
                    grad[part, :, h * 512 + c * 128:h * 512 + c * 128 + 128] = block[first:first + 32]

    edge_all_copy().wait_send()
    for f in range(2):
        y_wait_send(send_f, recv_f, f_ssem, f_rsem, f)
    z_wait_send(mat_all, m_ssem, m_rsem)
    z_wait_send(rhs_all, r_ssem, r_rsem)
    y_wait_recv(send_b, recv_b, b_ssem, b_rsem, 0)
    unstage(0, grad)
    for part in range(2):
        halo_send[0, part:part + 1, :] = grad[part, planes - 1:planes, :]
        halo_send[1, part:part + 1, :] = grad[part, 0:1, :]
    halo_p = halo_copies()
    halo_p[0].start()
    halo_p[1].start()
    out[0, 0] = vel[0, 0] + kx_lane * grad[1]
    out[0, 1] = vel[0, 1] - kx_lane * grad[0]
    y_wait_send(send_b, recv_b, b_ssem, b_rsem, 0)
    y_wait_recv(send_b, recv_b, b_ssem, b_rsem, 1)
    unstage(1, grad_q)
    for part in range(2):
        out[1, part] = vel[1, part] - grad_q[part]
    halo_p[0].wait_recv()
    halo_p[1].wait_recv()
    for part in range(2):
        low = jnp.where(mz > 0, halo_recv[0, part:part + 1, :], 0.0)
        high = jnp.where(mz < gz - 1, halo_recv[1, part:part + 1, :], 0.0)
        out[2, part] = vel[2, part] - slope_diff(grad[part], low, high)

    for copy in halo_p:
        copy.wait_send()
    y_wait_send(send_b, recv_b, b_ssem, b_rsem, 1)


def shards(velocity, z_lower, z_upper, z_slope):
    gy, gz = lax.axis_size("gy"), lax.axis_size("gz")
    planes = velocity.shape[2]
    ftab, itab, etab, turn = (jnp.asarray(table) for table in fourier_tables())
    f32 = jnp.float32
    hbm = pl.BlockSpec(memory_space=pl.ANY)
    lines = (planes * 8 + 8, LANES)
    dma = pltpu.SemaphoreType.DMA
    return pl.pallas_call(
        functools.partial(kernel, planes, gy, gz),
        out_shape=jax.ShapeDtypeStruct(velocity.shape, f32),
        in_specs=[pl.BlockSpec(memory_space=pltpu.HBM)] * 8,
        out_specs=pl.BlockSpec(memory_space=pltpu.VMEM),
        scratch_shapes=[
            pltpu.VMEM(velocity.shape, f32),
            pltpu.SMEM((planes,), f32),
            pltpu.SMEM((planes,), f32),
            pltpu.SMEM((planes,), f32),
            pltpu.VMEM(ftab.shape, jnp.bfloat16),
            pltpu.VMEM(itab.shape, jnp.bfloat16),
            pltpu.VMEM(etab.shape, jnp.bfloat16),
            pltpu.VMEM(turn.shape, f32),
            pltpu.VMEM((LANES, LANES), f32),
            pltpu.VMEM((160, LANES), f32),
            pltpu.VMEM((gy, 2, LANES), f32),
            pltpu.VMEM((gy, 2, LANES), f32),
            pltpu.VMEM((16, LANES, LANES), f32),
            pltpu.VMEM((3, 2, 8, LANES), f32),
            pltpu.VMEM((528, LANES), f32),
            pltpu.VMEM((2, gy, 32, LANES), f32),
            pltpu.VMEM((2, gy, 32, LANES), f32),
            pltpu.VMEM((2, gy, 32, LANES), f32),
            pltpu.VMEM((2, gy, 32, LANES), f32),
            pltpu.VMEM((4, 2, NY), f32),
            pltpu.VMEM((4, 2, NY), f32),
            pltpu.VMEM((8, 2, planes, LANES), f32),
            pltpu.VMEM(lines, f32),
            pltpu.VMEM(lines, f32),
            pltpu.VMEM(lines, f32),
            pltpu.VMEM(lines, f32),
            pltpu.VMEM(lines, f32),
            pltpu.VMEM(lines, f32),
            pltpu.VMEM(lines, f32),
            pltpu.VMEM(lines, f32),
            pltpu.VMEM(lines, f32),
            pltpu.VMEM((gz, 4, 8, LANES), f32),
            pltpu.VMEM((gz, 4, 8, LANES), f32),
            pltpu.VMEM((gz, 8, LANES), f32),
            pltpu.VMEM((gz, 8, LANES), f32),
            pltpu.VMEM((gz, 8, LANES), f32),
            pltpu.VMEM((gz, 8, LANES), f32),
            pltpu.VMEM((gz, 8, LANES), f32),
            pltpu.VMEM((gz + 1, 8, LANES), f32),
            pltpu.VMEM((gz + 1, 2, 8, LANES), f32),
            pltpu.VMEM((gz, 2, 8, LANES), f32),
            pltpu.VMEM((gz + 1, 2, 8, LANES), f32),
            pltpu.VMEM((2, planes, NY), f32),
            pltpu.VMEM((2, planes, NY), f32),
            dma((10,)), dma, dma, dma((2,)), dma((2,)),
            dma((2,)), dma((2,)), dma((2,)), dma((2,)),
            dma, dma, dma, dma,
        ],
        compiler_params=pltpu.CompilerParams(
            collective_id=0, has_side_effects=True, vmem_limit_bytes=40 * 1024 * 1024
        ),
        name="project",
    )(*(pltpu.with_memory_space_constraint(a, pltpu.HBM) for a in (velocity, z_lower, z_upper, z_slope, ftab, itab, etab, turn)))


def solution(mesh):
    placed = (P(None, None, "gz", "gy"), P("gz"), P("gz"), P("gz"))
    return jax.shard_map(
        shards, mesh=mesh, in_specs=placed, out_specs=P(None, None, "gz", "gy"), check_vma=False
    )
```

```python
import functools

import jax
import jax.numpy as jnp
import ml_dtypes
import numpy as np
from jax import lax
from jax.experimental import pallas as pl
from jax.experimental.pallas import tpu as pltpu
from jax.sharding import PartitionSpec as P

NY = 1024
KX = 16
LANES = 128
MESH = pl.DeviceIdType.MESH
Y_ORDER = (4, 3, -3, 2, -2, 1, -1)
Z_ORDER = sorted(
    ((dx, dy) for dx in (2, 1, -1, 0) for dy in (2, 1, -1, 0) if (dx, dy) != (0, 0)),
    key=lambda pair: -abs(pair[0]) - abs(pair[1]),
)


def fourier_tables():
    place = np.arange(256)
    y = 64 * ((place % 128) // 32) + 32 * (place // 128) + place % 32

    def pair(m):
        phase = 2.0 * np.pi * ((y[:, None] * m[None, :]) % NY) / NY
        return np.cos(phase), np.sin(phase)

    c0, s0 = pair(4 * np.arange(128))
    s0[:, 0] = (-1.0) ** y
    c2, s2 = pair(4 * np.arange(128) + 2)
    c1, s1 = pair(4 * np.arange(256) + 1)
    table = np.concatenate([c0, s0, c2, s2, c1, s1], axis=1)

    def split(values):
        high = values.astype(ml_dtypes.bfloat16)
        low = (values - high.astype(np.float64)).astype(ml_dtypes.bfloat16)
        return np.stack([high, low])

    t, u = np.arange(128), np.arange(256)
    half = 4 * t
    half[0] = NY // 2
    m = np.concatenate([4 * t, -half, 4 * t + 2, -4 * t - 2, 4 * u + 1, -4 * u - 1]) % NY

    def both(y):
        phase = 2.0 * np.pi * ((y[:, None] * m[None, :]) % NY) / NY
        return np.cos(phase), np.sin(phase)

    r = np.arange(32)
    edge = np.concatenate(both(64 * (r // 2) + r % 2), axis=1)
    turn = np.stack(both(8 * (r % 8) + 2 * (r // 8))).astype(np.float32)
    return split(table), split(table.T / NY), split(edge), turn


def dot(a, b):
    return jnp.dot(a, b, preferred_element_type=jnp.float32)


def product(values, high, low):
    top = values.astype(jnp.bfloat16)
    rest = (values - top.astype(jnp.float32)).astype(jnp.bfloat16)
    rows = values.shape[0]
    both = dot(jnp.concatenate([top, rest], axis=0), high)
    return both[:rows] + both[rows:] + dot(top, low)


def kernel(
    planes, gy, gz,
    vel_hbm, zl_hbm, zu_hbm, zs_hbm, ftab_hbm, itab_hbm, etab_hbm, turn_hbm, out,
    vel, zl, zu, zs, ftab, itab, etab, turn, edge_buf, edge_rows, edge_send, edge_recv, edge_sum, edge, rows_buf, send_f, recv_f, send_b, recv_b,
    halo_send, halo_recv, vhat, field_re, field_im,
    inv_piv, mult, ratio, beta, gamma, low_row, high_row,
    mat_all, rhs_all, red_den, red_bden, red_psi, red_b31, red_br, red_r, red_e, red_phi, red_f,
    grad, grad_q,
    in_sem, e_ssem, e_rsem, halo_ssem, halo_rsem, f_ssem, f_rsem, b_ssem, b_rsem, m_ssem, m_rsem, r_ssem, r_rsem,
):
    me = lax.axis_index("gy")
    mz = lax.axis_index("gz")
    f32 = jnp.float32

    copy_in = [pltpu.make_async_copy(vel_hbm.at[c], vel.at[c], in_sem.at[c]) for c in range(3)]
    copy_z = [
        pltpu.make_async_copy(src, dst, in_sem.at[3 + i])
        for i, (src, dst) in enumerate(((zl_hbm, zl), (zu_hbm, zu), (zs_hbm, zs)))
    ]
    copy_ft = pltpu.make_async_copy(ftab_hbm, ftab, in_sem.at[6])
    copy_it = pltpu.make_async_copy(itab_hbm, itab, in_sem.at[7])
    copy_et = pltpu.make_async_copy(etab_hbm, etab, in_sem.at[8])
    copy_tt = pltpu.make_async_copy(turn_hbm, turn, in_sem.at[9])
    copy_in[1].start()
    copy_in[2].start()
    barrier = pltpu.get_barrier_semaphore()

    chips, chip, core = gy // 2, me // 2, lax.rem(me, 2)
    mate = me + 1 - 2 * core

    def y_partner(dz, c):
        return lax.rem(chip + dz + chips, chips) * 2 + c

    def z_partner(o, sign):
        dx, dy = Z_ORDER[o]
        return lax.rem(mz // 4 + sign * dx + 4, 4) * 4 + lax.rem(mz + sign * dy + 4, 4)

    z_all = range(len(Z_ORDER))
    y_all = [y_partner(dz, c) for dz in Y_ORDER for c in range(2)] + [mate]
    for g in y_all:
        pl.semaphore_signal(barrier, inc=1, device_id={"gy": g}, device_id_type=MESH)
    for o in z_all:
        pl.semaphore_signal(barrier, inc=1, device_id={"gz": z_partner(o, 1)}, device_id_type=MESH)
    for copy in (copy_z[2], copy_in[0], copy_z[0], copy_z[1], copy_et, copy_tt, copy_ft, copy_it):
        copy.start()

    def stage(f, re, im):
        for c in range(4):
            a = slice(c * 128, c * 128 + 128)
            b = slice(512 + c * 128, 512 + c * 128 + 128)
            block = jnp.concatenate([re[:, a], im[:, a], re[:, b], im[:, b]], axis=0)
            rows_buf[c * 128:(c + 1) * 128, :] = block.T
        for j in range(KX):
            send_f[f, j] = rows_buf[pl.ds(j, 32, stride=16), :]

    def y_copy(src, dst, ssem, rsem, f, g):
        return pltpu.make_async_remote_copy(
            src_ref=src.at[f, g], dst_ref=dst.at[f, me],
            send_sem=ssem.at[f], recv_sem=rsem.at[f],
            device_id={"gy": g}, device_id_type=MESH)

    def y_send(src, dst, ssem, rsem, f, partners):
        for g in partners:
            y_copy(src, dst, ssem, rsem, f, g).start()

    def y_send_first(src, dst, ssem, rsem, f, first):
        for t in first:
            @pl.when(chip != t)
            def _():
                y_send(src, dst, ssem, rsem, f, [2 * t, 2 * t + 1])
        for dz in Y_ORDER:
            g = y_partner(dz, 0)
            other = g >= 0
            for t in first:
                other = other & (g != 2 * t)

            @pl.when(other)
            def _():
                y_send(src, dst, ssem, rsem, f, [g, g + 1])

    def y_all_copy(src, dst, ssem, rsem, f):
        rest = pl.ds(0, gy - 1)
        return pltpu.make_async_remote_copy(
            src_ref=src.at[f, rest], dst_ref=dst.at[f, rest], send_sem=ssem.at[f], recv_sem=rsem.at[f],
            device_id={"gy": mate}, device_id_type=MESH)

    def y_wait_recv(src, dst, ssem, rsem, f):
        y_all_copy(src, dst, ssem, rsem, f).wait_recv()

    def y_wait_send(src, dst, ssem, rsem, f):
        y_all_copy(src, dst, ssem, rsem, f).wait_send()

    def z_copy(buf, ssem, rsem, g, slots):
        return pltpu.make_async_remote_copy(
            src_ref=buf.at[slots], dst_ref=buf.at[slots], send_sem=ssem, recv_sem=rsem,
            device_id={"gz": g}, device_id_type=MESH)

    def z_send(buf, ssem, rsem):
        for o in z_all:
            z_copy(buf, ssem, rsem, z_partner(o, 1), mz).start()

    def z_wait_recv(buf, ssem, rsem):
        z_copy(buf, ssem, rsem, z_partner(0, 1), pl.ds(0, gz - 1)).wait_recv()

    def z_wait_send(buf, ssem, rsem):
        z_copy(buf, ssem, rsem, z_partner(0, 1), pl.ds(0, gz - 1)).wait_send()

    def edge_copy(g):
        return pltpu.make_async_remote_copy(
            src_ref=edge_send.at[g], dst_ref=edge_recv.at[me], send_sem=e_ssem, recv_sem=e_rsem,
            device_id={"gy": g}, device_id_type=MESH)

    def edge_all_copy():
        rest = pl.ds(0, gy - 1)
        return pltpu.make_async_remote_copy(
            src_ref=edge_send.at[rest], dst_ref=edge_recv.at[rest], send_sem=e_ssem, recv_sem=e_rsem,
            device_id={"gy": mate}, device_id_type=MESH)

    def halo_copies():
        up = pltpu.make_async_remote_copy(
            src_ref=halo_send.at[0], dst_ref=halo_recv.at[0],
            send_sem=halo_ssem.at[0], recv_sem=halo_rsem.at[0],
            device_id={"gz": lax.rem(mz + 1, gz)}, device_id_type=MESH)
        down = pltpu.make_async_remote_copy(
            src_ref=halo_send.at[1], dst_ref=halo_recv.at[1],
            send_sem=halo_ssem.at[1], recv_sem=halo_rsem.at[1],
            device_id={"gz": lax.rem(mz + gz - 1, gz)}, device_id_type=MESH)
        return up, down

    plane_id = lax.broadcasted_iota(jnp.int32, (planes, LANES), 0)

    def column(ref):
        def one(k, col):
            return jnp.where(plane_id == k, ref[k], col)

        return lax.fori_loop(0, planes, one, jnp.zeros((planes, LANES), f32))

    kx_lane = (lax.broadcasted_iota(jnp.int32, (1, NY), 1) % KX + 1).astype(f32)

    def slope_diff(values, low, high):
        above = jnp.concatenate([values[1:], high], axis=0)
        below = jnp.concatenate([low, values[:-1]], axis=0)
        return slope_wide * (above - below)

    copy_z[2].wait()
    slope = column(zs)
    slope_wide = jnp.concatenate([slope] * 8, axis=1)
    nothing = jnp.zeros((1, NY), f32)
    copy_in[1].wait()
    stage(1, vel[1, 0], vel[1, 1])
    copy_in[2].wait()
    for t in range(8):
        for part in range(2):
            for e, k in enumerate((0, planes - 1)):
                r = 4 * t + 2 * part + e
                edge_rows[r:r + 1, :] = vel[2, part, k:k + 1, t * 128:t * 128 + 128]
    edge_buf[...] = jnp.zeros((LANES, LANES), f32)
    for q in range(4):
        edge_buf[q * 32:q * 32 + 32, :32] = edge_rows[:32, q * 32:q * 32 + 32]
    edge_rows[:32, :] = edge_buf[...].T[:32]
    for j in range(KX):
        edge_send[j] = edge_rows[pl.ds(j, 2, stride=16), :]
    copy_in[0].wait()
    stage(
        0,
        slope_diff(vel[2, 0], nothing, nothing) - kx_lane * vel[0, 1],
        slope_diff(vel[2, 1], nothing, nothing) + kx_lane * vel[0, 0],
    )
    pl.semaphore_wait(barrier, len(y_all) + len(Z_ORDER))
    to_core = [[y_partner(dz, c) for dz in Y_ORDER] for c in range(2)]
    for partners in (to_core[0] + [mate], to_core[1]):
        y_send(send_f, recv_f, f_ssem, f_rsem, 1, partners)
        for g in partners:
            edge_copy(g).start()
        y_send(send_f, recv_f, f_ssem, f_rsem, 0, partners)
    for f in range(2):
        recv_f[f, me] = send_f[f, me]
    edge_recv[me] = edge_send[me]

    copy_z[0].wait()
    copy_z[1].wait()
    row = lax.broadcasted_iota(jnp.int32, (8, LANES), 0)
    lane = lax.broadcasted_iota(jnp.int32, (8, LANES), 1)
    offset = jnp.where(row < 2, 0, jnp.where(row < 4, 2, jnp.where((row == 4) | (row == 6), 1, -511)))
    ky_int = 4 * lane + offset
    ky_int = jnp.where((row == 1) | (row == 3) | (row >= 6), -ky_int, ky_int)
    ky_int = jnp.where((row == 1) & (lane == 0), -512, ky_int)
    ky = ky_int.astype(f32)
    kx = (me + 1).astype(f32)
    square = kx * kx + ky * ky

    def rows_of(k):
        return pl.ds(pl.multiple_of(k * 8, 8), 8)

    def factor(k, state):
        r, g = state
        low, up = zl[k], zu[k]
        inverse = 1.0 / (-(low + up) - square - low * r)
        m = low * inverse
        r = up * inverse
        g = -m * g
        inv_piv[rows_of(k), :] = inverse
        mult[rows_of(k), :] = m
        ratio[rows_of(k), :] = r
        beta[rows_of(k), :] = g
        return r, g

    zero = jnp.zeros((8, LANES), f32)
    one_v = jnp.ones((8, LANES), f32)
    lax.fori_loop(0, planes, factor, (zero, one_v))

    def unfold(i, state):
        b, g, width = state
        k = planes - 1 - i
        r = ratio[rows_of(k), :]
        b = beta[rows_of(k), :] - r * b
        g = -r * g
        beta[rows_of(k), :] = b
        gamma[rows_of(k), :] = g
        low_row[rows_of(k), :] = b * width
        high_row[rows_of(k), :] = g * width
        before = jnp.maximum(k - 1, 0)
        wider = width * (jnp.full((8, LANES), zl[k]) / jnp.full((8, LANES), zu[before]))
        return b, g, jnp.where(k > 0, wider, width)

    b0, g0, first_width = lax.fori_loop(0, planes, unfold, (zero, one_v, one_v))
    low_scale = -1.0 / (jnp.full((8, LANES), zl[0]) * first_width)
    high_scale = -1.0 / jnp.full((8, LANES), zu[planes - 1])
    last = slice((planes - 1) * 8, planes * 8)
    mat_all[mz, 0] = b0
    mat_all[mz, 1] = g0
    mat_all[mz, 2] = beta[last, :]
    mat_all[mz, 3] = gamma[last, :]
    z_send(mat_all, m_ssem, m_rsem)

    copy_ft.wait()
    first_lane = lax.broadcasted_iota(jnp.int32, (planes, LANES), 1) == 0

    def forward(f):
        quarters = []
        for q in range(4):
            block = recv_f[f, 4 * q:4 * q + 4].reshape(LANES, LANES).T
            quarters.append(jnp.concatenate([block[:64], block[64:]], axis=1))
        a = quarters[0] + quarters[2]
        b = quarters[0] - quarters[2]
        c = quarters[1] + quarters[3]
        e = quarters[1] - quarters[3]
        turned = jnp.concatenate([e[planes:], -e[:planes]], axis=0)
        spectra = []
        for first, z in ((0, a + c), (256, a - c)):
            both = product(z, ftab[0, :, first:first + 256], ftab[1, :, first:first + 256])
            rc, rs = both[:planes, :128], both[:planes, 128:]
            ic, is_ = both[planes:, :128], both[planes:, 128:]
            if first == 0:
                rs0, is0 = jnp.where(first_lane, 0.0, rs), jnp.where(first_lane, 0.0, is_)
                spectra.append((rc + is0, ic - rs0))
                spectra.append((jnp.where(first_lane, rs, rc - is_), jnp.where(first_lane, is_, ic + rs)))
            else:
                spectra.append((rc + is_, ic - rs))
                spectra.append((rc - is_, ic + rs))
        both = product(jnp.concatenate([b + turned, b - turned], axis=0), ftab[0, :, 512:], ftab[1, :, 512:])
        for half in range(2):
            cos, sin = both[:, half * 128:half * 128 + 128], both[:, 256 + half * 128:384 + half * 128]
            spectra.append((cos[:planes] + sin[planes:2 * planes], cos[planes:2 * planes] - sin[:planes]))
        for half in range(2):
            cos, sin = both[:, half * 128:half * 128 + 128], both[:, 256 + half * 128:384 + half * 128]
            spectra.append((cos[2 * planes:3 * planes] - sin[3 * planes:], cos[3 * planes:] + sin[2 * planes:3 * planes]))
        return spectra

    y_wait_recv(send_f, recv_f, f_ssem, f_rsem, 1)
    for s, (re, im) in enumerate(forward(1)):
        ky_row = ky[s:s + 1, :]
        vhat[s, 0] = -ky_row * im
        vhat[s, 1] = ky_row * re
    copy_et.wait()
    copy_tt.wait()
    edge_all_copy().wait_recv()
    for d in range(gy):
        edge_buf[2 * d:2 * d + 2, :] = edge_recv[d]
    partial = product(edge_buf[...].T[:, :32], etab[0], etab[1])
    for s in range(16):
        edge_sum[s] = partial[:, s * 128:s * 128 + 128]
    for s in range(8):
        cos, sin = turn[0, :, s * 128:s * 128 + 128], turn[1, :, s * 128:s * 128 + 128]
        for e in range(2):
            rc, rs, ic, is_ = (
                edge_sum[s + off, pl.ds(part + e, 32, stride=4), :] for part in (0, 2) for off in (0, 8))
            re, im = rc + is_, ic - rs
            edge[e, 0, s:s + 1, :] = jnp.sum(re * cos + im * sin, axis=0, keepdims=True)
            edge[e, 1, s:s + 1, :] = jnp.sum(im * cos - re * sin, axis=0, keepdims=True)
    below = jnp.full((8, LANES), zs[0]) / jnp.full((8, LANES), zl[0])
    above = jnp.full((8, LANES), zs[planes - 1]) / jnp.full((8, LANES), zu[planes - 1])
    y_wait_recv(send_f, recv_f, f_ssem, f_rsem, 0)
    for s, (re, im) in enumerate(forward(0)):
        field_re[pl.ds(s, planes, stride=8), :] = re + vhat[s, 0]
        field_im[pl.ds(s, planes, stride=8), :] = im + vhat[s, 1]

    sums = [[zero] * 4 for _ in range(4)]
    for k in range(planes):
        rows = slice(k * 8, k * 8 + 8)
        re, im, low, high = field_re[rows, :], field_im[rows, :], low_row[rows, :], high_row[rows, :]
        for n, term in enumerate((low * re, low * im, high * re, high * im)):
            sums[n][k % 4] = sums[n][k % 4] + term
    lr, li, hr, hi = ((t[0] + t[1]) + (t[2] + t[3]) for t in sums)
    rhs_all[mz, 0] = low_scale * lr - below * edge[0, 0]
    rhs_all[mz, 1] = low_scale * li - below * edge[0, 1]
    rhs_all[mz, 2] = high_scale * hr + above * edge[1, 0]
    rhs_all[mz, 3] = high_scale * hi + above * edge[1, 1]
    z_send(rhs_all, r_ssem, r_rsem)

    def down(k, state):
        sr, si = state
        inverse, m = inv_piv[rows_of(k), :], mult[rows_of(k), :]
        sr = field_re[rows_of(k), :] * inverse - m * sr
        si = field_im[rows_of(k), :] * inverse - m * si
        field_re[rows_of(k), :] = sr
        field_im[rows_of(k), :] = si
        return sr, si

    lax.fori_loop(0, planes, down, (zero, zero), unroll=True)

    def back(i, state):
        ar, ai = state
        k = planes - 1 - i
        r = ratio[rows_of(k), :]
        ar = field_re[rows_of(k), :] - r * ar
        ai = field_im[rows_of(k), :] - r * ai
        field_re[rows_of(k), :] = ar
        field_im[rows_of(k), :] = ai
        return ar, ai

    lax.fori_loop(0, planes, back, (zero, zero), unroll=True)

    z_wait_recv(mat_all, m_ssem, m_rsem)
    red_r[0] = zero
    red_e[0, 0] = zero
    red_e[0, 1] = zero

    def reduce_matrix(d, r):
        den = 1.0 / (1.0 - mat_all[d, 0] * r)
        psi = mat_all[d, 1] * den
        br = mat_all[d, 2] * r
        red_den[d] = den
        red_bden[d] = mat_all[d, 0] * den
        red_psi[d] = psi
        red_b31[d] = mat_all[d, 2] + br * (mat_all[d, 0] * den)
        red_br[d] = br * den
        r = mat_all[d, 3] + br * psi
        red_r[d + 1] = r
        return r

    lax.fori_loop(0, gz, reduce_matrix, zero)
    z_wait_recv(rhs_all, r_ssem, r_rsem)

    def reduce_rhs(d, state):
        er, ei = state
        den, bden, brden, step = red_den[d], red_bden[d], red_br[d], red_b31[d]
        red_phi[d, 0] = den * rhs_all[d, 0] + bden * er
        red_phi[d, 1] = den * rhs_all[d, 1] + bden * ei
        er = (rhs_all[d, 2] + brden * rhs_all[d, 0]) + step * er
        ei = (rhs_all[d, 3] + brden * rhs_all[d, 1]) + step * ei
        red_e[d + 1, 0] = er
        red_e[d + 1, 1] = ei
        return er, ei

    lax.fori_loop(0, gz, reduce_rhs, (zero, zero), unroll=True)
    red_f[gz, 0] = zero
    red_f[gz, 1] = zero

    def reduce_back(i, state):
        fr, fi = state
        d = gz - 1 - i
        psi = red_psi[d]
        fr = red_phi[d, 0] + psi * fr
        fi = red_phi[d, 1] + psi * fi
        red_f[d, 0] = fr
        red_f[d, 1] = fi
        return fr, fi

    lax.fori_loop(0, gz, reduce_back, (zero, zero), unroll=True)
    before = [red_e[mz, part] + red_r[mz] * red_f[mz, part] for part in range(2)]
    after = [red_f[mz + 1, part] for part in range(2)]

    def finish(k, _):
        b, g = beta[rows_of(k), :], gamma[rows_of(k), :]
        field_re[rows_of(k), :] = field_re[rows_of(k), :] + b * before[0] + g * after[0]
        field_im[rows_of(k), :] = field_im[rows_of(k), :] + b * before[1] + g * after[1]
        return 0

    lax.fori_loop(0, planes, finish, 0, unroll=True)

    copy_it.wait()

    def inverse(f, spectra):
        parts = []
        for first in (0, 256):
            (pr, pi), (nr, ni) = spectra[first // 128], spectra[first // 128 + 1]
            cr, sr, ci, si = pr + nr, ni - pi, pi + ni, pr - nr
            if first == 0:
                cr, sr = jnp.where(first_lane, pr, cr), jnp.where(first_lane, nr, sr)
                ci, si = jnp.where(first_lane, pi, ci), jnp.where(first_lane, ni, si)
            z = jnp.concatenate([jnp.concatenate([cr, sr], axis=1), jnp.concatenate([ci, si], axis=1)], axis=0)
            parts.append(product(z, itab[0, first:first + 256, :], itab[1, first:first + 256, :]))
        (ar, ai), (br, bi), (cr, ci), (dr, di) = spectra[4:]
        z = jnp.concatenate([
            jnp.concatenate([ar, br, -ai, -bi], axis=1),
            jnp.concatenate([ai, bi, ar, br], axis=1),
            jnp.concatenate([cr, dr, ci, di], axis=1),
            jnp.concatenate([ci, di, -cr, -dr], axis=1)], axis=0)
        odd = product(z, itab[0, 512:, :], itab[1, 512:, :])
        g1, g3 = odd[:64], odd[64:]
        s02, d02 = parts[0] + parts[1], parts[0] - parts[1]
        s13, d13 = g1 + g3, g1 - g3
        turned = jnp.concatenate([-d13[planes:], d13[:planes]], axis=0)
        for q, value in enumerate((s02 + s13, d02 + turned, s02 - s13, d02 - turned)):
            block = jnp.concatenate([value[:, :128], value[:, 128:]], axis=0).T
            send_b[f, 4 * q:4 * q + 4] = block.reshape(4, 32, LANES)

    tiles = [(field_re[pl.ds(s, planes, stride=8), :], field_im[pl.ds(s, planes, stride=8), :]) for s in range(8)]
    inverse(0, tiles)
    y_send_first(send_b, recv_b, b_ssem, b_rsem, 0, (0, 1, 2))
    y_send(send_b, recv_b, b_ssem, b_rsem, 0, [mate])
    recv_b[0, me] = send_b[0, me]
    inverse(1, [(-ky[s:s + 1, :] * im, ky[s:s + 1, :] * re) for s, (re, im) in enumerate(tiles)])
    y_send_first(send_b, recv_b, b_ssem, b_rsem, 1, (0, 1, 2))
    y_send(send_b, recv_b, b_ssem, b_rsem, 1, [mate])
    recv_b[1, me] = send_b[1, me]

    def unstage(f, grad):
        for j in range(KX):
            rows_buf[pl.ds(j, 32, stride=16), :] = recv_b[f, j]
        for c in range(4):
            block = rows_buf[c * 128:(c + 1) * 128, :].T
            for h in range(2):
                for part in range(2):
                    first = h * 64 + part * 32
                    grad[part, :, h * 512 + c * 128:h * 512 + c * 128 + 128] = block[first:first + 32]

    edge_all_copy().wait_send()
    for f in range(2):
        y_wait_send(send_f, recv_f, f_ssem, f_rsem, f)
    z_wait_send(mat_all, m_ssem, m_rsem)
    z_wait_send(rhs_all, r_ssem, r_rsem)
    y_wait_recv(send_b, recv_b, b_ssem, b_rsem, 0)
    unstage(0, grad)
    for part in range(2):
        halo_send[0, part:part + 1, :] = grad[part, planes - 1:planes, :]
        halo_send[1, part:part + 1, :] = grad[part, 0:1, :]
    halo_p = halo_copies()
    halo_p[0].start()
    halo_p[1].start()
    out[0, 0] = vel[0, 0] + kx_lane * grad[1]
    out[0, 1] = vel[0, 1] - kx_lane * grad[0]
    y_wait_send(send_b, recv_b, b_ssem, b_rsem, 0)
    y_wait_recv(send_b, recv_b, b_ssem, b_rsem, 1)
    unstage(1, grad_q)
    for part in range(2):
        out[1, part] = vel[1, part] - grad_q[part]
    halo_p[0].wait_recv()
    halo_p[1].wait_recv()
    for part in range(2):
        low = jnp.where(mz > 0, halo_recv[0, part:part + 1, :], 0.0)
        high = jnp.where(mz < gz - 1, halo_recv[1, part:part + 1, :], 0.0)
        out[2, part] = vel[2, part] - slope_diff(grad[part], low, high)

    for copy in halo_p:
        copy.wait_send()
    y_wait_send(send_b, recv_b, b_ssem, b_rsem, 1)


def shards(velocity, z_lower, z_upper, z_slope):
    gy, gz = lax.axis_size("gy"), lax.axis_size("gz")
    planes = velocity.shape[2]
    ftab, itab, etab, turn = (jnp.asarray(table) for table in fourier_tables())
    f32 = jnp.float32
    hbm = pl.BlockSpec(memory_space=pl.ANY)
    lines = (planes * 8 + 8, LANES)
    dma = pltpu.SemaphoreType.DMA
    return pl.pallas_call(
        functools.partial(kernel, planes, gy, gz),
        out_shape=jax.ShapeDtypeStruct(velocity.shape, f32),
        in_specs=[pl.BlockSpec(memory_space=pltpu.HBM)] * 8,
        out_specs=pl.BlockSpec(memory_space=pltpu.VMEM),
        scratch_shapes=[
            pltpu.VMEM(velocity.shape, f32),
            pltpu.SMEM((planes,), f32),
            pltpu.SMEM((planes,), f32),
            pltpu.SMEM((planes,), f32),
            pltpu.VMEM(ftab.shape, jnp.bfloat16),
            pltpu.VMEM(itab.shape, jnp.bfloat16),
            pltpu.VMEM(etab.shape, jnp.bfloat16),
            pltpu.VMEM(turn.shape, f32),
            pltpu.VMEM((LANES, LANES), f32),
            pltpu.VMEM((160, LANES), f32),
            pltpu.VMEM((gy, 2, LANES), f32),
            pltpu.VMEM((gy, 2, LANES), f32),
            pltpu.VMEM((16, LANES, LANES), f32),
            pltpu.VMEM((3, 2, 8, LANES), f32),
            pltpu.VMEM((528, LANES), f32),
            pltpu.VMEM((2, gy, 32, LANES), f32),
            pltpu.VMEM((2, gy, 32, LANES), f32),
            pltpu.VMEM((2, gy, 32, LANES), f32),
            pltpu.VMEM((2, gy, 32, LANES), f32),
            pltpu.VMEM((4, 2, NY), f32),
            pltpu.VMEM((4, 2, NY), f32),
            pltpu.VMEM((8, 2, planes, LANES), f32),
            pltpu.VMEM(lines, f32),
            pltpu.VMEM(lines, f32),
            pltpu.VMEM(lines, f32),
            pltpu.VMEM(lines, f32),
            pltpu.VMEM(lines, f32),
            pltpu.VMEM(lines, f32),
            pltpu.VMEM(lines, f32),
            pltpu.VMEM(lines, f32),
            pltpu.VMEM(lines, f32),
            pltpu.VMEM((gz, 4, 8, LANES), f32),
            pltpu.VMEM((gz, 4, 8, LANES), f32),
            pltpu.VMEM((gz, 8, LANES), f32),
            pltpu.VMEM((gz, 8, LANES), f32),
            pltpu.VMEM((gz, 8, LANES), f32),
            pltpu.VMEM((gz, 8, LANES), f32),
            pltpu.VMEM((gz, 8, LANES), f32),
            pltpu.VMEM((gz + 1, 8, LANES), f32),
            pltpu.VMEM((gz + 1, 2, 8, LANES), f32),
            pltpu.VMEM((gz, 2, 8, LANES), f32),
            pltpu.VMEM((gz + 1, 2, 8, LANES), f32),
            pltpu.VMEM((2, planes, NY), f32),
            pltpu.VMEM((2, planes, NY), f32),
            dma((10,)), dma, dma, dma((2,)), dma((2,)),
            dma((2,)), dma((2,)), dma((2,)), dma((2,)),
            dma, dma, dma, dma,
        ],
        compiler_params=pltpu.CompilerParams(
            collective_id=0, has_side_effects=True, vmem_limit_bytes=40 * 1024 * 1024
        ),
        name="project",
    )(*(pltpu.with_memory_space_constraint(a, pltpu.HBM) for a in (velocity, z_lower, z_upper, z_slope, ftab, itab, etab, turn)))


def solution(mesh):
    placed = (P(None, None, "gz", "gy"), P("gz"), P("gz"), P("gz"))
    return jax.shard_map(
        shards, mesh=mesh, in_specs=placed, out_specs=P(None, None, "gz", "gy"), check_vma=False
    )
```

```python
import functools

import jax
import jax.numpy as jnp
import ml_dtypes
import numpy as np
from jax import lax
from jax.experimental import pallas as pl
from jax.experimental.pallas import tpu as pltpu
from jax.sharding import PartitionSpec as P

NY = 1024
KX = 16
LANES = 128
MESH = pl.DeviceIdType.MESH
Y_ORDER = (4, 3, -3, 2, -2, 1, -1)
Z_ORDER = sorted(
    ((dx, dy) for dx in (2, 1, -1, 0) for dy in (2, 1, -1, 0) if (dx, dy) != (0, 0)),
    key=lambda pair: -abs(pair[0]) - abs(pair[1]),
)


def fourier_tables():
    place = np.arange(256)
    y = 64 * ((place % 128) // 32) + 32 * (place // 128) + place % 32

    def pair(m):
        phase = 2.0 * np.pi * ((y[:, None] * m[None, :]) % NY) / NY
        return np.cos(phase), np.sin(phase)

    c0, s0 = pair(4 * np.arange(128))
    s0[:, 0] = (-1.0) ** y
    c2, s2 = pair(4 * np.arange(128) + 2)
    c1, s1 = pair(4 * np.arange(256) + 1)
    table = np.concatenate([c0, s0, c2, s2, c1, s1], axis=1)

    def split(values):
        high = values.astype(ml_dtypes.bfloat16)
        low = (values - high.astype(np.float64)).astype(ml_dtypes.bfloat16)
        return np.stack([high, low])

    t, u = np.arange(128), np.arange(256)
    half = 4 * t
    half[0] = NY // 2
    m = np.concatenate([4 * t, -half, 4 * t + 2, -4 * t - 2, 4 * u + 1, -4 * u - 1]) % NY

    def both(y):
        phase = 2.0 * np.pi * ((y[:, None] * m[None, :]) % NY) / NY
        return np.cos(phase), np.sin(phase)

    r = np.arange(32)
    edge = np.concatenate(both(64 * (r // 2) + r % 2), axis=1)
    turn = np.stack(both(8 * (r % 8) + 2 * (r // 8))).astype(np.float32)
    return split(table), split(table.T / NY), split(edge), turn


def dot(a, b):
    return jnp.dot(a, b, preferred_element_type=jnp.float32)


def product(values, high, low):
    top = values.astype(jnp.bfloat16)
    rest = (values - top.astype(jnp.float32)).astype(jnp.bfloat16)
    rows = values.shape[0]
    both = dot(jnp.concatenate([top, rest], axis=0), high)
    return both[:rows] + both[rows:] + dot(top, low)


def kernel(
    planes, gy, gz,
    vel_hbm, zl_hbm, zu_hbm, zs_hbm, ftab_hbm, itab_hbm, etab_hbm, turn_hbm, out,
    vel, zl, zu, zs, ftab, itab, etab, turn, edge_buf, edge_rows, edge_send, edge_recv, edge_sum, edge, rows_buf, send_f, recv_f, send_b, recv_b,
    halo_send, halo_recv, vhat, field_re, field_im,
    inv_piv, mult, ratio, beta, gamma, low_row, high_row,
    mat_all, rhs_all, red_den, red_bden, red_psi, red_b31, red_br, red_r, red_e, red_phi, red_f,
    grad, grad_q,
    in_sem, e_ssem, e_rsem, halo_ssem, halo_rsem, f_ssem, f_rsem, b_ssem, b_rsem, m_ssem, m_rsem, r_ssem, r_rsem,
):
    me = lax.axis_index("gy")
    mz = lax.axis_index("gz")
    f32 = jnp.float32

    copy_in = [pltpu.make_async_copy(vel_hbm.at[c], vel.at[c], in_sem.at[c]) for c in range(3)]
    copy_z = [
        pltpu.make_async_copy(src, dst, in_sem.at[3 + i])
        for i, (src, dst) in enumerate(((zl_hbm, zl), (zu_hbm, zu), (zs_hbm, zs)))
    ]
    copy_ft = pltpu.make_async_copy(ftab_hbm, ftab, in_sem.at[6])
    copy_it = pltpu.make_async_copy(itab_hbm, itab, in_sem.at[7])
    copy_et = pltpu.make_async_copy(etab_hbm, etab, in_sem.at[8])
    copy_tt = pltpu.make_async_copy(turn_hbm, turn, in_sem.at[9])
    copy_in[1].start()
    copy_in[2].start()
    barrier = pltpu.get_barrier_semaphore()

    chips, chip, core = gy // 2, me // 2, lax.rem(me, 2)
    mate = me + 1 - 2 * core

    def y_partner(dz, c):
        return lax.rem(chip + dz + chips, chips) * 2 + c

    def z_partner(o, sign):
        dx, dy = Z_ORDER[o]
        return lax.rem(mz // 4 + sign * dx + 4, 4) * 4 + lax.rem(mz + sign * dy + 4, 4)

    z_all = range(len(Z_ORDER))
    y_all = [y_partner(dz, c) for dz in Y_ORDER for c in range(2)] + [mate]
    for g in y_all:
        pl.semaphore_signal(barrier, inc=1, device_id={"gy": g}, device_id_type=MESH)
    for o in z_all:
        pl.semaphore_signal(barrier, inc=1, device_id={"gz": z_partner(o, 1)}, device_id_type=MESH)
    for copy in (copy_z[2], copy_in[0], copy_z[0], copy_z[1], copy_et, copy_tt, copy_ft, copy_it):
        copy.start()

    def stage(f, re, im):
        for c in range(4):
            a = slice(c * 128, c * 128 + 128)
            b = slice(512 + c * 128, 512 + c * 128 + 128)
            block = jnp.concatenate([re[:, a], im[:, a], re[:, b], im[:, b]], axis=0)
            rows_buf[c * 128:(c + 1) * 128, :] = block.T
        for j in range(KX):
            send_f[f, j] = rows_buf[pl.ds(j, 32, stride=16), :]

    def y_copy(src, dst, ssem, rsem, f, g):
        return pltpu.make_async_remote_copy(
            src_ref=src.at[f, g], dst_ref=dst.at[f, me],
            send_sem=ssem.at[f], recv_sem=rsem.at[f],
            device_id={"gy": g}, device_id_type=MESH)

    def y_send(src, dst, ssem, rsem, f, partners):
        for g in partners:
            y_copy(src, dst, ssem, rsem, f, g).start()

    def y_send_first(src, dst, ssem, rsem, f, first):
        for t in first:
            @pl.when(chip != t)
            def _():
                y_send(src, dst, ssem, rsem, f, [2 * t, 2 * t + 1])
        for dz in Y_ORDER:
            g = y_partner(dz, 0)
            other = g >= 0
            for t in first:
                other = other & (g != 2 * t)

            @pl.when(other)
            def _():
                y_send(src, dst, ssem, rsem, f, [g, g + 1])

    def y_all_copy(src, dst, ssem, rsem, f):
        rest = pl.ds(0, gy - 1)
        return pltpu.make_async_remote_copy(
            src_ref=src.at[f, rest], dst_ref=dst.at[f, rest], send_sem=ssem.at[f], recv_sem=rsem.at[f],
            device_id={"gy": mate}, device_id_type=MESH)

    def y_wait_recv(src, dst, ssem, rsem, f):
        y_all_copy(src, dst, ssem, rsem, f).wait_recv()

    def y_wait_send(src, dst, ssem, rsem, f):
        y_all_copy(src, dst, ssem, rsem, f).wait_send()

    def z_copy(buf, ssem, rsem, g, slots):
        return pltpu.make_async_remote_copy(
            src_ref=buf.at[slots], dst_ref=buf.at[slots], send_sem=ssem, recv_sem=rsem,
            device_id={"gz": g}, device_id_type=MESH)

    def z_send(buf, ssem, rsem):
        for o in z_all:
            z_copy(buf, ssem, rsem, z_partner(o, 1), mz).start()

    def z_wait_recv(buf, ssem, rsem):
        z_copy(buf, ssem, rsem, z_partner(0, 1), pl.ds(0, gz - 1)).wait_recv()

    def z_wait_send(buf, ssem, rsem):
        z_copy(buf, ssem, rsem, z_partner(0, 1), pl.ds(0, gz - 1)).wait_send()

    def edge_copy(g):
        return pltpu.make_async_remote_copy(
            src_ref=edge_send.at[g], dst_ref=edge_recv.at[me], send_sem=e_ssem, recv_sem=e_rsem,
            device_id={"gy": g}, device_id_type=MESH)

    def edge_all_copy():
        rest = pl.ds(0, gy - 1)
        return pltpu.make_async_remote_copy(
            src_ref=edge_send.at[rest], dst_ref=edge_recv.at[rest], send_sem=e_ssem, recv_sem=e_rsem,
            device_id={"gy": mate}, device_id_type=MESH)

    def halo_copies():
        up = pltpu.make_async_remote_copy(
            src_ref=halo_send.at[0], dst_ref=halo_recv.at[0],
            send_sem=halo_ssem.at[0], recv_sem=halo_rsem.at[0],
            device_id={"gz": lax.rem(mz + 1, gz)}, device_id_type=MESH)
        down = pltpu.make_async_remote_copy(
            src_ref=halo_send.at[1], dst_ref=halo_recv.at[1],
            send_sem=halo_ssem.at[1], recv_sem=halo_rsem.at[1],
            device_id={"gz": lax.rem(mz + gz - 1, gz)}, device_id_type=MESH)
        return up, down

    plane_id = lax.broadcasted_iota(jnp.int32, (planes, LANES), 0)

    def column(ref):
        def one(k, col):
            return jnp.where(plane_id == k, ref[k], col)

        return lax.fori_loop(0, planes, one, jnp.zeros((planes, LANES), f32))

    kx_lane = (lax.broadcasted_iota(jnp.int32, (1, NY), 1) % KX + 1).astype(f32)

    def slope_diff(values, low, high):
        above = jnp.concatenate([values[1:], high], axis=0)
        below = jnp.concatenate([low, values[:-1]], axis=0)
        return slope_wide * (above - below)

    copy_z[2].wait()
    slope = column(zs)
    slope_wide = jnp.concatenate([slope] * 8, axis=1)
    nothing = jnp.zeros((1, NY), f32)
    copy_in[1].wait()
    stage(1, vel[1, 0], vel[1, 1])
    copy_in[2].wait()
    for t in range(8):
        for part in range(2):
            for e, k in enumerate((0, planes - 1)):
                r = 4 * t + 2 * part + e
                edge_rows[r:r + 1, :] = vel[2, part, k:k + 1, t * 128:t * 128 + 128]
    edge_buf[...] = jnp.zeros((LANES, LANES), f32)
    for q in range(4):
        edge_buf[q * 32:q * 32 + 32, :32] = edge_rows[:32, q * 32:q * 32 + 32]
    edge_rows[:32, :] = edge_buf[...].T[:32]
    for j in range(KX):
        edge_send[j] = edge_rows[pl.ds(j, 2, stride=16), :]
    copy_in[0].wait()
    stage(
        0,
        slope_diff(vel[2, 0], nothing, nothing) - kx_lane * vel[0, 1],
        slope_diff(vel[2, 1], nothing, nothing) + kx_lane * vel[0, 0],
    )
    pl.semaphore_wait(barrier, len(y_all) + len(Z_ORDER))
    to_core = [[y_partner(dz, c) for dz in Y_ORDER] for c in range(2)]
    for partners in (to_core[0] + [mate], to_core[1]):
        for g in partners:
            edge_copy(g).start()
        y_send(send_f, recv_f, f_ssem, f_rsem, 1, partners)
        y_send(send_f, recv_f, f_ssem, f_rsem, 0, partners)
    for f in range(2):
        recv_f[f, me] = send_f[f, me]
    edge_recv[me] = edge_send[me]

    copy_z[0].wait()
    copy_z[1].wait()
    row = lax.broadcasted_iota(jnp.int32, (8, LANES), 0)
    lane = lax.broadcasted_iota(jnp.int32, (8, LANES), 1)
    offset = jnp.where(row < 2, 0, jnp.where(row < 4, 2, jnp.where((row == 4) | (row == 6), 1, -511)))
    ky_int = 4 * lane + offset
    ky_int = jnp.where((row == 1) | (row == 3) | (row >= 6), -ky_int, ky_int)
    ky_int = jnp.where((row == 1) & (lane == 0), -512, ky_int)
    ky = ky_int.astype(f32)
    kx = (me + 1).astype(f32)
    square = kx * kx + ky * ky

    def rows_of(k):
        return pl.ds(pl.multiple_of(k * 8, 8), 8)

    def factor(k, state):
        r, g = state
        low, up = zl[k], zu[k]
        inverse = 1.0 / (-(low + up) - square - low * r)
        m = low * inverse
        r = up * inverse
        g = -m * g
        inv_piv[rows_of(k), :] = inverse
        mult[rows_of(k), :] = m
        ratio[rows_of(k), :] = r
        beta[rows_of(k), :] = g
        return r, g

    zero = jnp.zeros((8, LANES), f32)
    one_v = jnp.ones((8, LANES), f32)
    lax.fori_loop(0, planes, factor, (zero, one_v))

    def unfold(i, state):
        b, g, width = state
        k = planes - 1 - i
        r = ratio[rows_of(k), :]
        b = beta[rows_of(k), :] - r * b
        g = -r * g
        beta[rows_of(k), :] = b
        gamma[rows_of(k), :] = g
        low_row[rows_of(k), :] = b * width
        high_row[rows_of(k), :] = g * width
        before = jnp.maximum(k - 1, 0)
        wider = width * (jnp.full((8, LANES), zl[k]) / jnp.full((8, LANES), zu[before]))
        return b, g, jnp.where(k > 0, wider, width)

    b0, g0, first_width = lax.fori_loop(0, planes, unfold, (zero, one_v, one_v))
    low_scale = -1.0 / (jnp.full((8, LANES), zl[0]) * first_width)
    high_scale = -1.0 / jnp.full((8, LANES), zu[planes - 1])
    last = slice((planes - 1) * 8, planes * 8)
    mat_all[mz, 0] = b0
    mat_all[mz, 1] = g0
    mat_all[mz, 2] = beta[last, :]
    mat_all[mz, 3] = gamma[last, :]
    z_send(mat_all, m_ssem, m_rsem)

    copy_ft.wait()
    first_lane = lax.broadcasted_iota(jnp.int32, (planes, LANES), 1) == 0

    def forward(f):
        quarters = []
        for q in range(4):
            block = recv_f[f, 4 * q:4 * q + 4].reshape(LANES, LANES).T
            quarters.append(jnp.concatenate([block[:64], block[64:]], axis=1))
        a = quarters[0] + quarters[2]
        b = quarters[0] - quarters[2]
        c = quarters[1] + quarters[3]
        e = quarters[1] - quarters[3]
        turned = jnp.concatenate([e[planes:], -e[:planes]], axis=0)
        spectra = []
        for first, z in ((0, a + c), (256, a - c)):
            both = product(z, ftab[0, :, first:first + 256], ftab[1, :, first:first + 256])
            rc, rs = both[:planes, :128], both[:planes, 128:]
            ic, is_ = both[planes:, :128], both[planes:, 128:]
            if first == 0:
                rs0, is0 = jnp.where(first_lane, 0.0, rs), jnp.where(first_lane, 0.0, is_)
                spectra.append((rc + is0, ic - rs0))
                spectra.append((jnp.where(first_lane, rs, rc - is_), jnp.where(first_lane, is_, ic + rs)))
            else:
                spectra.append((rc + is_, ic - rs))
                spectra.append((rc - is_, ic + rs))
        both = product(jnp.concatenate([b + turned, b - turned], axis=0), ftab[0, :, 512:], ftab[1, :, 512:])
        for half in range(2):
            cos, sin = both[:, half * 128:half * 128 + 128], both[:, 256 + half * 128:384 + half * 128]
            spectra.append((cos[:planes] + sin[planes:2 * planes], cos[planes:2 * planes] - sin[:planes]))
        for half in range(2):
            cos, sin = both[:, half * 128:half * 128 + 128], both[:, 256 + half * 128:384 + half * 128]
            spectra.append((cos[2 * planes:3 * planes] - sin[3 * planes:], cos[3 * planes:] + sin[2 * planes:3 * planes]))
        return spectra

    y_wait_recv(send_f, recv_f, f_ssem, f_rsem, 1)
    for s, (re, im) in enumerate(forward(1)):
        ky_row = ky[s:s + 1, :]
        vhat[s, 0] = -ky_row * im
        vhat[s, 1] = ky_row * re
    copy_et.wait()
    copy_tt.wait()
    edge_all_copy().wait_recv()
    for d in range(gy):
        edge_buf[2 * d:2 * d + 2, :] = edge_recv[d]
    partial = product(edge_buf[...].T[:, :32], etab[0], etab[1])
    for s in range(16):
        edge_sum[s] = partial[:, s * 128:s * 128 + 128]
    for s in range(8):
        cos, sin = turn[0, :, s * 128:s * 128 + 128], turn[1, :, s * 128:s * 128 + 128]
        for e in range(2):
            rc, rs, ic, is_ = (
                edge_sum[s + off, pl.ds(part + e, 32, stride=4), :] for part in (0, 2) for off in (0, 8))
            re, im = rc + is_, ic - rs
            edge[e, 0, s:s + 1, :] = jnp.sum(re * cos + im * sin, axis=0, keepdims=True)
            edge[e, 1, s:s + 1, :] = jnp.sum(im * cos - re * sin, axis=0, keepdims=True)
    below = jnp.full((8, LANES), zs[0]) / jnp.full((8, LANES), zl[0])
    above = jnp.full((8, LANES), zs[planes - 1]) / jnp.full((8, LANES), zu[planes - 1])
    y_wait_recv(send_f, recv_f, f_ssem, f_rsem, 0)
    for s, (re, im) in enumerate(forward(0)):
        field_re[pl.ds(s, planes, stride=8), :] = re + vhat[s, 0]
        field_im[pl.ds(s, planes, stride=8), :] = im + vhat[s, 1]

    sums = [[zero] * 4 for _ in range(4)]
    for k in range(planes):
        rows = slice(k * 8, k * 8 + 8)
        re, im, low, high = field_re[rows, :], field_im[rows, :], low_row[rows, :], high_row[rows, :]
        for n, term in enumerate((low * re, low * im, high * re, high * im)):
            sums[n][k % 4] = sums[n][k % 4] + term
    lr, li, hr, hi = ((t[0] + t[1]) + (t[2] + t[3]) for t in sums)
    rhs_all[mz, 0] = low_scale * lr - below * edge[0, 0]
    rhs_all[mz, 1] = low_scale * li - below * edge[0, 1]
    rhs_all[mz, 2] = high_scale * hr + above * edge[1, 0]
    rhs_all[mz, 3] = high_scale * hi + above * edge[1, 1]
    z_send(rhs_all, r_ssem, r_rsem)

    def down(k, state):
        sr, si = state
        inverse, m = inv_piv[rows_of(k), :], mult[rows_of(k), :]
        sr = field_re[rows_of(k), :] * inverse - m * sr
        si = field_im[rows_of(k), :] * inverse - m * si
        field_re[rows_of(k), :] = sr
        field_im[rows_of(k), :] = si
        return sr, si

    lax.fori_loop(0, planes, down, (zero, zero), unroll=True)

    def back(i, state):
        ar, ai = state
        k = planes - 1 - i
        r = ratio[rows_of(k), :]
        ar = field_re[rows_of(k), :] - r * ar
        ai = field_im[rows_of(k), :] - r * ai
        field_re[rows_of(k), :] = ar
        field_im[rows_of(k), :] = ai
        return ar, ai

    lax.fori_loop(0, planes, back, (zero, zero), unroll=True)

    z_wait_recv(mat_all, m_ssem, m_rsem)
    red_r[0] = zero
    red_e[0, 0] = zero
    red_e[0, 1] = zero

    def reduce_matrix(d, r):
        den = 1.0 / (1.0 - mat_all[d, 0] * r)
        psi = mat_all[d, 1] * den
        br = mat_all[d, 2] * r
        red_den[d] = den
        red_bden[d] = mat_all[d, 0] * den
        red_psi[d] = psi
        red_b31[d] = mat_all[d, 2] + br * (mat_all[d, 0] * den)
        red_br[d] = br * den
        r = mat_all[d, 3] + br * psi
        red_r[d + 1] = r
        return r

    lax.fori_loop(0, gz, reduce_matrix, zero)
    z_wait_recv(rhs_all, r_ssem, r_rsem)

    def reduce_rhs(d, state):
        er, ei = state
        den, bden, brden, step = red_den[d], red_bden[d], red_br[d], red_b31[d]
        red_phi[d, 0] = den * rhs_all[d, 0] + bden * er
        red_phi[d, 1] = den * rhs_all[d, 1] + bden * ei
        er = (rhs_all[d, 2] + brden * rhs_all[d, 0]) + step * er
        ei = (rhs_all[d, 3] + brden * rhs_all[d, 1]) + step * ei
        red_e[d + 1, 0] = er
        red_e[d + 1, 1] = ei
        return er, ei

    lax.fori_loop(0, gz, reduce_rhs, (zero, zero), unroll=True)
    red_f[gz, 0] = zero
    red_f[gz, 1] = zero

    def reduce_back(i, state):
        fr, fi = state
        d = gz - 1 - i
        psi = red_psi[d]
        fr = red_phi[d, 0] + psi * fr
        fi = red_phi[d, 1] + psi * fi
        red_f[d, 0] = fr
        red_f[d, 1] = fi
        return fr, fi

    lax.fori_loop(0, gz, reduce_back, (zero, zero), unroll=True)
    before = [red_e[mz, part] + red_r[mz] * red_f[mz, part] for part in range(2)]
    after = [red_f[mz + 1, part] for part in range(2)]

    def finish(k, _):
        b, g = beta[rows_of(k), :], gamma[rows_of(k), :]
        field_re[rows_of(k), :] = field_re[rows_of(k), :] + b * before[0] + g * after[0]
        field_im[rows_of(k), :] = field_im[rows_of(k), :] + b * before[1] + g * after[1]
        return 0

    lax.fori_loop(0, planes, finish, 0, unroll=True)

    copy_it.wait()

    def inverse(f, spectra):
        parts = []
        for first in (0, 256):
            (pr, pi), (nr, ni) = spectra[first // 128], spectra[first // 128 + 1]
            cr, sr, ci, si = pr + nr, ni - pi, pi + ni, pr - nr
            if first == 0:
                cr, sr = jnp.where(first_lane, pr, cr), jnp.where(first_lane, nr, sr)
                ci, si = jnp.where(first_lane, pi, ci), jnp.where(first_lane, ni, si)
            z = jnp.concatenate([jnp.concatenate([cr, sr], axis=1), jnp.concatenate([ci, si], axis=1)], axis=0)
            parts.append(product(z, itab[0, first:first + 256, :], itab[1, first:first + 256, :]))
        (ar, ai), (br, bi), (cr, ci), (dr, di) = spectra[4:]
        z = jnp.concatenate([
            jnp.concatenate([ar, br, -ai, -bi], axis=1),
            jnp.concatenate([ai, bi, ar, br], axis=1),
            jnp.concatenate([cr, dr, ci, di], axis=1),
            jnp.concatenate([ci, di, -cr, -dr], axis=1)], axis=0)
        odd = product(z, itab[0, 512:, :], itab[1, 512:, :])
        g1, g3 = odd[:64], odd[64:]
        s02, d02 = parts[0] + parts[1], parts[0] - parts[1]
        s13, d13 = g1 + g3, g1 - g3
        turned = jnp.concatenate([-d13[planes:], d13[:planes]], axis=0)
        for q, value in enumerate((s02 + s13, d02 + turned, s02 - s13, d02 - turned)):
            block = jnp.concatenate([value[:, :128], value[:, 128:]], axis=0).T
            send_b[f, 4 * q:4 * q + 4] = block.reshape(4, 32, LANES)

    tiles = [(field_re[pl.ds(s, planes, stride=8), :], field_im[pl.ds(s, planes, stride=8), :]) for s in range(8)]
    inverse(0, tiles)
    y_send_first(send_b, recv_b, b_ssem, b_rsem, 0, (0, 1, 2))
    y_send(send_b, recv_b, b_ssem, b_rsem, 0, [mate])
    recv_b[0, me] = send_b[0, me]
    inverse(1, [(-ky[s:s + 1, :] * im, ky[s:s + 1, :] * re) for s, (re, im) in enumerate(tiles)])
    y_send_first(send_b, recv_b, b_ssem, b_rsem, 1, (0, 1, 2))
    y_send(send_b, recv_b, b_ssem, b_rsem, 1, [mate])
    recv_b[1, me] = send_b[1, me]

    def unstage(f, grad):
        for j in range(KX):
            rows_buf[pl.ds(j, 32, stride=16), :] = recv_b[f, j]
        for c in range(4):
            block = rows_buf[c * 128:(c + 1) * 128, :].T
            for h in range(2):
                for part in range(2):
                    first = h * 64 + part * 32
                    grad[part, :, h * 512 + c * 128:h * 512 + c * 128 + 128] = block[first:first + 32]

    edge_all_copy().wait_send()
    for f in range(2):
        y_wait_send(send_f, recv_f, f_ssem, f_rsem, f)
    z_wait_send(mat_all, m_ssem, m_rsem)
    z_wait_send(rhs_all, r_ssem, r_rsem)
    y_wait_recv(send_b, recv_b, b_ssem, b_rsem, 0)
    unstage(0, grad)
    for part in range(2):
        halo_send[0, part:part + 1, :] = grad[part, planes - 1:planes, :]
        halo_send[1, part:part + 1, :] = grad[part, 0:1, :]
    halo_p = halo_copies()
    halo_p[0].start()
    halo_p[1].start()
    out[0, 0] = vel[0, 0] + kx_lane * grad[1]
    out[0, 1] = vel[0, 1] - kx_lane * grad[0]
    y_wait_send(send_b, recv_b, b_ssem, b_rsem, 0)
    for copy in halo_p:
        copy.wait_send()
    y_wait_send(send_b, recv_b, b_ssem, b_rsem, 1)
    y_wait_recv(send_b, recv_b, b_ssem, b_rsem, 1)
    unstage(1, grad_q)
    for part in range(2):
        out[1, part] = vel[1, part] - grad_q[part]
    halo_p[0].wait_recv()
    halo_p[1].wait_recv()
    for part in range(2):
        low = jnp.where(mz > 0, halo_recv[0, part:part + 1, :], 0.0)
        high = jnp.where(mz < gz - 1, halo_recv[1, part:part + 1, :], 0.0)
        out[2, part] = vel[2, part] - slope_diff(grad[part], low, high)


def shards(velocity, z_lower, z_upper, z_slope):
    gy, gz = lax.axis_size("gy"), lax.axis_size("gz")
    planes = velocity.shape[2]
    ftab, itab, etab, turn = (jnp.asarray(table) for table in fourier_tables())
    f32 = jnp.float32
    hbm = pl.BlockSpec(memory_space=pl.ANY)
    lines = (planes * 8 + 8, LANES)
    dma = pltpu.SemaphoreType.DMA
    return pl.pallas_call(
        functools.partial(kernel, planes, gy, gz),
        out_shape=jax.ShapeDtypeStruct(velocity.shape, f32),
        in_specs=[pl.BlockSpec(memory_space=pltpu.HBM)] * 8,
        out_specs=pl.BlockSpec(memory_space=pltpu.VMEM),
        scratch_shapes=[
            pltpu.VMEM(velocity.shape, f32),
            pltpu.SMEM((planes,), f32),
            pltpu.SMEM((planes,), f32),
            pltpu.SMEM((planes,), f32),
            pltpu.VMEM(ftab.shape, jnp.bfloat16),
            pltpu.VMEM(itab.shape, jnp.bfloat16),
            pltpu.VMEM(etab.shape, jnp.bfloat16),
            pltpu.VMEM(turn.shape, f32),
            pltpu.VMEM((LANES, LANES), f32),
            pltpu.VMEM((160, LANES), f32),
            pltpu.VMEM((gy, 2, LANES), f32),
            pltpu.VMEM((gy, 2, LANES), f32),
            pltpu.VMEM((16, LANES, LANES), f32),
            pltpu.VMEM((3, 2, 8, LANES), f32),
            pltpu.VMEM((528, LANES), f32),
            pltpu.VMEM((2, gy, 32, LANES), f32),
            pltpu.VMEM((2, gy, 32, LANES), f32),
            pltpu.VMEM((2, gy, 32, LANES), f32),
            pltpu.VMEM((2, gy, 32, LANES), f32),
            pltpu.VMEM((4, 2, NY), f32),
            pltpu.VMEM((4, 2, NY), f32),
            pltpu.VMEM((8, 2, planes, LANES), f32),
            pltpu.VMEM(lines, f32),
            pltpu.VMEM(lines, f32),
            pltpu.VMEM(lines, f32),
            pltpu.VMEM(lines, f32),
            pltpu.VMEM(lines, f32),
            pltpu.VMEM(lines, f32),
            pltpu.VMEM(lines, f32),
            pltpu.VMEM(lines, f32),
            pltpu.VMEM(lines, f32),
            pltpu.VMEM((gz, 4, 8, LANES), f32),
            pltpu.VMEM((gz, 4, 8, LANES), f32),
            pltpu.VMEM((gz, 8, LANES), f32),
            pltpu.VMEM((gz, 8, LANES), f32),
            pltpu.VMEM((gz, 8, LANES), f32),
            pltpu.VMEM((gz, 8, LANES), f32),
            pltpu.VMEM((gz, 8, LANES), f32),
            pltpu.VMEM((gz + 1, 8, LANES), f32),
            pltpu.VMEM((gz + 1, 2, 8, LANES), f32),
            pltpu.VMEM((gz, 2, 8, LANES), f32),
            pltpu.VMEM((gz + 1, 2, 8, LANES), f32),
            pltpu.VMEM((2, planes, NY), f32),
            pltpu.VMEM((2, planes, NY), f32),
            dma((10,)), dma, dma, dma((2,)), dma((2,)),
            dma((2,)), dma((2,)), dma((2,)), dma((2,)),
            dma, dma, dma, dma,
        ],
        compiler_params=pltpu.CompilerParams(
            collective_id=0, has_side_effects=True, vmem_limit_bytes=40 * 1024 * 1024
        ),
        name="project",
    )(*(pltpu.with_memory_space_constraint(a, pltpu.HBM) for a in (velocity, z_lower, z_upper, z_slope, ftab, itab, etab, turn)))


def solution(mesh):
    placed = (P(None, None, "gz", "gy"), P("gz"), P("gz"), P("gz"))
    return jax.shard_map(
        shards, mesh=mesh, in_specs=placed, out_specs=P(None, None, "gz", "gy"), check_vma=False
    )
```
